256 devices in a mesh: qrow: 16 (over z, x_lo), kcol: 8 (over x_hi, y), head: 2 (over core).
Axes of the slice: x: 4 (x_hi: 2, x_lo: 2; x = x_hi * 2 + x_lo), y: 4, z: 8, core: 2. Of those that a mesh axis runs over, the one named last changes fastest.
Arguments:
- query: bfloat16 [16384, 1024], P(('qrow', 'kcol'), 'head'), parts along dimension 1, may hold values from -5 to 5, as said below
- key: bfloat16 [16384, 256], P(('kcol', 'qrow'), 'head'), parts along dimension 1, may hold values from -5 to 5, as said below
- value: bfloat16 [16384, 256], P(('kcol', 'qrow'), 'head'), parts along dimension 1, may hold values from -0.5 to 2.5
- dout: bfloat16 [16384, 1024], P(('qrow', 'kcol'), 'head'), parts along dimension 1, may hold values from -6 to 6
- document: int32 [16384], replicated, may hold values from 0 to 7, never falling along the last dimension, each value on 1 to 8192 neighbouring positions
Outputs:
- attended: bfloat16 [16384, 1024], P(('qrow', 'kcol'), 'head'), parts along dimension 1
- grad_query: bfloat16 [16384, 1024], P(('qrow', 'kcol'), 'head'), parts along dimension 1
- grad_key: bfloat16 [16384, 256], P(('kcol', 'qrow'), 'head'), parts along dimension 1
- grad_value: bfloat16 [16384, 256], P(('kcol', 'qrow'), 'head'), parts along dimension 1
The draws below stay inside these ranges and needn't reach their ends.
There are 2 independent parts, one for each index of `head`. The reference program is written for one: setup_inputs(seed, part) draws one part's arguments, and reference() takes and returns one part's arrays. A program takes and returns all parts, laid end to end along the dimension named above; an argument that names none is the same for every part. Nothing has to cross between parts.
Inputs may be any that keep to these rules, and one draw needn't show every extreme that they name: `query`: entries of order one. `key`: entries of order one. Document numbers never fall along the sequence; each document is a run of 1 to 8192 positions, and one has exactly 8192.
All inputs are finite; a program needn't handle non-finite values.
Results may differ from the reference program's by a relative error of at most 0.035.
Values may be sent and summed in bfloat16 or wider, within the bound.
No kernel may reach another device: no remote copies, remote signals or barrier semaphores. Data moves between devices by JAX's collectives and lax.ppermute only.
A program may use at most 128 MiB of HBM per device.

```python
import math
import jax
import jax.numpy as jnp
import numpy as np
from jax import lax

HEAD_DIM = 128
GROUP = 4
DOCS = 8
SEQ = 16384


def draw_query(key, part):
    key = jax.random.fold_in(key, 11)
    values = jnp.clip(jax.random.normal(key, (SEQ, GROUP * HEAD_DIM), jnp.float32), -4.0, 4.0)
    return values.astype(jnp.bfloat16)


def draw_key(key, part):
    key = jax.random.fold_in(key, 23)
    values = jnp.clip(jax.random.normal(key, (SEQ, HEAD_DIM), jnp.float32), -4.0, 4.0)
    return values.astype(jnp.bfloat16)


def levels(key, extent, shards, smallest, top_value):
    def one(dim, blocks):
        steps = jax.random.uniform(jax.random.fold_in(jax.random.fold_in(key, 6), dim), (blocks,), jnp.float32, smallest / len(shards), top_value / len(shards))
        return jnp.repeat(jnp.exp(steps), extent[dim] // blocks).reshape((-1,) + (1,) * (len(extent) - dim - 1))

    factor_of = one(*shards[0])
    for cut in shards[1:]:
        factor_of = factor_of * one(*cut)
    return factor_of


def length_profile(number_of, total, most, skew):
    loads = [(1 << 20) // math.isqrt(standing ** skew) + 1 for standing in range(2, number_of + 1)]
    surplus, given = total - most - (number_of - 1), [1] * (number_of - 1)
    while surplus > 0:
        movable = [i for i in range(number_of - 1) if given[i] < most]
        pool, budget = sum([loads[i] for i in movable]), surplus
        for i in movable:
            addition = min(most - given[i], max(1, budget * loads[i] // pool), surplus)
            given[i] = given[i] + addition
            surplus = surplus - addition
    return np.array([most] + given)


def ragged(stream_key, count, total, limit, skew):
    if count == 2:
        one = jax.random.randint(stream_key, (), max(1, total - limit), min(limit, total - 1) + 1)
        return jnp.stack([one, total - one])
    sizes = jnp.asarray(length_profile(count, total, limit, skew), jnp.int32)
    couples = (count - 1) // 2
    donor, taker = sizes[1:1 + 2 * couples:2], sizes[2:2 + 2 * couples:2]
    room = jnp.minimum(donor - 1, limit - taker)
    moved = jax.random.randint(jax.random.fold_in(stream_key, 1), (couples,), 0, 1 << 20) % (room + 1)
    sizes = sizes.at[1:1 + 2 * couples:2].set(donor - moved).at[2:2 + 2 * couples:2].set(taker + moved)
    return sizes[jax.random.permutation(jax.random.fold_in(stream_key, 2), count)]


def normal_values(own_key, shape, scale, most, cuts=(), kind=jnp.bfloat16):
    loudness = levels(own_key, shape, cuts, -0.22, 0.18) if cuts else 1.0
    array = jax.random.normal(own_key, shape, jnp.float32) * scale * loudness
    return jnp.minimum(jnp.maximum(array, -most), most).astype(kind)


def setup_inputs(seed: int = 0, part: int = 0) -> dict:
    streams_of = jax.random.split(jax.random.key(seed), 6)
    part_splits = jax.random.split(jax.random.fold_in(streams_of[5], part), 6)
    query = draw_query(jax.random.fold_in(jax.random.fold_in(streams_of[5], part), 71), part)
    key = draw_key(jax.random.fold_in(jax.random.fold_in(streams_of[5], part), 71), part)
    value = jnp.clip(-0.5 + 3.0 * jax.random.uniform(part_splits[2], (SEQ, HEAD_DIM), jnp.float32) ** levels(part_splits[2], (SEQ, HEAD_DIM), ((0, 128),), -0.2, 0.2), -0.5, 2.5).astype(jnp.bfloat16)
    dout = normal_values(part_splits[3], (SEQ, GROUP * HEAD_DIM), 1.0, 6.0, ((0, 128),))
    document = jnp.searchsorted(jnp.cumsum(ragged(streams_of[4], DOCS, SEQ, SEQ // 2, 1)), jnp.arange(SEQ), side="right").astype(jnp.int32)
    return {"query": query, "key": key, "value": value, "dout": dout, "document": document}


NEG = -1e+30

def reference(query, key, value, dout, document):
    scale = 1.0 / math.sqrt(HEAD_DIM)
    block = math.gcd(SEQ, 512)
    count = SEQ // block
    positions = jnp.arange(SEQ, dtype=jnp.int32)
    keys_wide = key.astype(jnp.float32)
    values_wide = value.astype(jnp.float32)

    def step(carry, index):
        grad_k, grad_v = carry
        begin = (index * block).astype(jnp.int32)
        heads = lax.dynamic_slice_in_dim(query, begin, block).astype(jnp.float32).reshape(block, GROUP, HEAD_DIM)
        grad_heads = lax.dynamic_slice_in_dim(dout, begin, block).astype(jnp.float32).reshape(block, GROUP, HEAD_DIM)
        row_doc = lax.dynamic_slice_in_dim(document, begin, block)
        row_pos = begin + jnp.arange(block, dtype=jnp.int32)
        allowed = (row_doc[:, None] == document[None, :]) & (positions[None, :] <= row_pos[:, None])
        score = jnp.einsum('rhd,cd->hrc', heads, keys_wide) * scale
        score = jnp.where(allowed[None], score, NEG)
        high = lax.optimization_barrier(jnp.max(score, axis=2))
        total = lax.optimization_barrier(jnp.sum(jnp.where(allowed[None], jnp.exp(score - high[:, :, None]), 0.0), axis=2))
        lse = high + jnp.log(total)
        prob = jnp.where(allowed[None], jnp.exp(score - lse[:, :, None]), 0.0)
        prob_low = lax.optimization_barrier(prob.astype(jnp.bfloat16)).astype(jnp.float32)
        attended = jnp.einsum('hrc,cd->rhd', prob_low, values_wide).reshape(block, GROUP * HEAD_DIM).astype(jnp.bfloat16)
        attended_wide = lax.optimization_barrier(attended).astype(jnp.float32).reshape(block, GROUP, HEAD_DIM)
        delta = jnp.transpose(lax.optimization_barrier(jnp.sum(grad_heads * attended_wide, axis=2)))
        dprob = jnp.einsum('rhd,cd->hrc', grad_heads, values_wide)
        dscore = lax.optimization_barrier((prob * (dprob - delta[:, :, None])).astype(jnp.bfloat16)).astype(jnp.float32)
        grad_q = (scale * jnp.einsum('hrc,cd->rhd', dscore, keys_wide)).reshape(block, GROUP * HEAD_DIM).astype(jnp.bfloat16)
        grad_k = grad_k + scale * jnp.einsum('hrc,rhd->cd', dscore, heads)
        grad_v = grad_v + jnp.einsum('hrc,rhd->cd', prob_low, grad_heads)
        return ((grad_k, grad_v), (attended, grad_q))
    empty = jnp.zeros((SEQ, HEAD_DIM), jnp.float32)
    (grad_k, grad_v), (attended, grad_q) = lax.scan(step, (empty, empty), jnp.arange(count, dtype=jnp.int32))
    attended = attended.reshape(SEQ, GROUP * HEAD_DIM)
    grad_q = grad_q.reshape(SEQ, GROUP * HEAD_DIM)
    return (attended, grad_q, grad_k.astype(jnp.bfloat16), grad_v.astype(jnp.bfloat16))
```

```python
import functools
import math

import jax
import jax.numpy as jnp
from jax import lax
from jax.experimental import pallas as pl
from jax.experimental.pallas import tpu as pltpu
from jax.sharding import PartitionSpec as P

AXES = ("qrow", "kcol")
DEVICES = 128
CHUNK = 128
SLOTS = 4
PLANES = 5
ROWS = SLOTS * CHUNK
PAIR = 2 * CHUNK
BLOCKS = 2 * PLANES
NEG = -1e30
FLOOR = -1e29
LOG2E = math.log2(math.e)
F32 = jnp.float32
BF16 = jnp.bfloat16

SWAP_Y = [[(d, d ^ s) for d in range(DEVICES)] for s in range(SLOTS)]
SWAP_X = [[(d, d ^ m) for d in range(DEVICES)] for m in (0, 8, 4, 12)]


def spread(dz):
    pairs = []
    for d in range(DEVICES):
        z, x_lo, column = d // 16, d // 8 % 2, d % 8
        pairs.append((d, (column + dz) % 8 * 16 + x_lo * 8 + z))
    return pairs


def dot(a, b):
    return lax.dot_general(a, b, (((1,), (0,)), ((), ())), preferred_element_type=F32)


def dot_t(a, b):
    return lax.dot_general(a, b, (((1,), (1,)), ((), ())), preferred_element_type=F32)


def fill(qd, kv, q_s, do_s, k_s, v_s, t_s, group, width, which):
    for s in range(SLOTS):
        for h in range(group):
            at = pl.ds(s * CHUNK, CHUNK)
            q_s[h, at, :] = qd[s][:, h * width : (h + 1) * width]
            do_s[h, at, :] = qd[s][:, (group + h) * width : (group + h + 1) * width]
    for dz in range(PLANES):
        for s in range(SLOTS):
            kb, at = 2 * dz + s // 2, pl.ds(s % 2 * CHUNK, CHUNK)
            part = kv[s][dz * CHUNK : (dz + 1) * CHUNK, :]
            k_s[kb, at, :] = part[:, :width]
            v_s[kb, at, :] = part[:, width:]
            t_s[kb, :, at] = jnp.transpose(part[:, which * width : (which + 1) * width])


def place(sc, kb):
    place_of, x_lo, x_hi, y, first, last = (sc[n] for n in range(6))
    plane = (place_of // 16 - kb // 2) & 7
    base = plane * (16 * CHUNK) + (8 * (x_hi ^ (kb & 1)) + 2 * y) * CHUNK
    row = place_of // SLOTS * ROWS
    needed = (base <= row + ROWS - 1) & (base + PAIR - 1 >= first)
    whole = (base + PAIR - 1 <= row) & (base >= last)
    return base, needed, whole


def allowed_of(sc, start, base):
    key_at = base + (lax.broadcasted_iota(jnp.int32, (PAIR, 1), 0) ^ (sc[1] * CHUNK))
    row_at = sc[0] // SLOTS * ROWS + (
        lax.broadcasted_iota(jnp.int32, (1, ROWS), 1) ^ (sc[3] * CHUNK)
    )
    return (key_at >= start[...]) & (key_at <= row_at)


def forward(group, width, sc, start, *refs):
    qd, kv, refs = refs[:SLOTS], refs[SLOTS : 2 * SLOTS], refs[2 * SLOTS :]
    out, stat, refs = refs[:SLOTS], refs[SLOTS], refs[SLOTS + 1 :]
    q_s, do_s, k_s, v_s, t_s, acc, high, total, mixed = refs
    unit = LOG2E / math.sqrt(width)
    fill(qd, kv, q_s, do_s, k_s, v_s, t_s, group, width, 1)
    acc[...] = jnp.zeros_like(acc)
    high[...] = jnp.full_like(high, FLOOR)
    total[...] = jnp.zeros_like(total)
    mixed[...] = jnp.zeros_like(mixed)

    def block(kb, base, masked):
        if masked:
            allowed = allowed_of(sc, start, base)
        for h in range(group):
            score = dot_t(k_s[kb], q_s[h])
            if masked:
                score = jnp.where(allowed, score, NEG)
            old = high[h]
            new = jnp.maximum(old, jnp.max(score, axis=0, keepdims=True))
            high[h] = new
            shrink = jnp.exp2((old - new) * unit)
            e = jnp.exp2(score * unit - new * unit)
            dprob = dot_t(v_s[kb], do_s[h])
            total[h] = total[h] * shrink + jnp.sum(e, axis=0, keepdims=True)
            mixed[h] = mixed[h] * shrink + jnp.sum(e * dprob, axis=0, keepdims=True)
            acc[h] = acc[h] * shrink + dot(t_s[kb], e.astype(BF16))

    def step(kb, carry):
        base, needed, whole = place(sc, kb)

        @pl.when(needed & whole)
        def _():
            block(kb, base, False)

        @pl.when(needed & jnp.logical_not(whole))
        def _():
            block(kb, base, True)

        return carry

    lax.fori_loop(0, BLOCKS, step, 0)
    for h in range(group):
        one = total[h]
        value = (acc[h] * (1.0 / jnp.maximum(one, 1e-30))).astype(BF16)
        for s in range(SLOTS):
            out[s][h * width : (h + 1) * width, :] = value[:, s * CHUNK : (s + 1) * CHUNK]
        stat[h : h + 1, :] = high[h]
        stat[group + h : group + h + 1, :] = one
        stat[2 * group + h : 2 * group + h + 1, :] = mixed[h]


def backward(group, width, sc, start, *refs):
    qd, kv, refs = refs[:SLOTS], refs[SLOTS : 2 * SLOTS], refs[2 * SLOTS :]
    stats, refs = refs[:SLOTS], refs[SLOTS:]
    dq, dkv, refs = refs[:SLOTS], refs[SLOTS : 2 * SLOTS], refs[2 * SLOTS :]
    q_s, do_s, k_s, v_s, t_s, acc, lse, delta = refs
    scale = 1.0 / math.sqrt(width)
    unit = LOG2E * scale
    fill(qd, kv, q_s, do_s, k_s, v_s, t_s, group, width, 0)
    acc[...] = jnp.zeros_like(acc)
    for u in range(SLOTS):
        parts = [stats[s][:, (u ^ s) * CHUNK : (u ^ s) * CHUNK + CHUNK] for s in range(SLOTS)]
        top = functools.reduce(jnp.maximum, [p[:group] for p in parts])
        weights = [jnp.exp2((p[:group] - top) * unit) for p in parts]
        total = sum(w * p[group : 2 * group] for w, p in zip(weights, parts))
        mixed = sum(w * p[2 * group : 3 * group] for w, p in zip(weights, parts))
        low, small = top * unit + jnp.log2(total), mixed / total
        for h in range(group):
            lse[h, :, pl.ds(u * CHUNK, CHUNK)] = low[h : h + 1]
            delta[h, :, pl.ds(u * CHUNK, CHUNK)] = small[h : h + 1]

    def block(kb, base, masked):
        if masked:
            allowed = allowed_of(sc, start, base)
        dk = dv = None
        for h in range(group):
            score = dot_t(k_s[kb], q_s[h])
            if masked:
                score = jnp.where(allowed, score, NEG)
            prob = jnp.exp2(score * unit - lse[h])
            dprob = dot_t(v_s[kb], do_s[h])
            dscore = (prob * (dprob - delta[h])).astype(BF16)
            one = dot(prob.astype(BF16), do_s[h])
            two = dot(dscore, q_s[h])
            acc[h] = acc[h] + dot(t_s[kb], dscore)
            dv = one if dv is None else dv + one
            dk = two if dk is None else dk + two
        return (dk * scale).astype(BF16), dv.astype(BF16)

    def write(kb, dk, dv):
        dz, pair = kb // 2, kb & 1
        at = pl.ds(pl.multiple_of(dz * CHUNK, CHUNK), CHUNK)
        for n in range(2):

            @pl.when(pair == n)
            def _():
                for b in range(2):
                    ref = dkv[2 * n + b]
                    ref[at, :width] = dk[b * CHUNK : (b + 1) * CHUNK]
                    ref[at, width:] = dv[b * CHUNK : (b + 1) * CHUNK]

    def step(kb, carry):
        base, needed, whole = place(sc, kb)

        @pl.when(needed & whole)
        def _():
            write(kb, *block(kb, base, False))

        @pl.when(needed & jnp.logical_not(whole))
        def _():
            write(kb, *block(kb, base, True))

        @pl.when(jnp.logical_not(needed))
        def _():
            none = jnp.zeros((PAIR, width), BF16)
            write(kb, none, none)

        return carry

    lax.fori_loop(0, BLOCKS, step, 0)
    for h in range(group):
        value = (acc[h] * scale).astype(BF16)
        for s in range(SLOTS):
            dq[s][h * width : (h + 1) * width, :] = value[:, s * CHUNK : (s + 1) * CHUNK]


def combine(group, width, *refs):
    parts, stats, out = refs[:SLOTS], refs[SLOTS : 2 * SLOTS], refs[2 * SLOTS]
    unit = LOG2E / math.sqrt(width)
    stat = [stats[s][:, s * CHUNK : (s + 1) * CHUNK] for s in range(SLOTS)]
    top = functools.reduce(jnp.maximum, [p[:group] for p in stat])
    weights = [jnp.exp2((p[:group] - top) * unit) * p[group : 2 * group] for p in stat]
    total = sum(weights)
    for h in range(group):
        at = pl.ds(h * width, width)
        whole = sum(
            parts[s][at, :].astype(F32) * (weights[s] / total)[h : h + 1] for s in range(SLOTS)
        )
        out[:, at] = jnp.transpose(whole).astype(BF16)


def gather_up(group, width, *refs):
    parts, out = refs[:SLOTS], refs[SLOTS]
    for h in range(group):
        at = pl.ds(h * width, width)
        whole = sum(parts[s][at, :].astype(F32) for s in range(SLOTS))
        out[:, at] = jnp.transpose(whole).astype(BF16)


def local(query, key, value, dout, document):
    width = key.shape[1]
    group = query.shape[1] // width
    send = functools.partial(lax.ppermute, axis_name=AXES)
    qrow, kcol = lax.axis_index("qrow"), lax.axis_index("kcol")
    place_of = qrow * 8 + kcol
    x_lo, x_hi, y = qrow % 2, kcol // 4, kcol % 4

    kv_home = jnp.concatenate([key, value], axis=1)
    qd_home = jnp.concatenate([query, dout], axis=1)
    kv_own = jnp.concatenate([send(kv_home, perm=spread(dz)) for dz in range(PLANES)], axis=0)
    qd = [qd_home] + [send(qd_home, perm=SWAP_Y[s]) for s in range(1, SLOTS)]
    kv = [kv_own] + [send(kv_own, perm=SWAP_X[s]) for s in range(1, SLOTS)]

    numbers = jnp.arange(8, dtype=jnp.int32)
    starts = jnp.sum((document[None, :] < numbers[:, None]).astype(jnp.int32), axis=1)
    row_doc = jnp.concatenate(
        [
            lax.dynamic_slice_in_dim(document, (place_of ^ s) * CHUNK, CHUNK)
            for s in range(SLOTS)
        ]
    )
    start = jnp.sum(jnp.where(row_doc[None] == numbers[:, None], starts[:, None], 0), axis=0)
    sc = jnp.stack([place_of, x_lo, x_hi, y, jnp.min(start), jnp.max(start)]).astype(jnp.int32)
    start = start.reshape(1, ROWS)

    smem = pl.BlockSpec(memory_space=pltpu.SMEM)
    vmem = pl.BlockSpec(memory_space=pltpu.VMEM)
    params = pltpu.CompilerParams(vmem_limit_bytes=56 * 1024 * 1024)
    work = ROWS * group * BLOCKS * PAIR * width * 2
    shared = [
        pltpu.VMEM((group, ROWS, width), BF16),
        pltpu.VMEM((group, ROWS, width), BF16),
        pltpu.VMEM((BLOCKS, PAIR, width), BF16),
        pltpu.VMEM((BLOCKS, PAIR, width), BF16),
        pltpu.VMEM((BLOCKS, width, PAIR), BF16),
        pltpu.VMEM((group, width, ROWS), F32),
    ]
    line = pltpu.VMEM((group, 1, ROWS), F32)
    row_piece = jax.ShapeDtypeStruct((group * width, CHUNK), BF16)
    key_piece = jax.ShapeDtypeStruct((PLANES * CHUNK, 2 * width), BF16)
    stat_shape = jax.ShapeDtypeStruct((3 * group, ROWS), F32)
    *mixed, stat_own = pl.pallas_call(
        functools.partial(forward, group, width),
        out_shape=[row_piece] * SLOTS + [stat_shape],
        in_specs=[smem] + [vmem] * (1 + 2 * SLOTS),
        out_specs=[vmem] * (SLOTS + 1),
        scratch_shapes=shared + [line, line, line],
        compiler_params=params,
        cost_estimate=pl.CostEstimate(flops=3 * work, bytes_accessed=1 << 22, transcendentals=0),
        name="forward",
    )(sc, start, *qd, *kv)
    stats = [stat_own] + [send(stat_own, perm=SWAP_Y[s]) for s in range(1, SLOTS)]
    mixed = [mixed[0]] + [send(mixed[s], perm=SWAP_Y[s]) for s in range(1, SLOTS)]
    outs = pl.pallas_call(
        functools.partial(backward, group, width),
        out_shape=[row_piece] * SLOTS + [key_piece] * SLOTS,
        in_specs=[smem] + [vmem] * (1 + 3 * SLOTS),
        out_specs=[vmem] * (2 * SLOTS),
        scratch_shapes=shared + [line, line],
        compiler_params=params,
        cost_estimate=pl.CostEstimate(flops=5 * work, bytes_accessed=1 << 22, transcendentals=0),
        name="backward",
    )(sc, start, *qd, *kv, *stats)
    dq, dkv = outs[:SLOTS], outs[SLOTS:]
    dkv = [dkv[0]] + [send(dkv[s], perm=SWAP_X[s]) for s in range(1, SLOTS)]
    dq = [dq[0]] + [send(dq[s], perm=SWAP_Y[s]) for s in range(1, SLOTS)]
    out_shape = jax.ShapeDtypeStruct((CHUNK, group * width), BF16)
    attended = pl.pallas_call(
        functools.partial(combine, group, width),
        out_shape=out_shape,
        in_specs=[vmem] * (2 * SLOTS),
        out_specs=vmem,
        name="combine",
    )(*mixed, *stats)
    grad_query = pl.pallas_call(
        functools.partial(gather_up, group, width),
        out_shape=out_shape,
        in_specs=[vmem] * SLOTS,
        out_specs=vmem,
        name="gather_up",
    )(*dq)
    own = sum(part.astype(F32) for part in dkv).astype(BF16)
    back = [
        send(own[dz * CHUNK : (dz + 1) * CHUNK], perm=[(b, a) for a, b in spread(dz)])
        for dz in range(PLANES)
    ]
    grad = sum(part.astype(F32) for part in back).astype(BF16)
    return attended, grad_query, grad[:, :width], grad[:, width:]


def solution(mesh):
    by_row = P(("qrow", "kcol"), "head")
    by_key = P(("kcol", "qrow"), "head")
    return jax.shard_map(
        local,
        mesh=mesh,
        in_specs=(by_row, by_key, by_key, by_row, P()),
        out_specs=(by_row, by_row, by_key, by_key),
        check_vma=False,
    )
```

```python
import functools
import math

import jax
import jax.numpy as jnp
from jax import lax
from jax.experimental import pallas as pl
from jax.experimental.pallas import tpu as pltpu
from jax.sharding import PartitionSpec as P

AXES = ("qrow", "kcol")
DEVICES = 128
CHUNK = 128
SLOTS = 4
TILES = 2
ROWS = SLOTS * CHUNK
PAIR = 2 * CHUNK
PLANE = 16 * CHUNK
NEG = -1e30
FLOOR = -1e29
LOG2E = math.log2(math.e)
F32 = jnp.float32
BF16 = jnp.bfloat16


def flip(mask):
    return [(d, d ^ mask) for d in range(DEVICES)]


X_LO, X_HI = flip(8), flip(4)
Y = [flip(s) for s in range(SLOTS)]
EVEN = flip(16)
ODD = [(d, (d + (16 if d // 16 % 2 else -16)) % DEVICES) for d in range(DEVICES)]


def dot(a, b):
    return lax.dot_general(a, b, (((1,), (0,)), ((), ())), preferred_element_type=F32)


def dot_t(a, b):
    return lax.dot_general(a, b, (((1,), (1,)), ((), ())), preferred_element_type=F32)


def fill(rows, keys, q_s, do_s, k_s, v_s, t_s, group, width, which):
    own, other, near, last, far_own, far_other = rows
    top, low = pl.ds(0, CHUNK), pl.ds(CHUNK, CHUNK)
    parts = [
        [(own, top), (near, top), (far_own, top), (last, top)],
        [(other, top), (near, low), (far_other, top), (last, low)],
    ]
    for t in range(TILES):
        for s in range(SLOTS):
            ref, at = parts[t][s]
            part = ref[at, :]
            to = pl.ds(s * CHUNK, CHUNK)
            for h in range(group):
                q_s[t, h, to, :] = part[:, h * width : (h + 1) * width]
                do_s[t, h, to, :] = part[:, (group + h) * width : (group + h + 1) * width]
    for n, ref in enumerate(keys):
        for u in range(2):
            part = ref[pl.ds(u * CHUNK, CHUNK), :]
            block, at = n // 2 * 2 + u, pl.ds(n % 2 * CHUNK, CHUNK)
            k_s[block, at, :] = part[:, :width]
            v_s[block, at, :] = part[:, width:]
            t_s[block, :, at] = jnp.transpose(part[:, which * width : (which + 1) * width])


def place(sc, pair, u, t):
    z, x_lo, x_hi, y = (sc[n] for n in range(4))
    plane = (4 * (x_hi ^ u) + y) * PLANE + x_lo * CHUNK
    one, two = plane + sc[8 + 2 * pair] * PAIR, plane + sc[9 + 2 * pair] * PAIR
    row = ((z * 4 + x_lo * 2 + x_hi) ^ (2 * t)) * ROWS
    first, last = sc[4 + 2 * t], sc[5 + 2 * t]
    low, high = jnp.minimum(one, two), jnp.maximum(one, two)
    needed = (low <= row + ROWS - 1) & (high + CHUNK - 1 >= first)
    whole = (high + CHUNK - 1 <= row) & (low >= last)
    return one, two, row, needed, whole


def allowed_of(sc, start, one, two, row):
    index = lax.broadcasted_iota(jnp.int32, (PAIR, 1), 0)
    key_at = index + jnp.where(index < CHUNK, one, two - CHUNK)
    row_at = row + (lax.broadcasted_iota(jnp.int32, (1, ROWS), 1) ^ (sc[3] * CHUNK))
    return (key_at >= start) & (key_at <= row_at)


def forward(group, width, pairs, sc, start, *refs):
    rows, keys, refs = refs[:6], refs[6 : 6 + 2 * pairs], refs[6 + 2 * pairs :]
    acc, stat, q_s, do_s, k_s, v_s, t_s, high, total, mixed = refs
    unit = LOG2E / math.sqrt(width)
    heads = range(group)
    fill(rows, keys, q_s, do_s, k_s, v_s, t_s, group, width, 1)
    acc[...] = jnp.zeros_like(acc)
    high[...] = jnp.full_like(high, FLOOR)
    total[...] = jnp.zeros_like(total)
    mixed[...] = jnp.zeros_like(mixed)

    def block(b, t, one, two, row, masked):
        scores = [dot_t(k_s[b], q_s[t, h]) for h in heads]
        dprobs = [dot_t(v_s[b], do_s[t, h]) for h in heads]
        if masked:
            allowed = allowed_of(sc, start[t], one, two, row)
            scores = [jnp.where(allowed, s, NEG) for s in scores]
        olds = [high[t, h] for h in heads]
        news = [jnp.maximum(o, jnp.max(s, axis=0, keepdims=True)) for o, s in zip(olds, scores)]
        shrinks = [jnp.exp2((o - n) * unit) for o, n in zip(olds, news)]
        es = [jnp.exp2(s * unit - n * unit) for s, n in zip(scores, news)]
        totals = [total[t, h] * shrinks[h] + jnp.sum(es[h], axis=0, keepdims=True) for h in heads]
        mixeds = [
            mixed[t, h] * shrinks[h] + jnp.sum(es[h] * dprobs[h], axis=0, keepdims=True)
            for h in heads
        ]
        accs = [acc[t, h] * shrinks[h] + dot(t_s[b], es[h].astype(BF16)) for h in heads]
        for h in heads:
            high[t, h] = news[h]
            total[t, h] = totals[h]
            mixed[t, h] = mixeds[h]
            acc[t, h] = accs[h]

    def step(n, carry):
        b, t = n // 2, n & 1
        one, two, row, needed, whole = place(sc, n // 4, (n // 2) & 1, t)

        @pl.when(needed & whole)
        def _():
            block(b, t, one, two, row, False)

        @pl.when(needed & jnp.logical_not(whole))
        def _():
            block(b, t, one, two, row, True)

        return carry

    lax.fori_loop(0, 4 * pairs, step, 0)
    for t in range(TILES):
        for h in heads:
            stat[t, h : h + 1, :] = high[t, h]
            stat[t, group + h : group + h + 1, :] = total[t, h]
            stat[t, 2 * group + h : 2 * group + h + 1, :] = mixed[t, h]


def backward(group, width, pairs, begins, ends, sc, start, *refs):
    rows, keys, refs = refs[:6], refs[6 : 6 + 2 * pairs], refs[6 + 2 * pairs :]
    scale = 1.0 / math.sqrt(width)
    unit = LOG2E * scale
    heads = range(group)
    if begins:
        stats, own, values, refs = refs[:SLOTS], refs[SLOTS], refs[SLOTS + 1], refs[SLOTS + 2 :]
    else:
        acc_in, lse_in, delta_in, refs = *refs[:3], refs[3:]
    dkv, refs = refs[0], refs[1:]
    if begins:
        mixed, refs = refs[: TILES * SLOTS], refs[TILES * SLOTS :]
    if ends:
        dq, refs = refs[: TILES * SLOTS], refs[TILES * SLOTS :]
    acc, lse, delta, q_s, do_s, k_s, v_s, t_s, grads = refs
    fill(rows, keys, q_s, do_s, k_s, v_s, t_s, group, width, 0)
    if begins:
        acc[...] = jnp.zeros_like(acc)
        for t in range(TILES):
            for u in range(SLOTS):
                at = pl.ds(u * CHUNK, CHUNK)
                parts = [stats[s][t, :, pl.ds((u ^ s) * CHUNK, CHUNK)] for s in range(SLOTS)]
                top = functools.reduce(jnp.maximum, [p[:group] for p in parts])
                weights = [jnp.exp2((p[:group] - top) * unit) for p in parts]
                total = sum(w * p[group : 2 * group] for w, p in zip(weights, parts))
                product = sum(w * p[2 * group :] for w, p in zip(weights, parts))
                low, small = top * unit + jnp.log2(total), product / total
                part = jnp.exp2(own[t, :group, at] * unit - low)
                for h in heads:
                    lse[t, h, :, at] = low[h : h + 1]
                    delta[t, h, :, at] = small[h : h + 1]
                    mixed[t * SLOTS + u][h * width : (h + 1) * width, :] = (
                        values[t, h, :, at] * part[h : h + 1]
                    ).astype(BF16)
    else:
        acc[...] = acc_in[...]
        lse[...] = lse_in[...]
        delta[...] = delta_in[...]

    def block(b, t, one, two, row, masked):
        scores = [dot_t(k_s[b], q_s[t, h]) for h in heads]
        dprobs = [dot_t(v_s[b], do_s[t, h]) for h in heads]
        if masked:
            allowed = allowed_of(sc, start[t], one, two, row)
            scores = [jnp.where(allowed, s, NEG) for s in scores]
        probs = [jnp.exp2(scores[h] * unit - lse[t, h]) for h in heads]
        dscores = [(probs[h] * (dprobs[h] - delta[t, h])).astype(BF16) for h in heads]
        lows = [p.astype(BF16) for p in probs]
        dk = sum(dot(dscores[h], q_s[t, h]) for h in heads)
        dv = sum(dot(lows[h], do_s[t, h]) for h in heads)
        accs = [acc[t, h] + dot(t_s[b], dscores[h]) for h in heads]
        for h in heads:
            acc[t, h] = accs[h]
        grads[:, :width] = grads[:, :width] + dk * scale
        grads[:, width:] = grads[:, width:] + dv

    def step(b, carry):
        grads[...] = jnp.zeros_like(grads)

        def tile(t, carry):
            one, two, row, needed, whole = place(sc, b // 2, b & 1, t)

            @pl.when(needed & whole)
            def _():
                block(b, t, one, two, row, False)

            @pl.when(needed & jnp.logical_not(whole))
            def _():
                block(b, t, one, two, row, True)

            return carry

        lax.fori_loop(0, TILES, tile, 0)
        for n in range(2):
            dkv[b // 2 * 2 + n, b & 1] = grads[n * CHUNK : (n + 1) * CHUNK, :].astype(BF16)
        return carry

    lax.fori_loop(0, 2 * pairs, step, 0)
    if ends:
        for t in range(TILES):
            for h in heads:
                value = (acc[t, h] * scale).astype(BF16)
                for s in range(SLOTS):
                    dq[t * SLOTS + s][h * width : (h + 1) * width, :] = value[
                        :, s * CHUNK : (s + 1) * CHUNK
                    ]


def combine(group, width, *refs):
    parts, out = refs[:-1], refs[-1]
    for h in range(group):
        at = pl.ds(h * width, width)
        whole = sum(part[at, :].astype(F32) for part in parts)
        out[:, at] = jnp.transpose(whole).astype(BF16)


def add(*parts):
    return sum(part.astype(F32) for part in parts).astype(BF16)


def local(query, key, value, dout, document):
    width = key.shape[1]
    group = query.shape[1] // width
    send = functools.partial(lax.ppermute, axis_name=AXES)
    qrow, kcol = lax.axis_index("qrow"), lax.axis_index("kcol")
    z, x_lo, x_hi, y = qrow // 2, qrow % 2, kcol // 4, kcol % 4

    key_home = jnp.concatenate([key, value], axis=1)
    row_home = jnp.concatenate([query, dout], axis=1)
    row_other = send(row_home, perm=X_LO)
    own = jnp.concatenate([key_home, send(key_home, perm=X_HI)], axis=0)
    a, b = [own], [own]
    for k in range(3):
        a.append(send(b[k], perm=EVEN))
        b.append(send(a[k], perm=ODD))
    both = jnp.concatenate([row_home, row_other], axis=0)
    near, last = send(both, perm=Y[1]), send(both, perm=Y[3])
    far_own, far_other = send(last[:CHUNK], perm=Y[1]), send(near[CHUNK:], perm=Y[3])
    opposite = jnp.concatenate(
        [send(b[3][:CHUNK], perm=EVEN), send(a[3][CHUNK:], perm=ODD)], axis=0
    )
    rows = [row_home, row_other, near, last, far_own, far_other]
    keys = [a[0], a[1], b[1], b[2], a[2], a[3], b[3], opposite]

    numbers = jnp.arange(8, dtype=jnp.int32)
    starts = jnp.sum((document[None, :] < numbers[:, None]).astype(jnp.int32), axis=1)
    place_of = qrow * 8 + kcol
    row_doc = jnp.concatenate(
        [
            lax.dynamic_slice_in_dim(document, (place_of ^ (8 * t + s)) * CHUNK, CHUNK)
            for t in range(TILES)
            for s in range(SLOTS)
        ]
    )
    start = jnp.sum(jnp.where(row_doc[None] == numbers[:, None], starts[:, None], 0), axis=0)
    start = start.reshape(TILES, 1, ROWS)
    side = 1 - 2 * (z % 2)
    sources = jnp.stack([z + side * k for k in (0, 1, -1, -2, 2, 3, -3, 4)]) & 7
    sc = jnp.concatenate(
        [
            jnp.stack([z, x_lo, x_hi, y]),
            jnp.stack([jnp.min(start, axis=(1, 2)), jnp.max(start, axis=(1, 2))], 1).reshape(-1),
            sources,
        ]
    ).astype(jnp.int32)

    smem = pl.BlockSpec(memory_space=pltpu.SMEM)
    vmem = pl.BlockSpec(memory_space=pltpu.VMEM)
    params = pltpu.CompilerParams(vmem_limit_bytes=56 * 1024 * 1024)

    def cost(dots, pairs):
        work = TILES * ROWS * group * pairs * 2 * PAIR * width * 2
        return pl.CostEstimate(flops=dots * work // 2, bytes_accessed=1 << 23, transcendentals=0)

    def scratch(pairs):
        return [
            pltpu.VMEM((TILES, group, ROWS, width), BF16),
            pltpu.VMEM((TILES, group, ROWS, width), BF16),
            pltpu.VMEM((2 * pairs, PAIR, width), BF16),
            pltpu.VMEM((2 * pairs, PAIR, width), BF16),
            pltpu.VMEM((2 * pairs, width, PAIR), BF16),
        ]

    line = (TILES, group, 1, ROWS)
    acc_shape = jax.ShapeDtypeStruct((TILES, group, width, ROWS), F32)
    line_shape = jax.ShapeDtypeStruct(line, F32)
    stat_shape = jax.ShapeDtypeStruct((TILES, 3 * group, ROWS), F32)
    piece = jax.ShapeDtypeStruct((group * width, CHUNK), BF16)

    values, stat = pl.pallas_call(
        functools.partial(forward, group, width, 4),
        out_shape=[acc_shape, stat_shape],
        in_specs=[smem] + [vmem] * 15,
        out_specs=[vmem] * 2,
        scratch_shapes=scratch(4) + [pltpu.VMEM(line, F32)] * 3,
        compiler_params=params,
        cost_estimate=cost(3, 4),
        name="forward",
    )(sc, start, *rows, *keys)

    unit = LOG2E / math.sqrt(width)
    other = send(stat, perm=X_LO)[::-1]
    top = jnp.maximum(stat[:, :group], other[:, :group])
    mine, theirs = (jnp.exp2((s[:, :group] - top) * unit) for s in (stat, other))
    merged = jnp.concatenate(
        [top]
        + [
            stat[:, n * group : (n + 1) * group] * mine
            + other[:, n * group : (n + 1) * group] * theirs
            for n in (1, 2)
        ],
        axis=1,
    )
    stats = [merged] + [send(merged, perm=Y[s]) for s in range(1, SLOTS)]

    def back(pairs, begins, ends, sc, keys, *more):
        dkv_shape = jax.ShapeDtypeStruct((2 * pairs, 2, CHUNK, 2 * width), BF16)
        shapes = [dkv_shape] + [piece] * (TILES * SLOTS * (begins + ends))
        carried = [acc_shape, line_shape, line_shape]
        more_scratch = scratch(pairs) + [pltpu.VMEM((PAIR, 2 * width), F32)]
        if ends:
            more_scratch = [pltpu.VMEM(s.shape, F32) for s in carried] + more_scratch
        else:
            shapes = shapes + carried
        return pl.pallas_call(
            functools.partial(backward, group, width, pairs, begins, ends),
            out_shape=shapes,
            in_specs=[smem] + [vmem] * (7 + 2 * pairs + len(more)),
            out_specs=[vmem] * len(shapes),
            scratch_shapes=more_scratch,
            compiler_params=params,
            cost_estimate=cost(5, pairs),
            name="backward_begin" if begins else "backward_end",
        )(sc, start, *rows, *keys, *more)

    def shifted(skip):
        return jnp.concatenate([sc[:8], sc[8 + skip :]])

    late = back(2, True, False, shifted(4), keys[4:], *stats, stat, values)
    far, mixed, carried = late[0], late[1 : 1 + TILES * SLOTS], late[1 + TILES * SLOTS :]
    end = back(2, False, True, sc, keys[:4], *carried)
    close, dq = end[0], end[1:]

    def spread(parts):
        masks = [8 * t + s for t in range(TILES) for s in range(SLOTS)]
        return [parts[0]] + [send(p, perm=flip(m)) for p, m in zip(parts[1:], masks[1:])]

    flat = (PAIR, 2 * width)
    one = send(far[3, 0], perm=EVEN)
    two = send(far[3, 1], perm=ODD)
    mixed = spread(mixed)
    gb = jnp.concatenate([add(far[2, 0], one), far[2, 1]], axis=0)
    ga = jnp.concatenate([far[1, 0], add(far[1, 1], two)], axis=0)
    for pa, pb in ((far[0], close[3]), (close[1], close[2])):
        sent_b, sent_a = send(gb, perm=ODD), send(ga, perm=EVEN)
        ga, gb = add(pa.reshape(flat), sent_b), add(pb.reshape(flat), sent_a)
    grad = add(close[0].reshape(flat), send(ga, perm=EVEN), send(gb, perm=ODD))
    dq = spread(dq)
    grad = add(grad[:CHUNK], send(grad[CHUNK:], perm=X_HI))

    outs = [
        pl.pallas_call(
            functools.partial(combine, group, width),
            out_shape=jax.ShapeDtypeStruct((CHUNK, group * width), BF16),
            in_specs=[vmem] * (TILES * SLOTS),
            out_specs=vmem,
            name=name,
        )(*parts)
        for parts, name in ((mixed, "attended"), (dq, "grad_query"))
    ]
    return *outs, grad[:, :width], grad[:, width:]


def solution(mesh):
    by_row = P(("qrow", "kcol"), "head")
    by_key = P(("kcol", "qrow"), "head")
    return jax.shard_map(
        local,
        mesh=mesh,
        in_specs=(by_row, by_key, by_key, by_row, P()),
        out_specs=(by_row, by_row, by_key, by_key),
        check_vma=False,
    )
```

```python
import functools
import math

import jax
import jax.numpy as jnp
from jax import lax
from jax.experimental import pallas as pl
from jax.experimental.pallas import tpu as pltpu
from jax.sharding import PartitionSpec as P

AXES = ("qrow", "kcol")
DEVICES = 128
CHUNK = 128
SLOTS = 4
TILES = 2
ROWS = SLOTS * CHUNK
PAIR = 2 * CHUNK
PLANE = 16 * CHUNK
DOCS = 8
NEG = -1e30
FLOOR = -1e29
LOG2E = math.log2(math.e)
F32 = jnp.float32
BF16 = jnp.bfloat16


def flip(mask):
    return [(d, d ^ mask) for d in range(DEVICES)]


X_LO, X_HI = flip(8), flip(4)
Y = [flip(s) for s in range(SLOTS)]
EVEN = flip(16)
ODD = [(d, (d + (16 if d // 16 % 2 else -16)) % DEVICES) for d in range(DEVICES)]


def dot(a, b):
    return lax.dot_general(a, b, (((1,), (0,)), ((), ())), preferred_element_type=F32)


def dot_t(a, b):
    return lax.dot_general(a, b, (((1,), (1,)), ((), ())), preferred_element_type=F32)


def fill(rows, keys, q_s, do_s, k_s, v_s, t_s, group, width, which):
    own, other, near, last, far_own, far_other = rows
    top, low = pl.ds(0, CHUNK), pl.ds(CHUNK, CHUNK)
    parts = [
        [(own, top), (near, top), (far_own, top), (last, top)],
        [(other, top), (near, low), (far_other, top), (last, low)],
    ]
    for t in range(TILES):
        for s in range(SLOTS):
            ref, at = parts[t][s]
            part = ref[at, :]
            to = pl.ds(s * CHUNK, CHUNK)
            for h in range(group):
                q_s[t, h, to, :] = part[:, h * width : (h + 1) * width]
                do_s[t, h, to, :] = part[:, (group + h) * width : (group + h + 1) * width]
    for n, ref in enumerate(keys):
        for u in range(2):
            part = ref[pl.ds(u * CHUNK, CHUNK), :]
            block, at = n // 2 * 2 + u, pl.ds(n % 2 * CHUNK, CHUNK)
            k_s[block, at, :] = part[:, :width]
            v_s[block, at, :] = part[:, width:]
            t_s[block, :, at] = jnp.transpose(part[:, which * width : (which + 1) * width])


def start_of(sc, row):
    start = 0
    for n in range(DOCS):
        one = sc[4 + n]
        start = jnp.maximum(start, jnp.where(one <= row, one, 0))
    return start


def place(sc, pair, u, t):
    z, x_lo, x_hi, y = (sc[n] for n in range(4))
    plane = (4 * (x_hi ^ u) + y) * PLANE + x_lo * CHUNK
    one, two = (plane + sc[4 + DOCS + 2 * pair + n] * PAIR for n in range(2))
    row = ((z * 4 + x_lo * 2 + x_hi) ^ (2 * t)) * ROWS
    low, high = jnp.minimum(one, two), jnp.maximum(one, two)
    needed = (low <= row + ROWS - 1) & (high + CHUNK - 1 >= start_of(sc, row))
    whole = (high + CHUNK - 1 <= row) & (low >= start_of(sc, row + ROWS - 1))
    return one, two, row, needed, whole


def allowed_of(sc, one, two, row):
    index = lax.broadcasted_iota(jnp.int32, (PAIR, 1), 0)
    key_at = index + jnp.where(index < CHUNK, one, two - CHUNK)
    row_at = row + (lax.broadcasted_iota(jnp.int32, (1, ROWS), 1) ^ (sc[3] * CHUNK))
    return (key_at >= start_of(sc, row_at)) & (key_at <= row_at)


def pack(query, key, value, dout, rows, keys):
    width = query.shape[1]
    rows[:, :width] = query[...]
    rows[:, width:] = dout[...]
    width = key.shape[1]
    keys[:, :width] = key[...]
    keys[:, width:] = value[...]


def forward(group, width, pairs, sc, *refs):
    rows, keys, refs = refs[:6], refs[6 : 6 + 2 * pairs], refs[6 + 2 * pairs :]
    acc, stat, q_s, do_s, k_s, v_s, t_s, high, total, mixed = refs
    unit = LOG2E / math.sqrt(width)
    heads = range(group)
    fill(rows, keys, q_s, do_s, k_s, v_s, t_s, group, width, 1)
    acc[...] = jnp.zeros_like(acc)
    high[...] = jnp.full_like(high, FLOOR)
    total[...] = jnp.zeros_like(total)
    mixed[...] = jnp.zeros_like(mixed)

    def block(b, t, one, two, row, masked):
        scores = [dot_t(k_s[b], q_s[t, h]) for h in heads]
        dprobs = [dot_t(v_s[b], do_s[t, h]) for h in heads]
        if masked:
            allowed = allowed_of(sc, one, two, row)
            scores = [jnp.where(allowed, s, NEG) for s in scores]
        olds = [high[t, h] for h in heads]
        news = [jnp.maximum(o, jnp.max(s, axis=0, keepdims=True)) for o, s in zip(olds, scores)]
        shrinks = [jnp.exp2((o - n) * unit) for o, n in zip(olds, news)]
        es = [jnp.exp2(s * unit - n * unit) for s, n in zip(scores, news)]
        totals = [total[t, h] * shrinks[h] + jnp.sum(es[h], axis=0, keepdims=True) for h in heads]
        mixeds = [
            mixed[t, h] * shrinks[h] + jnp.sum(es[h] * dprobs[h], axis=0, keepdims=True)
            for h in heads
        ]
        accs = [acc[t, h] * shrinks[h] + dot(t_s[b], es[h].astype(BF16)) for h in heads]
        for h in heads:
            high[t, h] = news[h]
            total[t, h] = totals[h]
            mixed[t, h] = mixeds[h]
            acc[t, h] = accs[h]

    def step(n, carry):
        b, t = n // 2, n & 1
        one, two, row, needed, whole = place(sc, n // 4, (n // 2) & 1, t)

        @pl.when(needed & whole)
        def _():
            block(b, t, one, two, row, False)

        @pl.when(needed & jnp.logical_not(whole))
        def _():
            block(b, t, one, two, row, True)

        return carry

    lax.fori_loop(0, 4 * pairs, step, 0)
    for t in range(TILES):
        for h in heads:
            stat[t, h : h + 1, :] = high[t, h]
            stat[t, group + h : group + h + 1, :] = total[t, h]
            stat[t, 2 * group + h : 2 * group + h + 1, :] = mixed[t, h]


def backward(group, width, pairs, begins, ends, sc, *refs):
    rows, keys, refs = refs[:6], refs[6 : 6 + 2 * pairs], refs[6 + 2 * pairs :]
    scale = 1.0 / math.sqrt(width)
    unit = LOG2E * scale
    heads = range(group)
    if begins:
        stats, own, values, refs = refs[:SLOTS], refs[SLOTS], refs[SLOTS + 1], refs[SLOTS + 2 :]
    else:
        acc_in, lse_in, delta_in, refs = *refs[:3], refs[3:]
    dkv, refs = refs[0], refs[1:]
    if begins:
        mixed, refs = refs[:SLOTS], refs[SLOTS:]
    if ends:
        dq, refs = refs[:SLOTS], refs[SLOTS:]
    acc, lse, delta, q_s, do_s, k_s, v_s, t_s, grads = refs
    fill(rows, keys, q_s, do_s, k_s, v_s, t_s, group, width, 0)
    if begins:
        acc[...] = jnp.zeros_like(acc)
        for t in range(TILES):
            for u in range(SLOTS):
                at = pl.ds(u * CHUNK, CHUNK)
                parts = [stats[s][t, :, pl.ds((u ^ s) * CHUNK, CHUNK)] for s in range(SLOTS)]
                top = functools.reduce(jnp.maximum, [p[:group] for p in parts])
                weights = [jnp.exp2((p[:group] - top) * unit) for p in parts]
                total = sum(w * p[group : 2 * group] for w, p in zip(weights, parts))
                product = sum(w * p[2 * group :] for w, p in zip(weights, parts))
                low, small = top * unit + jnp.log2(total), product / total
                part = jnp.exp2(own[t, :group, at] * unit - low)
                for h in heads:
                    lse[t, h, :, at] = low[h : h + 1]
                    delta[t, h, :, at] = small[h : h + 1]
                    mixed[u][t, h * width : (h + 1) * width, :] = (
                        values[t, h, :, at] * part[h : h + 1]
                    ).astype(BF16)
    else:
        acc[...] = acc_in[...]
        lse[...] = lse_in[...]
        delta[...] = delta_in[...]

    def block(b, t, one, two, row, masked):
        scores = [dot_t(k_s[b], q_s[t, h]) for h in heads]
        dprobs = [dot_t(v_s[b], do_s[t, h]) for h in heads]
        if masked:
            allowed = allowed_of(sc, one, two, row)
            scores = [jnp.where(allowed, s, NEG) for s in scores]
        probs = [jnp.exp2(scores[h] * unit - lse[t, h]) for h in heads]
        dscores = [(probs[h] * (dprobs[h] - delta[t, h])).astype(BF16) for h in heads]
        lows = [p.astype(BF16) for p in probs]
        dk = sum(dot(dscores[h], q_s[t, h]) for h in heads)
        dv = sum(dot(lows[h], do_s[t, h]) for h in heads)
        accs = [acc[t, h] + dot(t_s[b], dscores[h]) for h in heads]
        for h in heads:
            acc[t, h] = accs[h]
        grads[:, :width] = grads[:, :width] + dk * scale
        grads[:, width:] = grads[:, width:] + dv

    def step(b, carry):
        grads[...] = jnp.zeros_like(grads)

        def tile(t, carry):
            one, two, row, needed, whole = place(sc, b // 2, b & 1, t)

            @pl.when(needed & whole)
            def _():
                block(b, t, one, two, row, False)

            @pl.when(needed & jnp.logical_not(whole))
            def _():
                block(b, t, one, two, row, True)

            return carry

        lax.fori_loop(0, TILES, tile, 0)
        for n in range(2):
            dkv[b // 2 * 2 + n, b & 1] = grads[n * CHUNK : (n + 1) * CHUNK, :].astype(BF16)
        return carry

    lax.fori_loop(0, 2 * pairs, step, 0)
    if ends:
        for t in range(TILES):
            for h in heads:
                value = (acc[t, h] * scale).astype(BF16)
                for s in range(SLOTS):
                    dq[s][t, h * width : (h + 1) * width, :] = value[
                        :, s * CHUNK : (s + 1) * CHUNK
                    ]


def combine(group, width, *refs):
    parts, out = refs[:-1], refs[-1]
    for h in range(group):
        at = pl.ds(h * width, width)
        whole = sum(part[at, :].astype(F32) for part in parts)
        out[:, at] = jnp.transpose(whole).astype(BF16)


def add(*parts):
    return sum(part.astype(F32) for part in parts).astype(BF16)


def local(query, key, value, dout, document):
    width = key.shape[1]
    group = query.shape[1] // width
    send = functools.partial(lax.ppermute, axis_name=AXES)
    qrow, kcol = lax.axis_index("qrow"), lax.axis_index("kcol")
    z, x_lo, x_hi, y = qrow // 2, qrow % 2, kcol // 4, kcol % 4

    row_home, key_home = pl.pallas_call(
        pack,
        out_shape=[
            jax.ShapeDtypeStruct((CHUNK, 2 * group * width), BF16),
            jax.ShapeDtypeStruct((CHUNK, 2 * width), BF16),
        ],
        name="pack",
    )(query, key, value, dout)
    row_other = send(row_home, perm=X_LO)
    own = jnp.concatenate([key_home, send(key_home, perm=X_HI)], axis=0)
    a, b = [own], [own]
    for k in range(3):
        a.append(send(b[k], perm=EVEN))
        b.append(send(a[k], perm=ODD))
    both = jnp.concatenate([row_home, row_other], axis=0)
    near, last = send(both, perm=Y[1]), send(both, perm=Y[3])
    far_own, far_other = send(last[:CHUNK], perm=Y[1]), send(near[CHUNK:], perm=Y[3])
    opposite = jnp.concatenate(
        [send(b[3][:CHUNK], perm=EVEN), send(a[3][CHUNK:], perm=ODD)], axis=0
    )
    rows = [row_home, row_other, near, last, far_own, far_other]
    keys = [a[0], a[1], b[1], b[2], a[2], a[3], b[3], opposite]

    numbers = jnp.arange(DOCS, dtype=jnp.int32)
    starts = jnp.sum((document[None, :] < numbers[:, None]).astype(jnp.int32), axis=1)
    side = 1 - 2 * (z % 2)
    sources = jnp.stack([z + side * k for k in (0, 1, -1, -2, 2, 3, -3, 4)]) & 7
    sc = jnp.concatenate([jnp.stack([z, x_lo, x_hi, y]), starts, sources]).astype(jnp.int32)

    smem = pl.BlockSpec(memory_space=pltpu.SMEM)
    vmem = pl.BlockSpec(memory_space=pltpu.VMEM)
    params = pltpu.CompilerParams(vmem_limit_bytes=56 * 1024 * 1024)

    def cost(dots, pairs):
        work = TILES * ROWS * group * pairs * 2 * PAIR * width * 2
        return pl.CostEstimate(flops=dots * work // 2, bytes_accessed=1 << 23, transcendentals=0)

    def scratch(pairs):
        return [
            pltpu.VMEM((TILES, group, ROWS, width), BF16),
            pltpu.VMEM((TILES, group, ROWS, width), BF16),
            pltpu.VMEM((2 * pairs, PAIR, width), BF16),
            pltpu.VMEM((2 * pairs, PAIR, width), BF16),
            pltpu.VMEM((2 * pairs, width, PAIR), BF16),
        ]

    line = (TILES, group, 1, ROWS)
    acc_shape = jax.ShapeDtypeStruct((TILES, group, width, ROWS), F32)
    line_shape = jax.ShapeDtypeStruct(line, F32)
    stat_shape = jax.ShapeDtypeStruct((TILES, 3 * group, ROWS), F32)
    piece = jax.ShapeDtypeStruct((TILES, group * width, CHUNK), BF16)

    values, stat = pl.pallas_call(
        functools.partial(forward, group, width, 4),
        out_shape=[acc_shape, stat_shape],
        in_specs=[smem] + [vmem] * 14,
        out_specs=[vmem] * 2,
        scratch_shapes=scratch(4) + [pltpu.VMEM(line, F32)] * 3,
        compiler_params=params,
        cost_estimate=cost(3, 4),
        name="forward",
    )(sc, *rows, *keys)

    unit = LOG2E / math.sqrt(width)
    other = send(stat, perm=X_LO)[::-1]
    top = jnp.maximum(stat[:, :group], other[:, :group])
    mine, theirs = (jnp.exp2((s[:, :group] - top) * unit) for s in (stat, other))
    merged = jnp.concatenate(
        [top]
        + [
            stat[:, n * group : (n + 1) * group] * mine
            + other[:, n * group : (n + 1) * group] * theirs
            for n in (1, 2)
        ],
        axis=1,
    )
    stats = [merged] + [send(merged, perm=Y[s]) for s in range(1, SLOTS)]

    def back(pairs, begins, ends, sc, keys, *more):
        dkv_shape = jax.ShapeDtypeStruct((2 * pairs, 2, CHUNK, 2 * width), BF16)
        shapes = [dkv_shape] + [piece] * (SLOTS * (begins + ends))
        carried = [acc_shape, line_shape, line_shape]
        more_scratch = scratch(pairs) + [pltpu.VMEM((PAIR, 2 * width), F32)]
        if ends:
            more_scratch = [pltpu.VMEM(s.shape, F32) for s in carried] + more_scratch
        else:
            shapes = shapes + carried
        return pl.pallas_call(
            functools.partial(backward, group, width, pairs, begins, ends),
            out_shape=shapes,
            in_specs=[smem] + [vmem] * (6 + 2 * pairs + len(more)),
            out_specs=[vmem] * len(shapes),
            scratch_shapes=more_scratch,
            compiler_params=params,
            cost_estimate=cost(5, pairs),
            name="backward_begin" if begins else "backward_end",
        )(sc, *rows, *keys, *more)

    def shifted(skip):
        return jnp.concatenate([sc[: 4 + DOCS], sc[4 + DOCS + skip :]])

    late = back(2, True, False, shifted(4), keys[4:], *stats, stat, values)
    far, mixed, carried = late[0], late[1 : 1 + SLOTS], late[1 + SLOTS :]
    end = back(2, False, True, sc, keys[:4], *carried)
    close, dq = end[0], end[1:]

    def over_y(parts):
        return add(parts[0], *[send(parts[s], perm=Y[s]) for s in range(1, SLOTS)])

    flat = (PAIR, 2 * width)
    one = send(far[3, 0], perm=EVEN)
    two = send(far[3, 1], perm=ODD)
    mixed = over_y(mixed)
    mixed = [mixed[0], send(mixed[1], perm=X_LO)]
    gb = jnp.concatenate([add(far[2, 0], one), far[2, 1]], axis=0)
    ga = jnp.concatenate([far[1, 0], add(far[1, 1], two)], axis=0)
    for pa, pb in ((far[0], close[3]), (close[1], close[2])):
        sent_b, sent_a = send(gb, perm=ODD), send(ga, perm=EVEN)
        ga, gb = add(pa.reshape(flat), sent_b), add(pb.reshape(flat), sent_a)
    grad = add(close[0].reshape(flat), send(ga, perm=EVEN), send(gb, perm=ODD))
    dq = over_y(dq)
    dq = [dq[0], send(dq[1], perm=X_LO)]
    grad = add(grad[:CHUNK], send(grad[CHUNK:], perm=X_HI))

    outs = [
        pl.pallas_call(
            functools.partial(combine, group, width),
            out_shape=jax.ShapeDtypeStruct((CHUNK, group * width), BF16),
            in_specs=[vmem] * TILES,
            out_specs=vmem,
            name=name,
        )(*parts)
        for parts, name in ((mixed, "attended"), (dq, "grad_query"))
    ]
    return *outs, grad[:, :width], grad[:, width:]


def solution(mesh):
    by_row = P(("qrow", "kcol"), "head")
    by_key = P(("kcol", "qrow"), "head")
    return jax.shard_map(
        local,
        mesh=mesh,
        in_specs=(by_row, by_key, by_key, by_row, P()),
        out_specs=(by_row, by_row, by_key, by_key),
        check_vma=False,
    )
```

```python
import functools
import math

import jax
import jax.numpy as jnp
from jax import lax
from jax.experimental import pallas as pl
from jax.experimental.pallas import tpu as pltpu
from jax.sharding import PartitionSpec as P

AXES = ("qrow", "kcol")
DEVICES = 128
CHUNK = 128
SLOTS = 4
TILES = 2
ROWS = SLOTS * CHUNK
PAIR = 2 * CHUNK
PLANE = 16 * CHUNK
DOCS = 8
NEG = -1e30
FLOOR = -1e29
LOG2E = math.log2(math.e)
F32 = jnp.float32
BF16 = jnp.bfloat16


def flip(mask):
    return [(d, d ^ mask) for d in range(DEVICES)]


Y = [flip(s) for s in range(SLOTS)]
X = [flip(m) for m in (0, 8, 4, 12)]
NEXT = flip(16)
NEAR = flip(32)
REST = [(d, (d + (32 if d // 32 % 2 else -32)) % DEVICES) for d in range(DEVICES)]


def dot(a, b):
    return lax.dot_general(a, b, (((1,), (0,)), ((), ())), preferred_element_type=F32)


def dot_t(a, b):
    return lax.dot_general(a, b, (((1,), (1,)), ((), ())), preferred_element_type=F32)


def fill(rows, keys, q_s, do_s, k_s, v_s, t_s, group, width, which):
    own, other, near, last, far_own, far_other = rows
    top, low = pl.ds(0, CHUNK), pl.ds(CHUNK, CHUNK)
    parts = [
        [(own, top), (near, top), (far_own, top), (last, top)],
        [(other, top), (near, low), (far_other, top), (last, low)],
    ]
    for t in range(TILES):
        for s in range(SLOTS):
            ref, at = parts[t][s]
            part = ref[at, :]
            to = pl.ds(s * CHUNK, CHUNK)
            for h in range(group):
                q_s[t, h, to, :] = part[:, h * width : (h + 1) * width]
                do_s[t, h, to, :] = part[:, (group + h) * width : (group + h + 1) * width]
    for n, ref in enumerate(keys):
        for u in range(2):
            part = ref[pl.ds(u * PAIR, PAIR), :]
            k_s[2 * n + u] = part[:, :width]
            v_s[2 * n + u] = part[:, width:]
            t_s[2 * n + u] = jnp.transpose(part[:, which * width : (which + 1) * width])


def start_of(sc, row):
    start = 0
    for n in range(DOCS):
        one = sc[4 + n]
        start = jnp.maximum(start, jnp.where(one <= row, one, 0))
    return start


def place(sc, block, t):
    z, x_lo, x_hi, y = (sc[n] for n in range(4))
    base = (4 * (x_hi ^ (block & 1)) + y) * PLANE + sc[4 + DOCS + block // 2] * PAIR
    row = ((z * 4 + x_lo * 2 + x_hi) ^ (4 * t)) * ROWS
    needed = (base <= row + ROWS - 1) & (base + PAIR - 1 >= start_of(sc, row))
    whole = (base + PAIR - 1 <= row) & (base >= start_of(sc, row + ROWS - 1))
    return base, row, needed, whole


def allowed_of(sc, base, row):
    key_at = base + (lax.broadcasted_iota(jnp.int32, (PAIR, 1), 0) ^ (sc[1] * CHUNK))
    row_at = row + (lax.broadcasted_iota(jnp.int32, (1, ROWS), 1) ^ (sc[3] * CHUNK))
    return (key_at >= start_of(sc, row_at)) & (key_at <= row_at)


def pack(query, key, value, dout, rows, keys):
    width = query.shape[1]
    rows[:, :width] = query[...]
    rows[:, width:] = dout[...]
    width = key.shape[1]
    keys[:, :width] = key[...]
    keys[:, width:] = value[...]


def forward(group, width, pieces, sc, *refs):
    rows, keys, refs = refs[:6], refs[6 : 6 + pieces], refs[6 + pieces :]
    acc, stat, q_s, do_s, k_s, v_s, t_s, high, total, mixed = refs
    unit = LOG2E / math.sqrt(width)
    heads = range(group)
    fill(rows, keys, q_s, do_s, k_s, v_s, t_s, group, width, 1)
    acc[...] = jnp.zeros_like(acc)
    high[...] = jnp.full_like(high, FLOOR)
    total[...] = jnp.zeros_like(total)
    mixed[...] = jnp.zeros_like(mixed)

    def block(b, t, base, row, masked):
        scores = [dot_t(k_s[b], q_s[t, h]) for h in heads]
        dprobs = [dot_t(v_s[b], do_s[t, h]) for h in heads]
        if masked:
            allowed = allowed_of(sc, base, row)
            scores = [jnp.where(allowed, s, NEG) for s in scores]
        olds = [high[t, h] for h in heads]
        news = [jnp.maximum(o, jnp.max(s, axis=0, keepdims=True)) for o, s in zip(olds, scores)]
        shrinks = [jnp.exp2((o - n) * unit) for o, n in zip(olds, news)]
        es = [jnp.exp2(s * unit - n * unit) for s, n in zip(scores, news)]
        totals = [total[t, h] * shrinks[h] + jnp.sum(es[h], axis=0, keepdims=True) for h in heads]
        mixeds = [
            mixed[t, h] * shrinks[h] + jnp.sum(es[h] * dprobs[h], axis=0, keepdims=True)
            for h in heads
        ]
        accs = [acc[t, h] * shrinks[h] + dot(t_s[b], es[h].astype(BF16)) for h in heads]
        for h in heads:
            high[t, h] = news[h]
            total[t, h] = totals[h]
            mixed[t, h] = mixeds[h]
            acc[t, h] = accs[h]

    def step(n, carry):
        b, t = n // 2, n & 1
        base, row, needed, whole = place(sc, b, t)

        @pl.when(needed & whole)
        def _():
            block(b, t, base, row, False)

        @pl.when(needed & jnp.logical_not(whole))
        def _():
            block(b, t, base, row, True)

        return carry

    lax.fori_loop(0, 4 * pieces, step, 0)
    for t in range(TILES):
        for h in heads:
            stat[t, h : h + 1, :] = high[t, h]
            stat[t, group + h : group + h + 1, :] = total[t, h]
            stat[t, 2 * group + h : 2 * group + h + 1, :] = mixed[t, h]


def backward(group, width, pieces, begins, ends, sc, *refs):
    rows, keys, refs = refs[:6], refs[6 : 6 + pieces], refs[6 + pieces :]
    scale = 1.0 / math.sqrt(width)
    unit = LOG2E * scale
    heads = range(group)
    if begins:
        stats, own, values, refs = refs[:SLOTS], refs[SLOTS], refs[SLOTS + 1], refs[SLOTS + 2 :]
    else:
        acc_in, lse_in, delta_in, refs = *refs[:3], refs[3:]
    dkv, refs = refs[0], refs[1:]
    if begins:
        mixed, refs = refs[:SLOTS], refs[SLOTS:]
    if ends:
        dq, refs = refs[:SLOTS], refs[SLOTS:]
    acc, lse, delta, q_s, do_s, k_s, v_s, t_s, grads = refs
    fill(rows, keys, q_s, do_s, k_s, v_s, t_s, group, width, 0)
    if begins:
        acc[...] = jnp.zeros_like(acc)
        for t in range(TILES):
            for u in range(SLOTS):
                at = pl.ds(u * CHUNK, CHUNK)
                parts = [stats[s][t, :, pl.ds((u ^ s) * CHUNK, CHUNK)] for s in range(SLOTS)]
                top = functools.reduce(jnp.maximum, [p[:group] for p in parts])
                weights = [jnp.exp2((p[:group] - top) * unit) for p in parts]
                total = sum(w * p[group : 2 * group] for w, p in zip(weights, parts))
                product = sum(w * p[2 * group :] for w, p in zip(weights, parts))
                low, small = top * unit + jnp.log2(total), product / total
                part = jnp.exp2(own[t, :group, at] * unit - low)
                for h in heads:
                    lse[t, h, :, at] = low[h : h + 1]
                    delta[t, h, :, at] = small[h : h + 1]
                    mixed[u][t, h * width : (h + 1) * width, :] = (
                        values[t, h, :, at] * part[h : h + 1]
                    ).astype(BF16)
    else:
        acc[...] = acc_in[...]
        lse[...] = lse_in[...]
        delta[...] = delta_in[...]

    def block(b, t, base, row, masked):
        scores = [dot_t(k_s[b], q_s[t, h]) for h in heads]
        dprobs = [dot_t(v_s[b], do_s[t, h]) for h in heads]
        if masked:
            allowed = allowed_of(sc, base, row)
            scores = [jnp.where(allowed, s, NEG) for s in scores]
        probs = [jnp.exp2(scores[h] * unit - lse[t, h]) for h in heads]
        dscores = [(probs[h] * (dprobs[h] - delta[t, h])).astype(BF16) for h in heads]
        lows = [p.astype(BF16) for p in probs]
        dk = sum(dot(dscores[h], q_s[t, h]) for h in heads)
        dv = sum(dot(lows[h], do_s[t, h]) for h in heads)
        accs = [acc[t, h] + dot(t_s[b], dscores[h]) for h in heads]
        for h in heads:
            acc[t, h] = accs[h]
        grads[:, :width] = grads[:, :width] + dk * scale
        grads[:, width:] = grads[:, width:] + dv

    def step(b, carry):
        grads[...] = jnp.zeros_like(grads)

        def tile(t, carry):
            base, row, needed, whole = place(sc, b, t)

            @pl.when(needed & whole)
            def _():
                block(b, t, base, row, False)

            @pl.when(needed & jnp.logical_not(whole))
            def _():
                block(b, t, base, row, True)

            return carry

        lax.fori_loop(0, TILES, tile, 0)
        dkv[b] = grads[...].astype(BF16)
        return carry

    lax.fori_loop(0, 2 * pieces, step, 0)
    if ends:
        for t in range(TILES):
            for h in heads:
                value = (acc[t, h] * scale).astype(BF16)
                for s in range(SLOTS):
                    dq[s][t, h * width : (h + 1) * width, :] = value[
                        :, s * CHUNK : (s + 1) * CHUNK
                    ]


def combine(group, width, *refs):
    parts, out = refs[:-1], refs[-1]
    for h in range(group):
        at = pl.ds(h * width, width)
        whole = sum(part[at, :].astype(F32) for part in parts)
        out[:, at] = jnp.transpose(whole).astype(BF16)


def add(*parts):
    return sum(part.astype(F32) for part in parts).astype(BF16)


def local(query, key, value, dout, document):
    width = key.shape[1]
    group = query.shape[1] // width
    send = functools.partial(lax.ppermute, axis_name=AXES)
    qrow, kcol = lax.axis_index("qrow"), lax.axis_index("kcol")
    z, x_lo, x_hi, y = qrow // 2, qrow % 2, kcol // 4, kcol % 4

    row_home, key_home = pl.pallas_call(
        pack,
        out_shape=[
            jax.ShapeDtypeStruct((CHUNK, 2 * group * width), BF16),
            jax.ShapeDtypeStruct((CHUNK, 2 * width), BF16),
        ],
        name="pack",
    )(query, key, value, dout)
    own = jnp.concatenate(
        [key_home] + [send(key_home, perm=X[n]) for n in range(1, 4)], axis=0
    )
    row_other = send(row_home, perm=NEXT)
    a, b = send(own, perm=NEAR), send(own, perm=REST)
    both = jnp.concatenate([row_home, row_other], axis=0)
    near, last = send(both, perm=Y[1]), send(both, perm=Y[3])
    opposite = jnp.concatenate([send(b[:PAIR], perm=NEAR), send(a[PAIR:], perm=REST)], axis=0)
    far_own, far_other = send(last[:CHUNK], perm=Y[1]), send(near[CHUNK:], perm=Y[3])
    rows = [row_home, row_other, near, last, far_own, far_other]
    keys = [own, a, b, opposite]

    numbers = jnp.arange(DOCS, dtype=jnp.int32)
    starts = jnp.sum((document[None, :] < numbers[:, None]).astype(jnp.int32), axis=1)
    side = 2 - 4 * (z // 2 % 2)
    sources = jnp.stack([z, z + side, z - side, z + 4]) & 7
    sc = jnp.concatenate([jnp.stack([z, x_lo, x_hi, y]), starts, sources]).astype(jnp.int32)

    smem = pl.BlockSpec(memory_space=pltpu.SMEM)
    vmem = pl.BlockSpec(memory_space=pltpu.VMEM)
    params = pltpu.CompilerParams(vmem_limit_bytes=56 * 1024 * 1024)

    def cost(dots, pieces):
        work = TILES * ROWS * group * pieces * 2 * PAIR * width * 2
        return pl.CostEstimate(flops=dots * work // 2, bytes_accessed=1 << 23, transcendentals=0)

    def scratch(pieces):
        return [
            pltpu.VMEM((TILES, group, ROWS, width), BF16),
            pltpu.VMEM((TILES, group, ROWS, width), BF16),
            pltpu.VMEM((2 * pieces, PAIR, width), BF16),
            pltpu.VMEM((2 * pieces, PAIR, width), BF16),
            pltpu.VMEM((2 * pieces, width, PAIR), BF16),
        ]

    line = (TILES, group, 1, ROWS)
    acc_shape = jax.ShapeDtypeStruct((TILES, group, width, ROWS), F32)
    line_shape = jax.ShapeDtypeStruct(line, F32)
    stat_shape = jax.ShapeDtypeStruct((TILES, 3 * group, ROWS), F32)
    piece = jax.ShapeDtypeStruct((TILES, group * width, CHUNK), BF16)

    values, stat = pl.pallas_call(
        functools.partial(forward, group, width, 4),
        out_shape=[acc_shape, stat_shape],
        in_specs=[smem] + [vmem] * 10,
        out_specs=[vmem] * 2,
        scratch_shapes=scratch(4) + [pltpu.VMEM(line, F32)] * 3,
        compiler_params=params,
        cost_estimate=cost(3, 4),
        name="forward",
    )(sc, *rows, *keys)

    unit = LOG2E / math.sqrt(width)
    other = send(stat, perm=NEXT)[::-1]
    top = jnp.maximum(stat[:, :group], other[:, :group])
    mine, theirs = (jnp.exp2((s[:, :group] - top) * unit) for s in (stat, other))
    merged = jnp.concatenate(
        [top]
        + [
            stat[:, n * group : (n + 1) * group] * mine
            + other[:, n * group : (n + 1) * group] * theirs
            for n in (1, 2)
        ],
        axis=1,
    )
    stats = [merged] + [send(merged, perm=Y[s]) for s in range(1, SLOTS)]

    def back(pieces, begins, ends, sc, keys, *more):
        dkv_shape = jax.ShapeDtypeStruct((2 * pieces, PAIR, 2 * width), BF16)
        shapes = [dkv_shape] + [piece] * (SLOTS * (begins + ends))
        carried = [acc_shape, line_shape, line_shape]
        more_scratch = scratch(pieces) + [pltpu.VMEM((PAIR, 2 * width), F32)]
        if ends:
            more_scratch = [pltpu.VMEM(s.shape, F32) for s in carried] + more_scratch
        else:
            shapes = shapes + carried
        return pl.pallas_call(
            functools.partial(backward, group, width, pieces, begins, ends),
            out_shape=shapes,
            in_specs=[smem] + [vmem] * (6 + pieces + len(more)),
            out_specs=[vmem] * len(shapes),
            scratch_shapes=more_scratch,
            compiler_params=params,
            cost_estimate=cost(5, pieces),
            name="backward_begin" if begins else "backward_end",
        )(sc, *rows, *keys, *more)

    def shifted(skip):
        return jnp.concatenate([sc[: 4 + DOCS], sc[4 + DOCS + skip :]])

    late = back(2, True, False, shifted(2), keys[2:], *stats, stat, values)
    far, mixed, carried = late[0], late[1 : 1 + SLOTS], late[1 + SLOTS :]
    end = back(2, False, True, sc, keys[:2], *carried)
    close, dq = end[0], end[1:]

    def over_y(parts):
        return add(parts[0], *[send(parts[s], perm=Y[s]) for s in range(1, SLOTS)])

    one, two = send(far[2], perm=NEAR), send(far[3], perm=REST)
    mixed = over_y(mixed)
    mixed = [mixed[0], send(mixed[1], perm=NEXT)]
    ga = send(jnp.concatenate([close[2], add(close[3], two)], axis=0), perm=NEAR)
    gb = send(jnp.concatenate([add(far[0], one), far[1]], axis=0), perm=REST)
    grad = add(close[:2].reshape(2 * PAIR, 2 * width), ga, gb).reshape(4, CHUNK, 2 * width)
    dq = over_y(dq)
    grad = add(grad[0], *[send(grad[n], perm=X[n]) for n in range(1, 4)])
    dq = [dq[0], send(dq[1], perm=NEXT)]

    outs = [
        pl.pallas_call(
            functools.partial(combine, group, width),
            out_shape=jax.ShapeDtypeStruct((CHUNK, group * width), BF16),
            in_specs=[vmem] * TILES,
            out_specs=vmem,
            name=name,
        )(*parts)
        for parts, name in ((mixed, "attended"), (dq, "grad_query"))
    ]
    return *outs, grad[:, :width], grad[:, width:]


def solution(mesh):
    by_row = P(("qrow", "kcol"), "head")
    by_key = P(("kcol", "qrow"), "head")
    return jax.shard_map(
        local,
        mesh=mesh,
        in_specs=(by_row, by_key, by_key, by_row, P()),
        out_specs=(by_row, by_row, by_key, by_key),
        check_vma=False,
    )
```

```python
import functools
import math

import jax
import jax.numpy as jnp
from jax import lax
from jax.experimental import pallas as pl
from jax.experimental.pallas import tpu as pltpu
from jax.sharding import PartitionSpec as P

AXES = ("qrow", "kcol")
DEVICES = 128
CHUNK = 128
SLOTS = 4
TILES = 2
ROWS = SLOTS * CHUNK
PAIR = 2 * CHUNK
PLANE = 16 * CHUNK
DOCS = 8
NEG = -1e30
FLOOR = -1e29
LOG2E = math.log2(math.e)
F32 = jnp.float32
BF16 = jnp.bfloat16


def flip(mask):
    return [(d, d ^ mask) for d in range(DEVICES)]


Y = [flip(s) for s in range(SLOTS)]
X = [flip(m) for m in (0, 8, 4, 12)]
NEXT = flip(16)
NEAR = flip(32)
REST = [(d, (d + (32 if d // 32 % 2 else -32)) % DEVICES) for d in range(DEVICES)]


def dot(a, b):
    return lax.dot_general(a, b, (((1,), (0,)), ((), ())), preferred_element_type=F32)


def dot_t(a, b):
    return lax.dot_general(a, b, (((1,), (1,)), ((), ())), preferred_element_type=F32)


def fill(rows, keys, q_s, do_s, k_s, v_s, t_s, group, width, which):
    own, other, near, last, far_own, far_other = rows
    top, low = pl.ds(0, CHUNK), pl.ds(CHUNK, CHUNK)
    parts = [
        [(own, top), (near, top), (far_own, top), (last, top)],
        [(other, top), (near, low), (far_other, top), (last, low)],
    ]
    for t in range(TILES):
        for s in range(SLOTS):
            ref, at = parts[t][s]
            part = ref[at, :]
            to = pl.ds(s * CHUNK, CHUNK)
            for h in range(group):
                q_s[t, h, to, :] = part[:, h * width : (h + 1) * width]
                do_s[t, h, to, :] = part[:, (group + h) * width : (group + h + 1) * width]
    for n, ref in enumerate(keys):
        for u in range(2):
            part = ref[pl.ds(u * PAIR, PAIR), :]
            k_s[2 * n + u] = part[:, :width]
            v_s[2 * n + u] = part[:, width:]
            t_s[2 * n + u] = jnp.transpose(part[:, which * width : (which + 1) * width])


def start_of(sc, row):
    start = 0
    for n in range(DOCS):
        one = sc[4 + n]
        start = jnp.maximum(start, jnp.where(one <= row, one, 0))
    return start


def place(sc, block, t):
    z, x_lo, x_hi, y = (sc[n] for n in range(4))
    base = (4 * (x_hi ^ (block & 1)) + y) * PLANE + sc[4 + DOCS + block // 2] * PAIR
    row = ((z * 4 + x_lo * 2 + x_hi) ^ (4 * t)) * ROWS
    needed = (base <= row + ROWS - 1) & (base + PAIR - 1 >= start_of(sc, row))
    whole = (base + PAIR - 1 <= row) & (base >= start_of(sc, row + ROWS - 1))
    return base, row, needed, whole


def allowed_of(sc, base, row):
    key_at = base + (lax.broadcasted_iota(jnp.int32, (PAIR, 1), 0) ^ (sc[1] * CHUNK))
    row_at = row + (lax.broadcasted_iota(jnp.int32, (1, ROWS), 1) ^ (sc[3] * CHUNK))
    return (key_at >= start_of(sc, row_at)) & (key_at <= row_at)


def pack(query, key, value, dout, rows, keys):
    width = query.shape[1]
    rows[:, :width] = query[...]
    rows[:, width:] = dout[...]
    width = key.shape[1]
    keys[:, :width] = key[...]
    keys[:, width:] = value[...]


def forward(group, width, pieces, sc, *refs):
    rows, keys, refs = refs[:6], refs[6 : 6 + pieces], refs[6 + pieces :]
    acc, stat, q_s, do_s, k_s, v_s, t_s, high, total, mixed = refs
    unit = LOG2E / math.sqrt(width)
    heads = range(group)
    fill(rows, keys, q_s, do_s, k_s, v_s, t_s, group, width, 1)
    acc[...] = jnp.zeros_like(acc)
    high[...] = jnp.full_like(high, FLOOR)
    total[...] = jnp.zeros_like(total)
    mixed[...] = jnp.zeros_like(mixed)

    def block(b, t, base, row, masked):
        scores = [dot_t(k_s[b], q_s[t, h]) for h in heads]
        dprobs = [dot_t(v_s[b], do_s[t, h]) for h in heads]
        if masked:
            allowed = allowed_of(sc, base, row)
            scores = [jnp.where(allowed, s, NEG) for s in scores]
        olds = [high[t, h] for h in heads]
        news = [jnp.maximum(o, jnp.max(s, axis=0, keepdims=True)) for o, s in zip(olds, scores)]
        shrinks = [jnp.exp2((o - n) * unit) for o, n in zip(olds, news)]
        es = [jnp.exp2(s * unit - n * unit) for s, n in zip(scores, news)]
        totals = [total[t, h] * shrinks[h] + jnp.sum(es[h], axis=0, keepdims=True) for h in heads]
        mixeds = [
            mixed[t, h] * shrinks[h] + jnp.sum(es[h] * dprobs[h], axis=0, keepdims=True)
            for h in heads
        ]
        accs = [acc[t, h] * shrinks[h] + dot(t_s[b], es[h].astype(BF16)) for h in heads]
        for h in heads:
            high[t, h] = news[h]
            total[t, h] = totals[h]
            mixed[t, h] = mixeds[h]
            acc[t, h] = accs[h]

    def step(n, carry):
        b, t = n // 2, n & 1
        base, row, needed, whole = place(sc, b, t)

        @pl.when(needed & whole)
        def _():
            block(b, t, base, row, False)

        @pl.when(needed & jnp.logical_not(whole))
        def _():
            block(b, t, base, row, True)

        return carry

    lax.fori_loop(0, 4 * pieces, step, 0)
    for t in range(TILES):
        for h in heads:
            stat[t, h : h + 1, :] = high[t, h]
            stat[t, group + h : group + h + 1, :] = total[t, h]
            stat[t, 2 * group + h : 2 * group + h + 1, :] = mixed[t, h]


def backward(group, width, pieces, begins, ends, sc, *refs):
    rows, keys, refs = refs[:6], refs[6 : 6 + pieces], refs[6 + pieces :]
    scale = 1.0 / math.sqrt(width)
    unit = LOG2E * scale
    heads = range(group)
    if begins:
        stats, own, values, refs = refs[:SLOTS], refs[SLOTS], refs[SLOTS + 1], refs[SLOTS + 2 :]
    else:
        acc_in, lse_in, delta_in, refs = *refs[:3], refs[3:]
    dkv, refs = refs[0], refs[1:]
    if begins:
        mixed, refs = refs[:SLOTS], refs[SLOTS:]
    if ends:
        dq, refs = refs[:SLOTS], refs[SLOTS:]
    acc, lse, delta, q_s, do_s, k_s, v_s, t_s, grads = refs
    fill(rows, keys, q_s, do_s, k_s, v_s, t_s, group, width, 0)
    if begins:
        acc[...] = jnp.zeros_like(acc)
        for t in range(TILES):
            for u in range(SLOTS):
                at = pl.ds(u * CHUNK, CHUNK)
                parts = [stats[s][t, :, pl.ds((u ^ s) * CHUNK, CHUNK)] for s in range(SLOTS)]
                top = functools.reduce(jnp.maximum, [p[:group] for p in parts])
                weights = [jnp.exp2((p[:group] - top) * unit) for p in parts]
                total = sum(w * p[group : 2 * group] for w, p in zip(weights, parts))
                product = sum(w * p[2 * group :] for w, p in zip(weights, parts))
                low, small = top * unit + jnp.log2(total), product / total
                part = jnp.exp2(own[t, :group, at] * unit - low)
                for h in heads:
                    lse[t, h, :, at] = low[h : h + 1]
                    delta[t, h, :, at] = small[h : h + 1]
                    mixed[u][t, h * width : (h + 1) * width, :] = (
                        values[t, h, :, at] * part[h : h + 1]
                    ).astype(BF16)
    else:
        acc[...] = acc_in[...]
        lse[...] = lse_in[...]
        delta[...] = delta_in[...]

    def block(b, t, base, row, masked):
        scores = [dot_t(k_s[b], q_s[t, h]) for h in heads]
        dprobs = [dot_t(v_s[b], do_s[t, h]) for h in heads]
        if masked:
            allowed = allowed_of(sc, base, row)
            scores = [jnp.where(allowed, s, NEG) for s in scores]
        probs = [jnp.exp2(scores[h] * unit - lse[t, h]) for h in heads]
        dscores = [(probs[h] * (dprobs[h] - delta[t, h])).astype(BF16) for h in heads]
        lows = [p.astype(BF16) for p in probs]
        dk = sum(dot(dscores[h], q_s[t, h]) for h in heads)
        dv = sum(dot(lows[h], do_s[t, h]) for h in heads)
        accs = [acc[t, h] + dot(t_s[b], dscores[h]) for h in heads]
        for h in heads:
            acc[t, h] = accs[h]
        grads[:, :width] = grads[:, :width] + dk * scale
        grads[:, width:] = grads[:, width:] + dv

    def step(b, carry):
        grads[...] = jnp.zeros_like(grads)

        def tile(t, carry):
            base, row, needed, whole = place(sc, b, t)

            @pl.when(needed & whole)
            def _():
                block(b, t, base, row, False)

            @pl.when(needed & jnp.logical_not(whole))
            def _():
                block(b, t, base, row, True)

            return carry

        lax.fori_loop(0, TILES, tile, 0)
        dkv[b] = grads[...].astype(BF16)
        return carry

    lax.fori_loop(0, 2 * pieces, step, 0)
    if ends:
        for t in range(TILES):
            for h in heads:
                value = (acc[t, h] * scale).astype(BF16)
                for s in range(SLOTS):
                    dq[s][t, h * width : (h + 1) * width, :] = value[
                        :, s * CHUNK : (s + 1) * CHUNK
                    ]


def combine(group, width, *refs):
    parts, out = refs[:-1], refs[-1]
    for h in range(group):
        at = pl.ds(h * width, width)
        whole = sum(part[at, :].astype(F32) for part in parts)
        out[:, at] = jnp.transpose(whole).astype(BF16)


SMEM = pl.BlockSpec(memory_space=pltpu.SMEM)
VMEM = pl.BlockSpec(memory_space=pltpu.VMEM)
PARAMS = pltpu.CompilerParams(vmem_limit_bytes=28 * 1024 * 1024)


def cost(group, width, dots, pieces):
    work = TILES * ROWS * group * pieces * 2 * PAIR * width * 2
    return pl.CostEstimate(flops=2 * dots * work, bytes_accessed=1 << 23, transcendentals=0)


def scratch(group, width, pieces):
    return [
        pltpu.VMEM((TILES, group, ROWS, width), BF16),
        pltpu.VMEM((TILES, group, ROWS, width), BF16),
        pltpu.VMEM((2 * pieces, PAIR, width), BF16),
        pltpu.VMEM((2 * pieces, PAIR, width), BF16),
        pltpu.VMEM((2 * pieces, width, PAIR), BF16),
    ]


def state_shapes(group, width):
    acc = jax.ShapeDtypeStruct((TILES, group, width, ROWS), F32)
    line = jax.ShapeDtypeStruct((TILES, group, 1, ROWS), F32)
    return [acc, line, line]


def run_forward(group, width, sc, rows, keys):
    pieces = len(keys)
    acc, line, _ = state_shapes(group, width)
    return pl.pallas_call(
        functools.partial(forward, group, width, pieces),
        out_shape=[acc, jax.ShapeDtypeStruct((TILES, 3 * group, ROWS), F32)],
        in_specs=[SMEM] + [VMEM] * (6 + pieces),
        out_specs=[VMEM] * 2,
        scratch_shapes=scratch(group, width, pieces) + [pltpu.VMEM(line.shape, F32)] * 3,
        compiler_params=PARAMS,
        cost_estimate=cost(group, width, 3, pieces),
        name="forward",
    )(sc, *rows, *keys)


def run_backward(group, width, begins, sc, rows, keys, *more):
    pieces = len(keys)
    carried = state_shapes(group, width)
    piece = jax.ShapeDtypeStruct((TILES, group * width, CHUNK), BF16)
    shapes = [jax.ShapeDtypeStruct((2 * pieces, PAIR, 2 * width), BF16)] + [piece] * SLOTS
    spaces = scratch(group, width, pieces) + [pltpu.VMEM((PAIR, 2 * width), F32)]
    if begins:
        shapes = shapes + carried
    else:
        spaces = [pltpu.VMEM(s.shape, F32) for s in carried] + spaces
    return pl.pallas_call(
        functools.partial(backward, group, width, pieces, begins, not begins),
        out_shape=shapes,
        in_specs=[SMEM] + [VMEM] * (6 + pieces + len(more)),
        out_specs=[VMEM] * len(shapes),
        scratch_shapes=spaces,
        compiler_params=PARAMS,
        cost_estimate=cost(group, width, 5, pieces),
        name="backward_begin" if begins else "backward_end",
    )(sc, *rows, *keys, *more)


def add(*parts):
    return sum(part.astype(F32) for part in parts).astype(BF16)


def local(query, key, value, dout, document):
    width = key.shape[1]
    group = query.shape[1] // width
    send = functools.partial(lax.ppermute, axis_name=AXES)
    qrow, kcol = lax.axis_index("qrow"), lax.axis_index("kcol")
    z, x_lo, x_hi, y = qrow // 2, qrow % 2, kcol // 4, kcol % 4

    row_home, key_home = pl.pallas_call(
        pack,
        out_shape=[
            jax.ShapeDtypeStruct((CHUNK, 2 * group * width), BF16),
            jax.ShapeDtypeStruct((CHUNK, 2 * width), BF16),
        ],
        name="pack",
    )(query, key, value, dout)
    own = jnp.concatenate(
        [key_home] + [send(key_home, perm=X[n]) for n in range(1, 4)], axis=0
    )
    row_other = send(row_home, perm=NEXT)
    a, b = send(own, perm=NEAR), send(own, perm=REST)
    both = jnp.concatenate([row_home, row_other], axis=0)
    near, last = send(both, perm=Y[1]), send(both, perm=Y[3])
    opposite = jnp.concatenate([send(b[:PAIR], perm=NEAR), send(a[PAIR:], perm=REST)], axis=0)
    far_own, far_other = send(last[:CHUNK], perm=Y[1]), send(near[CHUNK:], perm=Y[3])
    rows = [row_home, row_other, near, last, far_own, far_other]
    keys = [own, a, b, opposite]

    numbers = jnp.arange(DOCS, dtype=jnp.int32)
    starts = jnp.sum((document[None, :] < numbers[:, None]).astype(jnp.int32), axis=1)
    side = 2 - 4 * (z // 2 % 2)
    sources = jnp.stack([z, z + side, z - side, z + 4]) & 7
    sc = jnp.concatenate([jnp.stack([z, x_lo, x_hi, y]), starts, sources]).astype(jnp.int32)

    values, stat = run_forward(group, width, sc, rows, keys)
    unit = LOG2E / math.sqrt(width)
    other = send(stat, perm=NEXT)[::-1]
    top = jnp.maximum(stat[:, :group], other[:, :group])
    mine, theirs = (jnp.exp2((s[:, :group] - top) * unit) for s in (stat, other))
    merged = jnp.concatenate(
        [top]
        + [
            stat[:, n * group : (n + 1) * group] * mine
            + other[:, n * group : (n + 1) * group] * theirs
            for n in (1, 2)
        ],
        axis=1,
    )
    stats = [merged] + [send(merged, perm=Y[s]) for s in range(1, SLOTS)]

    def shifted(skip):
        return jnp.concatenate([sc[: 4 + DOCS], sc[4 + DOCS + skip :]])

    late = run_backward(group, width, True, shifted(2), rows, keys[2:], *stats, stat, values)
    far, mixed, carried = late[0], late[1 : 1 + SLOTS], late[1 + SLOTS :]
    end = run_backward(group, width, False, sc, rows, keys[:2], *carried)
    close, dq = end[0], end[1:]

    def over_y(parts):
        return add(parts[0], *[send(parts[s], perm=Y[s]) for s in range(1, SLOTS)])

    one, two = send(far[2], perm=NEAR), send(far[3], perm=REST)
    mixed = over_y(mixed)
    mixed = [mixed[0], send(mixed[1], perm=NEXT)]
    ga = send(jnp.concatenate([close[2], add(close[3], two)], axis=0), perm=NEAR)
    gb = send(jnp.concatenate([add(far[0], one), far[1]], axis=0), perm=REST)
    grad = add(close[:2].reshape(2 * PAIR, 2 * width), ga, gb).reshape(4, CHUNK, 2 * width)
    dq = over_y(dq)
    grad = add(grad[0], *[send(grad[n], perm=X[n]) for n in range(1, 4)])
    dq = [dq[0], send(dq[1], perm=NEXT)]

    outs = [
        pl.pallas_call(
            functools.partial(combine, group, width),
            out_shape=jax.ShapeDtypeStruct((CHUNK, group * width), BF16),
            in_specs=[VMEM] * TILES,
            out_specs=VMEM,
            name=name,
        )(*parts)
        for parts, name in ((mixed, "attended"), (dq, "grad_query"))
    ]
    return *outs, grad[:, :width], grad[:, width:]


def solution(mesh):
    by_row = P(("qrow", "kcol"), "head")
    by_key = P(("kcol", "qrow"), "head")
    return jax.shard_map(
        local,
        mesh=mesh,
        in_specs=(by_row, by_key, by_key, by_row, P()),
        out_specs=(by_row, by_row, by_key, by_key),
        check_vma=False,
    )
```

```python
import functools
import math

import jax
import jax.numpy as jnp
from jax import lax
from jax.experimental import pallas as pl
from jax.experimental.pallas import tpu as pltpu
from jax.sharding import PartitionSpec as P

AXES = ("qrow", "kcol")
DEVICES = 128
CHUNK = 128
SLOTS = 4
TILES = 2
ROWS = SLOTS * CHUNK
PAIR = 2 * CHUNK
PLANE = 16 * CHUNK
DOCS = 8
NEG = -1e30
FLOOR = -1e29
LOG2E = math.log2(math.e)
F32 = jnp.float32
BF16 = jnp.bfloat16


def flip(mask):
    return [(d, d ^ mask) for d in range(DEVICES)]


Y = [flip(s) for s in range(SLOTS)]
X = [flip(m) for m in (0, 8, 4, 12)]
NEXT = flip(16)
NEAR = flip(32)
REST = [(d, (d + (32 if d // 32 % 2 else -32)) % DEVICES) for d in range(DEVICES)]


def dot(a, b):
    return lax.dot_general(a, b, (((1,), (0,)), ((), ())), preferred_element_type=F32)


def dot_t(a, b):
    return lax.dot_general(a, b, (((1,), (1,)), ((), ())), preferred_element_type=F32)


def fill(rows, keys, q_s, do_s, k_s, v_s, t_s, group, width, which):
    own, other, near, last, far_own, far_other = rows
    top, low = pl.ds(0, CHUNK), pl.ds(CHUNK, CHUNK)
    parts = [
        [(own, top), (near, top), (far_own, top), (last, top)],
        [(other, top), (near, low), (far_other, top), (last, low)],
    ]
    for t in range(TILES):
        for s in range(SLOTS):
            ref, at = parts[t][s]
            part = ref[at, :]
            to = pl.ds(s * CHUNK, CHUNK)
            for h in range(group):
                q_s[t, h, to, :] = part[:, h * width : (h + 1) * width]
                do_s[t, h, to, :] = part[:, (group + h) * width : (group + h + 1) * width]
    for n, ref in enumerate(keys):
        for u in range(2):
            part = ref[pl.ds(u * PAIR, PAIR), :]
            k_s[2 * n + u] = part[:, :width]
            v_s[2 * n + u] = part[:, width:]
            t_s[2 * n + u] = jnp.transpose(part[:, which * width : (which + 1) * width])


def start_of(sc, row):
    start = 0
    for n in range(DOCS):
        one = sc[4 + n]
        start = jnp.maximum(start, jnp.where(one <= row, one, 0))
    return start


def place(sc, block, t):
    z, x_lo, x_hi, y = (sc[n] for n in range(4))
    base = (4 * (x_hi ^ (block & 1)) + y) * PLANE + sc[4 + DOCS + block // 2] * PAIR
    row = ((z * 4 + x_lo * 2 + x_hi) ^ (4 * t)) * ROWS
    needed = (base <= row + ROWS - 1) & (base + PAIR - 1 >= start_of(sc, row))
    whole = (base + PAIR - 1 <= row) & (base >= start_of(sc, row + ROWS - 1))
    return base, row, needed, whole


def allowed_of(sc, base, row):
    key_at = base + (lax.broadcasted_iota(jnp.int32, (PAIR, 1), 0) ^ (sc[1] * CHUNK))
    row_at = row + (lax.broadcasted_iota(jnp.int32, (1, ROWS), 1) ^ (sc[3] * CHUNK))
    return (key_at >= start_of(sc, row_at)) & (key_at <= row_at)


def pack(query, key, value, dout, rows, keys):
    width = query.shape[1]
    rows[:, :width] = query[...]
    rows[:, width:] = dout[...]
    width = key.shape[1]
    keys[:, :width] = key[...]
    keys[:, width:] = value[...]


def forward(group, width, pieces, sc, *refs):
    rows, keys, refs = refs[:6], refs[6 : 6 + pieces], refs[6 + pieces :]
    values, stat, acc, q_s, do_s, k_s, v_s, t_s, high, total, mixed = refs
    unit = LOG2E / math.sqrt(width)
    heads = range(group)
    fill(rows, keys, q_s, do_s, k_s, v_s, t_s, group, width, 1)
    acc[...] = jnp.zeros_like(acc)
    high[...] = jnp.full_like(high, FLOOR)
    total[...] = jnp.zeros_like(total)
    mixed[...] = jnp.zeros_like(mixed)

    def block(b, t, base, row, masked):
        scores = [dot_t(k_s[b], q_s[t, h]) for h in heads]
        dprobs = [dot_t(v_s[b], do_s[t, h]) for h in heads]
        if masked:
            allowed = allowed_of(sc, base, row)
            scores = [jnp.where(allowed, s, NEG) for s in scores]
        olds = [high[t, h] for h in heads]
        news = [jnp.maximum(o, jnp.max(s, axis=0, keepdims=True)) for o, s in zip(olds, scores)]
        shrinks = [jnp.exp2((o - n) * unit) for o, n in zip(olds, news)]
        es = [jnp.exp2(s * unit - n * unit) for s, n in zip(scores, news)]
        totals = [total[t, h] * shrinks[h] + jnp.sum(es[h], axis=0, keepdims=True) for h in heads]
        mixeds = [
            mixed[t, h] * shrinks[h] + jnp.sum(es[h] * dprobs[h], axis=0, keepdims=True)
            for h in heads
        ]
        accs = [acc[t, h] * shrinks[h] + dot(t_s[b], es[h].astype(BF16)) for h in heads]
        for h in heads:
            high[t, h] = news[h]
            total[t, h] = totals[h]
            mixed[t, h] = mixeds[h]
            acc[t, h] = accs[h]

    def step(n, carry):
        b, t = n // 2, n & 1
        base, row, needed, whole = place(sc, b, t)

        @pl.when(needed & whole)
        def _():
            block(b, t, base, row, False)

        @pl.when(needed & jnp.logical_not(whole))
        def _():
            block(b, t, base, row, True)

        return carry

    lax.fori_loop(0, 4 * pieces, step, 0)
    for t in range(TILES):
        for h in heads:
            values[t, h] = (acc[t, h] * (1.0 / jnp.maximum(total[t, h], 1e-30))).astype(BF16)
            stat[t, h : h + 1, :] = high[t, h]
            stat[t, group + h : group + h + 1, :] = total[t, h]
            stat[t, 2 * group + h : 2 * group + h + 1, :] = mixed[t, h]


def backward(group, width, pieces, begins, ends, sc, *refs):
    rows, keys, refs = refs[:6], refs[6 : 6 + pieces], refs[6 + pieces :]
    scale = 1.0 / math.sqrt(width)
    unit = LOG2E * scale
    heads = range(group)
    if begins:
        stats, own, values, refs = refs[:SLOTS], refs[SLOTS], refs[SLOTS + 1], refs[SLOTS + 2 :]
    else:
        acc_in, lse_in, delta_in, refs = *refs[:3], refs[3:]
    dkv, refs = refs[0], refs[1:]
    if begins:
        mixed, refs = refs[:SLOTS], refs[SLOTS:]
    if ends:
        dq, refs = refs[:SLOTS], refs[SLOTS:]
    acc, lse, delta, q_s, do_s, k_s, v_s, t_s, grads = refs
    fill(rows, keys, q_s, do_s, k_s, v_s, t_s, group, width, 0)
    if begins:
        acc[...] = jnp.zeros_like(acc)
        for t in range(TILES):
            for u in range(SLOTS):
                at = pl.ds(u * CHUNK, CHUNK)
                parts = [stats[s][t, :, pl.ds((u ^ s) * CHUNK, CHUNK)] for s in range(SLOTS)]
                top = functools.reduce(jnp.maximum, [p[:group] for p in parts])
                weights = [jnp.exp2((p[:group] - top) * unit) for p in parts]
                total = sum(w * p[group : 2 * group] for w, p in zip(weights, parts))
                product = sum(w * p[2 * group :] for w, p in zip(weights, parts))
                low, small = top * unit + jnp.log2(total), product / total
                part = own[t, group : 2 * group, at] * jnp.exp2(own[t, :group, at] * unit - low)
                for h in heads:
                    lse[t, h, :, at] = low[h : h + 1]
                    delta[t, h, :, at] = small[h : h + 1]
                    mixed[u][t, h * width : (h + 1) * width, :] = (
                        values[t, h, :, at].astype(F32) * part[h : h + 1]
                    ).astype(BF16)
    else:
        acc[...] = acc_in[...]
        lse[...] = lse_in[...]
        delta[...] = delta_in[...]

    def block(b, t, base, row, masked):
        scores = [dot_t(k_s[b], q_s[t, h]) for h in heads]
        dprobs = [dot_t(v_s[b], do_s[t, h]) for h in heads]
        if masked:
            allowed = allowed_of(sc, base, row)
            scores = [jnp.where(allowed, s, NEG) for s in scores]
        probs = [jnp.exp2(scores[h] * unit - lse[t, h]) for h in heads]
        dscores = [(probs[h] * (dprobs[h] - delta[t, h])).astype(BF16) for h in heads]
        lows = [p.astype(BF16) for p in probs]
        dk = sum(dot(dscores[h], q_s[t, h]) for h in heads)
        dv = sum(dot(lows[h], do_s[t, h]) for h in heads)
        accs = [acc[t, h] + dot(t_s[b], dscores[h]) for h in heads]
        for h in heads:
            acc[t, h] = accs[h]
        grads[:, :width] = grads[:, :width] + dk * scale
        grads[:, width:] = grads[:, width:] + dv

    def step(b, carry):
        grads[...] = jnp.zeros_like(grads)

        def tile(t, carry):
            base, row, needed, whole = place(sc, b, t)

            @pl.when(needed & whole)
            def _():
                block(b, t, base, row, False)

            @pl.when(needed & jnp.logical_not(whole))
            def _():
                block(b, t, base, row, True)

            return carry

        lax.fori_loop(0, TILES, tile, 0)
        dkv[b] = grads[...].astype(BF16)
        return carry

    lax.fori_loop(0, 2 * pieces, step, 0)
    if ends:
        for t in range(TILES):
            for h in heads:
                value = (acc[t, h] * scale).astype(BF16)
                for s in range(SLOTS):
                    dq[s][t, h * width : (h + 1) * width, :] = value[
                        :, s * CHUNK : (s + 1) * CHUNK
                    ]


def combine(group, width, *refs):
    parts, out = refs[:-1], refs[-1]
    for h in range(group):
        at = pl.ds(h * width, width)
        whole = sum(part[at, :].astype(F32) for part in parts)
        out[:, at] = jnp.transpose(whole).astype(BF16)


SMEM = pl.BlockSpec(memory_space=pltpu.SMEM)
VMEM = pl.BlockSpec(memory_space=pltpu.VMEM)
PARAMS = pltpu.CompilerParams(vmem_limit_bytes=28 * 1024 * 1024)


def cost(group, width, dots, pieces):
    work = TILES * ROWS * group * pieces * 2 * PAIR * width * 2
    return pl.CostEstimate(flops=2 * dots * work, bytes_accessed=1 << 23, transcendentals=0)


def scratch(group, width, pieces):
    return [
        pltpu.VMEM((TILES, group, ROWS, width), BF16),
        pltpu.VMEM((TILES, group, ROWS, width), BF16),
        pltpu.VMEM((2 * pieces, PAIR, width), BF16),
        pltpu.VMEM((2 * pieces, PAIR, width), BF16),
        pltpu.VMEM((2 * pieces, width, PAIR), BF16),
    ]


def state_shapes(group, width):
    acc = jax.ShapeDtypeStruct((TILES, group, width, ROWS), F32)
    line = jax.ShapeDtypeStruct((TILES, group, 1, ROWS), F32)
    return [acc, line, line]


def run_forward(group, width, sc, rows, keys):
    pieces = len(keys)
    acc, line, _ = state_shapes(group, width)
    return pl.pallas_call(
        functools.partial(forward, group, width, pieces),
        out_shape=[
            jax.ShapeDtypeStruct(acc.shape, BF16),
            jax.ShapeDtypeStruct((TILES, 3 * group, ROWS), F32),
        ],
        in_specs=[SMEM] + [VMEM] * (6 + pieces),
        out_specs=[VMEM] * 2,
        scratch_shapes=[pltpu.VMEM(acc.shape, F32)]
        + scratch(group, width, pieces)
        + [pltpu.VMEM(line.shape, F32)] * 3,
        compiler_params=PARAMS,
        cost_estimate=cost(group, width, 3, pieces),
        name="forward",
    )(sc, *rows, *keys)


def run_backward(group, width, begins, ends, sc, rows, keys, *more):
    pieces = len(keys)
    carried = state_shapes(group, width)
    piece = jax.ShapeDtypeStruct((TILES, group * width, CHUNK), BF16)
    shapes = [jax.ShapeDtypeStruct((2 * pieces, PAIR, 2 * width), BF16)]
    shapes = shapes + [piece] * (SLOTS * (begins + ends))
    spaces = scratch(group, width, pieces) + [pltpu.VMEM((PAIR, 2 * width), F32)]
    if not ends:
        shapes = shapes + carried
    else:
        spaces = [pltpu.VMEM(s.shape, F32) for s in carried] + spaces
    return pl.pallas_call(
        functools.partial(backward, group, width, pieces, begins, ends),
        out_shape=shapes,
        in_specs=[SMEM] + [VMEM] * (6 + pieces + len(more)),
        out_specs=[VMEM] * len(shapes),
        scratch_shapes=spaces,
        compiler_params=PARAMS,
        cost_estimate=cost(group, width, 5, pieces),
        name="backward_begin" if begins else "backward_end" if ends else "backward_middle",
    )(sc, *rows, *keys, *more)


def add(*parts):
    return sum(part.astype(F32) for part in parts).astype(BF16)


def local(query, key, value, dout, document):
    width = key.shape[1]
    group = query.shape[1] // width
    send = functools.partial(lax.ppermute, axis_name=AXES)
    qrow, kcol = lax.axis_index("qrow"), lax.axis_index("kcol")
    z, x_lo, x_hi, y = qrow // 2, qrow % 2, kcol // 4, kcol % 4

    row_home, key_home = pl.pallas_call(
        pack,
        out_shape=[
            jax.ShapeDtypeStruct((CHUNK, 2 * group * width), BF16),
            jax.ShapeDtypeStruct((CHUNK, 2 * width), BF16),
        ],
        name="pack",
    )(query, key, value, dout)
    own = jnp.concatenate(
        [key_home] + [send(key_home, perm=X[n]) for n in range(1, 4)], axis=0
    )
    row_other = send(row_home, perm=NEXT)
    a, b = send(own, perm=NEAR), send(own, perm=REST)
    both = jnp.concatenate([row_home, row_other], axis=0)
    near, last = send(both, perm=Y[1]), send(both, perm=Y[3])
    opposite = jnp.concatenate([send(b[:PAIR], perm=NEAR), send(a[PAIR:], perm=REST)], axis=0)
    far_own, far_other = send(last[:CHUNK], perm=Y[1]), send(near[CHUNK:], perm=Y[3])
    rows = [row_home, row_other, near, last, far_own, far_other]
    keys = [own, a, b, opposite]

    numbers = jnp.arange(DOCS, dtype=jnp.int32)
    starts = jnp.sum((document[None, :] < numbers[:, None]).astype(jnp.int32), axis=1)
    side = 2 - 4 * (z // 2 % 2)
    sources = jnp.stack([z, z + side, z - side, z + 4]) & 7
    sc = jnp.concatenate([jnp.stack([z, x_lo, x_hi, y]), starts, sources]).astype(jnp.int32)

    values, stat = run_forward(group, width, sc, rows, keys)
    unit = LOG2E / math.sqrt(width)
    other = send(stat, perm=NEXT)[::-1]
    top = jnp.maximum(stat[:, :group], other[:, :group])
    mine, theirs = (jnp.exp2((s[:, :group] - top) * unit) for s in (stat, other))
    merged = jnp.concatenate(
        [top]
        + [
            stat[:, n * group : (n + 1) * group] * mine
            + other[:, n * group : (n + 1) * group] * theirs
            for n in (1, 2)
        ],
        axis=1,
    )
    stats = [merged] + [send(merged, perm=Y[s]) for s in range(1, SLOTS)]

    def over_y(parts):
        return add(parts[0], *[send(parts[s], perm=Y[s]) for s in range(1, SLOTS)])

    def part_of(begin, end):
        return jnp.concatenate([sc[: 4 + DOCS], sc[4 + DOCS + begin : 4 + DOCS + end]])

    back = functools.partial(run_backward, group, width)
    out = back(True, False, part_of(3, 4), rows, keys[3:], *stats, stat, values)
    far, mixed, carried = out[0], out[1 : 1 + SLOTS], out[1 + SLOTS :]
    one, two = send(far[0], perm=NEAR), send(far[1], perm=REST)
    mixed = over_y(mixed)
    near_by, *carried = back(False, False, part_of(1, 3), rows, keys[1:3], *carried)
    ga = jnp.concatenate([near_by[0], add(near_by[1], two)], axis=0)
    gb = jnp.concatenate([add(near_by[2], one), near_by[3]], axis=0)
    ga, gb, mixed, carried = lax.optimization_barrier((ga, gb, mixed, carried))
    ga, gb = send(ga, perm=NEAR), send(gb, perm=REST)
    mixed = [mixed[0], send(mixed[1], perm=NEXT)]
    close, *dq = back(False, True, part_of(0, 1), rows, keys[:1], *carried)
    grad = add(close.reshape(2 * PAIR, 2 * width), ga, gb).reshape(4, CHUNK, 2 * width)
    dq = over_y(dq)
    grad = add(grad[0], *[send(grad[n], perm=X[n]) for n in range(1, 4)])
    dq = [dq[0], send(dq[1], perm=NEXT)]

    outs = [
        pl.pallas_call(
            functools.partial(combine, group, width),
            out_shape=jax.ShapeDtypeStruct((CHUNK, group * width), BF16),
            in_specs=[VMEM] * TILES,
            out_specs=VMEM,
            name=name,
        )(*parts)
        for parts, name in ((mixed, "attended"), (dq, "grad_query"))
    ]
    return *outs, grad[:, :width], grad[:, width:]


def solution(mesh):
    by_row = P(("qrow", "kcol"), "head")
    by_key = P(("kcol", "qrow"), "head")
    return jax.shard_map(
        local,
        mesh=mesh,
        in_specs=(by_row, by_key, by_key, by_row, P()),
        out_specs=(by_row, by_row, by_key, by_key),
        check_vma=False,
    )
```

```python
import functools
import math

import jax
import jax.numpy as jnp
from jax import lax
from jax.experimental import pallas as pl
from jax.experimental.pallas import tpu as pltpu
from jax.sharding import PartitionSpec as P

AXES = ("qrow", "kcol")
DEVICES = 128
CHUNK = 128
SLOTS = 4
TILES = 2
ROWS = SLOTS * CHUNK
PAIR = 2 * CHUNK
PLANE = 16 * CHUNK
DOCS = 8
NEG = -1e30
FLOOR = -1e29
LOG2E = math.log2(math.e)
F32 = jnp.float32
BF16 = jnp.bfloat16


def flip(mask):
    return [(d, d ^ mask) for d in range(DEVICES)]


Y = [flip(s) for s in range(SLOTS)]
X = [flip(m) for m in (0, 8, 4, 12)]
NEXT = flip(16)
NEAR = flip(32)
REST = [(d, (d + (32 if d // 32 % 2 else -32)) % DEVICES) for d in range(DEVICES)]


def dot(a, b):
    return lax.dot_general(a, b, (((1,), (0,)), ((), ())), preferred_element_type=F32)


def dot_t(a, b):
    return lax.dot_general(a, b, (((1,), (1,)), ((), ())), preferred_element_type=F32)


def fill(rows, keys, q_s, do_s, k_s, v_s, t_s, group, width, span, which):
    own, other, near, last, far_own, far_other = rows
    top, low = pl.ds(0, CHUNK), pl.ds(CHUNK, CHUNK)
    parts = [
        [(own, top), (near, top), (far_own, top), (last, top)],
        [(other, top), (near, low), (far_other, top), (last, low)],
    ]
    for t in range(TILES):
        for s in range(SLOTS):
            ref, at = parts[t][s]
            part = ref[at, :]
            to = pl.ds(s * CHUNK, CHUNK)
            for h in range(group):
                q_s[t, h, to, :] = part[:, h * width : (h + 1) * width]
                do_s[t, h, to, :] = part[:, (group + h) * width : (group + h + 1) * width]
    for n, piece in enumerate(range(*span)):
        for m, ref in enumerate(keys):
            part = ref[pl.ds(piece * CHUNK, CHUNK), :]
            block, at = 2 * n + m // 2, pl.ds(m % 2 * CHUNK, CHUNK)
            k_s[block, at, :] = part[:, :width]
            v_s[block, at, :] = part[:, width:]
            t_s[block, :, at] = jnp.transpose(part[:, which * width : (which + 1) * width])


def start_of(sc, row):
    start = 0
    for n in range(DOCS):
        one = sc[4 + n]
        start = jnp.maximum(start, jnp.where(one <= row, one, 0))
    return start


def place(sc, first, block, t):
    z, x_lo, x_hi, y = (sc[n] for n in range(4))
    base = (4 * (x_hi ^ (block & 1)) + y) * PLANE + sc[4 + DOCS + first + block // 2] * PAIR
    row = ((z * 4 + x_lo * 2 + x_hi) ^ (4 * t)) * ROWS
    needed = (base <= row + ROWS - 1) & (base + PAIR - 1 >= start_of(sc, row))
    whole = (base + PAIR - 1 <= row) & (base >= start_of(sc, row + ROWS - 1))
    return base, row, needed, whole


def allowed_of(sc, base, row):
    key_at = base + (lax.broadcasted_iota(jnp.int32, (PAIR, 1), 0) ^ (sc[1] * CHUNK))
    row_at = row + (lax.broadcasted_iota(jnp.int32, (1, ROWS), 1) ^ (sc[3] * CHUNK))
    return (key_at >= start_of(sc, row_at)) & (key_at <= row_at)


def pack(query, key, value, dout, rows, keys):
    width = query.shape[1]
    rows[:, :width] = query[...]
    rows[:, width:] = dout[...]
    width = key.shape[1]
    keys[:, :width] = key[...]
    keys[:, width:] = value[...]


def forward(group, width, span, sc, *refs):
    pieces = span[1] - span[0]
    rows, keys, refs = refs[:6], refs[6:10], refs[10:]
    values, stat, acc, q_s, do_s, k_s, v_s, t_s, high, total, mixed = refs
    unit = LOG2E / math.sqrt(width)
    heads = range(group)
    fill(rows, keys, q_s, do_s, k_s, v_s, t_s, group, width, span, 1)
    acc[...] = jnp.zeros_like(acc)
    high[...] = jnp.full_like(high, FLOOR)
    total[...] = jnp.zeros_like(total)
    mixed[...] = jnp.zeros_like(mixed)

    def block(b, t, base, row, masked):
        scores = [dot_t(k_s[b], q_s[t, h]) for h in heads]
        dprobs = [dot_t(v_s[b], do_s[t, h]) for h in heads]
        if masked:
            allowed = allowed_of(sc, base, row)
            scores = [jnp.where(allowed, s, NEG) for s in scores]
        olds = [high[t, h] for h in heads]
        news = [jnp.maximum(o, jnp.max(s, axis=0, keepdims=True)) for o, s in zip(olds, scores)]
        shrinks = [jnp.exp2((o - n) * unit) for o, n in zip(olds, news)]
        es = [jnp.exp2(s * unit - n * unit) for s, n in zip(scores, news)]
        totals = [total[t, h] * shrinks[h] + jnp.sum(es[h], axis=0, keepdims=True) for h in heads]
        mixeds = [
            mixed[t, h] * shrinks[h] + jnp.sum(es[h] * dprobs[h], axis=0, keepdims=True)
            for h in heads
        ]
        accs = [acc[t, h] * shrinks[h] + dot(t_s[b], es[h].astype(BF16)) for h in heads]
        for h in heads:
            high[t, h] = news[h]
            total[t, h] = totals[h]
            mixed[t, h] = mixeds[h]
            acc[t, h] = accs[h]

    def step(n, carry):
        b, t = n // 2, n & 1
        base, row, needed, whole = place(sc, span[0], b, t)

        @pl.when(needed & whole)
        def _():
            block(b, t, base, row, False)

        @pl.when(needed & jnp.logical_not(whole))
        def _():
            block(b, t, base, row, True)

        return carry

    lax.fori_loop(0, 4 * pieces, step, 0)
    for t in range(TILES):
        for h in heads:
            values[t, h] = (acc[t, h] * (1.0 / jnp.maximum(total[t, h], 1e-30))).astype(BF16)
            stat[t, h : h + 1, :] = high[t, h]
            stat[t, group + h : group + h + 1, :] = total[t, h]
            stat[t, 2 * group + h : 2 * group + h + 1, :] = mixed[t, h]


def backward(group, width, span, begins, ends, sc, *refs):
    pieces = span[1] - span[0]
    rows, keys, refs = refs[:6], refs[6:10], refs[10:]
    scale = 1.0 / math.sqrt(width)
    unit = LOG2E * scale
    heads = range(group)
    if begins:
        stats, own, values, refs = refs[:SLOTS], refs[SLOTS], refs[SLOTS + 1], refs[SLOTS + 2 :]
    else:
        acc_in, lse_in, delta_in, refs = *refs[:3], refs[3:]
    dkv, refs = refs[0], refs[1:]
    if begins:
        mixed, refs = refs[:SLOTS], refs[SLOTS:]
    if ends:
        dq, refs = refs[:SLOTS], refs[SLOTS:]
    acc, lse, delta, q_s, do_s, k_s, v_s, t_s, grads = refs
    fill(rows, keys, q_s, do_s, k_s, v_s, t_s, group, width, span, 0)
    if begins:
        acc[...] = jnp.zeros_like(acc)
        for t in range(TILES):
            for u in range(SLOTS):
                at = pl.ds(u * CHUNK, CHUNK)
                parts = [stats[s][t, :, pl.ds((u ^ s) * CHUNK, CHUNK)] for s in range(SLOTS)]
                top = functools.reduce(jnp.maximum, [p[:group] for p in parts])
                weights = [jnp.exp2((p[:group] - top) * unit) for p in parts]
                total = sum(w * p[group : 2 * group] for w, p in zip(weights, parts))
                product = sum(w * p[2 * group :] for w, p in zip(weights, parts))
                low, small = top * unit + jnp.log2(total), product / total
                part = own[t, group : 2 * group, at] * jnp.exp2(own[t, :group, at] * unit - low)
                for h in heads:
                    lse[t, h, :, at] = low[h : h + 1]
                    delta[t, h, :, at] = small[h : h + 1]
                    mixed[u][t, h * width : (h + 1) * width, :] = (
                        values[t, h, :, at].astype(F32) * part[h : h + 1]
                    ).astype(BF16)
    else:
        acc[...] = acc_in[...]
        lse[...] = lse_in[...]
        delta[...] = delta_in[...]

    def block(b, t, base, row, masked):
        scores = [dot_t(k_s[b], q_s[t, h]) for h in heads]
        dprobs = [dot_t(v_s[b], do_s[t, h]) for h in heads]
        if masked:
            allowed = allowed_of(sc, base, row)
            scores = [jnp.where(allowed, s, NEG) for s in scores]
        probs = [jnp.exp2(scores[h] * unit - lse[t, h]) for h in heads]
        dscores = [(probs[h] * (dprobs[h] - delta[t, h])).astype(BF16) for h in heads]
        lows = [p.astype(BF16) for p in probs]
        dk = sum(dot(dscores[h], q_s[t, h]) for h in heads)
        dv = sum(dot(lows[h], do_s[t, h]) for h in heads)
        accs = [acc[t, h] + dot(t_s[b], dscores[h]) for h in heads]
        for h in heads:
            acc[t, h] = accs[h]
        grads[:, :width] = grads[:, :width] + dk * scale
        grads[:, width:] = grads[:, width:] + dv

    def step(b, carry):
        grads[...] = jnp.zeros_like(grads)

        def tile(t, carry):
            base, row, needed, whole = place(sc, span[0], b, t)

            @pl.when(needed & whole)
            def _():
                block(b, t, base, row, False)

            @pl.when(needed & jnp.logical_not(whole))
            def _():
                block(b, t, base, row, True)

            return carry

        lax.fori_loop(0, TILES, tile, 0)
        dkv[b] = grads[...].astype(BF16)
        return carry

    lax.fori_loop(0, 2 * pieces, step, 0)
    if ends:
        for t in range(TILES):
            for h in heads:
                value = (acc[t, h] * scale).astype(BF16)
                for s in range(SLOTS):
                    dq[s][t, h * width : (h + 1) * width, :] = value[
                        :, s * CHUNK : (s + 1) * CHUNK
                    ]


def combine(group, width, *refs):
    for one, two, out in zip(refs[:2], refs[2:4], refs[4:]):
        for h in range(group):
            at = pl.ds(h * width, width)
            whole = one[at, :].astype(F32) + two[at, :].astype(F32)
            out[:, at] = jnp.transpose(whole).astype(BF16)


SMEM = pl.BlockSpec(memory_space=pltpu.SMEM)
VMEM = pl.BlockSpec(memory_space=pltpu.VMEM)
PARAMS = pltpu.CompilerParams(vmem_limit_bytes=20 * 1024 * 1024)


def cost(group, width, dots, pieces):
    work = TILES * ROWS * group * pieces * 2 * PAIR * width * 2
    return pl.CostEstimate(flops=2 * dots * work, bytes_accessed=1 << 23, transcendentals=0)


def scratch(group, width, pieces):
    return [
        pltpu.VMEM((TILES, group, ROWS, width), BF16),
        pltpu.VMEM((TILES, group, ROWS, width), BF16),
        pltpu.VMEM((2 * pieces, PAIR, width), BF16),
        pltpu.VMEM((2 * pieces, PAIR, width), BF16),
        pltpu.VMEM((2 * pieces, width, PAIR), BF16),
    ]


def state_shapes(group, width):
    acc = jax.ShapeDtypeStruct((TILES, group, width, ROWS), F32)
    line = jax.ShapeDtypeStruct((TILES, group, 1, ROWS), F32)
    return [acc, line, line]


def run_forward(group, width, sc, rows, keys):
    pieces = len(keys)
    acc, line, _ = state_shapes(group, width)
    return pl.pallas_call(
        functools.partial(forward, group, width, (0, pieces)),
        out_shape=[
            jax.ShapeDtypeStruct(acc.shape, BF16),
            jax.ShapeDtypeStruct((TILES, 3 * group, ROWS), F32),
        ],
        in_specs=[SMEM] + [VMEM] * 10,
        out_specs=[VMEM] * 2,
        scratch_shapes=[pltpu.VMEM(acc.shape, F32)]
        + scratch(group, width, pieces)
        + [pltpu.VMEM(line.shape, F32)] * 3,
        compiler_params=PARAMS,
        cost_estimate=cost(group, width, 3, pieces),
        name="forward",
    )(sc, *rows, *keys)


def run_backward(group, width, span, begins, ends, sc, rows, keys, *more):
    pieces = span[1] - span[0]
    carried = state_shapes(group, width)
    piece = jax.ShapeDtypeStruct((TILES, group * width, CHUNK), BF16)
    shapes = [jax.ShapeDtypeStruct((2 * pieces, PAIR, 2 * width), BF16)]
    shapes = shapes + [piece] * (SLOTS * (begins + ends))
    spaces = scratch(group, width, pieces) + [pltpu.VMEM((PAIR, 2 * width), F32)]
    if not ends:
        shapes = shapes + carried
    else:
        spaces = [pltpu.VMEM(s.shape, F32) for s in carried] + spaces
    return pl.pallas_call(
        functools.partial(backward, group, width, span, begins, ends),
        out_shape=shapes,
        in_specs=[SMEM] + [VMEM] * (10 + len(more)),
        out_specs=[VMEM] * len(shapes),
        scratch_shapes=spaces,
        compiler_params=PARAMS,
        cost_estimate=cost(group, width, 5, pieces),
        name="backward_begin" if begins else "backward_end" if ends else "backward_middle",
    )(sc, *rows, *keys, *more)


def add(*parts):
    return sum(part.astype(F32) for part in parts).astype(BF16)


def local(query, key, value, dout, document):
    width = key.shape[1]
    group = query.shape[1] // width
    send = functools.partial(lax.ppermute, axis_name=AXES)
    qrow, kcol = lax.axis_index("qrow"), lax.axis_index("kcol")
    z, x_lo, x_hi, y = qrow // 2, qrow % 2, kcol // 4, kcol % 4

    row_home, key_home = pl.pallas_call(
        pack,
        out_shape=[
            jax.ShapeDtypeStruct((CHUNK, 2 * group * width), BF16),
            jax.ShapeDtypeStruct((CHUNK, 2 * width), BF16),
        ],
        name="pack",
    )(query, key, value, dout)
    row_other = send(row_home, perm=NEXT)
    a, b = send(key_home, perm=NEAR), send(key_home, perm=REST)
    row_other, a, b = lax.optimization_barrier((row_other, a, b))
    both = jnp.concatenate([row_home, row_other], axis=0)
    near, last = send(both, perm=Y[1]), send(both, perm=Y[3])
    held = jnp.concatenate([key_home, a, b, send(b, perm=NEAR)], axis=0)
    keys = [held] + [send(held, perm=X[n]) for n in range(1, 4)]
    far_own, far_other = send(last[:CHUNK], perm=Y[1]), send(near[CHUNK:], perm=Y[3])
    rows = [row_home, row_other, near, last, far_own, far_other]

    numbers = jnp.arange(DOCS, dtype=jnp.int32)
    starts = jnp.sum((document[None, :] < numbers[:, None]).astype(jnp.int32), axis=1)
    side = 2 - 4 * (z // 2 % 2)
    sources = jnp.stack([z, z + side, z - side, z + 4]) & 7
    sc = jnp.concatenate([jnp.stack([z, x_lo, x_hi, y]), starts, sources]).astype(jnp.int32)

    values, stat = run_forward(group, width, sc, rows, keys)
    unit = LOG2E / math.sqrt(width)
    other = send(stat, perm=NEXT)[::-1]
    top = jnp.maximum(stat[:, :group], other[:, :group])
    mine, theirs = (jnp.exp2((s[:, :group] - top) * unit) for s in (stat, other))
    merged = jnp.concatenate(
        [top]
        + [
            stat[:, n * group : (n + 1) * group] * mine
            + other[:, n * group : (n + 1) * group] * theirs
            for n in (1, 2)
        ],
        axis=1,
    )
    stats = [merged] + [send(merged, perm=Y[s]) for s in range(1, SLOTS)]

    back = functools.partial(run_backward, group, width)
    out = back((3, 4), True, False, sc, rows, keys, *stats, stat, values)
    far, mixed, carried = out[0], out[1 : 1 + SLOTS], out[1 + SLOTS :]
    one, two = send(far[0], perm=NEAR), send(far[1], perm=REST)
    mixed = add(mixed[0], *[send(mixed[s], perm=Y[s]) for s in range(1, SLOTS)])
    near_by, *carried = back((1, 3), False, False, sc, rows, keys, *carried)
    ga = jnp.concatenate([near_by[0], add(near_by[1], two)], axis=0)
    gb = jnp.concatenate([add(near_by[2], one), near_by[3]], axis=0)
    ga, gb, mixed, carried = lax.optimization_barrier((ga, gb, mixed, carried))
    ga, gb = send(ga, perm=NEAR), send(gb, perm=REST)
    close, *dq = back((0, 1), False, True, sc, rows, keys, *carried)
    dq = [dq[0]] + [send(dq[s], perm=Y[s]) for s in range(1, SLOTS)]
    grad = add(close.reshape(2 * PAIR, 2 * width), ga, gb)
    _, mixed, dq = lax.optimization_barrier((grad, mixed, dq))
    mixed = [mixed[0], send(mixed[1], perm=NEXT)]
    grad = grad.reshape(4, CHUNK, 2 * width)
    grad = add(grad[0], *[send(grad[n], perm=X[n]) for n in range(1, 4)])
    dq = add(*dq)
    dq = [dq[0], send(dq[1], perm=NEXT)]
    out_shape = jax.ShapeDtypeStruct((CHUNK, group * width), BF16)
    attended, grad_query = pl.pallas_call(
        functools.partial(combine, group, width),
        out_shape=[out_shape, out_shape],
        in_specs=[VMEM] * 4,
        out_specs=[VMEM] * 2,
        compiler_params=PARAMS,
        name="combine",
    )(mixed[0], dq[0], mixed[1], dq[1])
    return attended, grad_query, grad[:, :width], grad[:, width:]


def solution(mesh):
    by_row = P(("qrow", "kcol"), "head")
    by_key = P(("kcol", "qrow"), "head")
    return jax.shard_map(
        local,
        mesh=mesh,
        in_specs=(by_row, by_key, by_key, by_row, P()),
        out_specs=(by_row, by_row, by_key, by_key),
        check_vma=False,
    )
```

```python
import functools
import math

import jax
import jax.numpy as jnp
from jax import lax
from jax.experimental import pallas as pl
from jax.experimental.pallas import tpu as pltpu
from jax.sharding import PartitionSpec as P

AXES = ("qrow", "kcol")
DEVICES = 128
CHUNK = 128
SLOTS = 4
TILES = 2
ROWS = SLOTS * CHUNK
PAIR = 2 * CHUNK
PIECES = 4
PLANE = 16 * CHUNK
DOCS = 8
NEG = -1e30
FLOOR = -1e29
LOG2E = math.log2(math.e)
F32 = jnp.float32
BF16 = jnp.bfloat16


def flip(mask):
    return [(d, d ^ mask) for d in range(DEVICES)]


Y = [flip(s) for s in range(SLOTS)]
X = [flip(m) for m in (0, 8, 4, 12)]
NEXT = flip(16)
NEAR = flip(32)
REST = [(d, (d + (32 if d // 32 % 2 else -32)) % DEVICES) for d in range(DEVICES)]


def dot(a, b):
    return lax.dot_general(a, b, (((1,), (0,)), ((), ())), preferred_element_type=F32)


def dot_t(a, b):
    return lax.dot_general(a, b, (((1,), (1,)), ((), ())), preferred_element_type=F32)


def fill(rows, keys, q_s, do_s, k_s, v_s, kt_s, vt_s, group, width):
    for t in range(TILES):
        for s in range(SLOTS):
            ref, to = rows[t * SLOTS + s], pl.ds(s * CHUNK, CHUNK)
            for h in range(group):
                q_s[t, h, to, :] = ref[:, h * width : (h + 1) * width]
                do_s[t, h, to, :] = ref[:, (group + h) * width : (group + h + 1) * width]
    for piece in range(PIECES):
        for m, ref in enumerate(keys):
            part = ref[pl.ds(piece * CHUNK, CHUNK), :]
            block, at = 2 * piece + m // 2, pl.ds(m % 2 * CHUNK, CHUNK)
            k_s[block, at, :] = part[:, :width]
            v_s[block, at, :] = part[:, width:]
            kt_s[block, :, at] = jnp.transpose(part[:, :width])
            vt_s[block, :, at] = jnp.transpose(part[:, width:])


def start_of(sc, row):
    start = 0
    for n in range(DOCS):
        one = sc[4 + n]
        start = jnp.maximum(start, jnp.where(one <= row, one, 0))
    return start


def place(sc, block, t):
    z, x_lo, x_hi, y = (sc[n] for n in range(4))
    base = (4 * (x_hi ^ (block & 1)) + y) * PLANE + sc[4 + DOCS + block // 2] * PAIR
    row = ((z * 4 + x_lo * 2 + x_hi) ^ (4 * t)) * ROWS
    needed = (base <= row + ROWS - 1) & (base + PAIR - 1 >= start_of(sc, row))
    whole = (base + PAIR - 1 <= row) & (base >= start_of(sc, row + ROWS - 1))
    return base, row, needed, whole


def allowed_of(sc, base, row):
    key_at = base + (lax.broadcasted_iota(jnp.int32, (PAIR, 1), 0) ^ (sc[1] * CHUNK))
    row_at = row + (lax.broadcasted_iota(jnp.int32, (1, ROWS), 1) ^ (sc[3] * CHUNK))
    return (key_at >= start_of(sc, row_at)) & (key_at <= row_at)


def pack(query, key, value, dout, rows, keys):
    width = query.shape[1]
    rows[:, :width] = query[...]
    rows[:, width:] = dout[...]
    width = key.shape[1]
    keys[:, :width] = key[...]
    keys[:, width:] = value[...]


def forward(group, width, sc, *refs):
    rows, keys, refs = refs[: TILES * SLOTS], refs[TILES * SLOTS :][:4], refs[TILES * SLOTS + 4 :]
    values, stat, q_s, do_s, k_s, v_s, kt_s, t_s, acc, high, total, mixed = refs
    unit = LOG2E / math.sqrt(width)
    heads = range(group)
    fill(rows, keys, q_s, do_s, k_s, v_s, kt_s, t_s, group, width)
    acc[...] = jnp.zeros_like(acc)
    high[...] = jnp.full_like(high, FLOOR)
    total[...] = jnp.zeros_like(total)
    mixed[...] = jnp.zeros_like(mixed)

    def block(b, t, base, row, masked):
        scores = [dot_t(k_s[b], q_s[t, h]) for h in heads]
        dprobs = [dot_t(v_s[b], do_s[t, h]) for h in heads]
        if masked:
            allowed = allowed_of(sc, base, row)
            scores = [jnp.where(allowed, s, NEG) for s in scores]
        olds = [high[t, h] for h in heads]
        news = [jnp.maximum(o, jnp.max(s, axis=0, keepdims=True)) for o, s in zip(olds, scores)]
        shrinks = [jnp.exp2((o - n) * unit) for o, n in zip(olds, news)]
        es = [jnp.exp2(s * unit - n * unit) for s, n in zip(scores, news)]
        totals = [total[t, h] * shrinks[h] + jnp.sum(es[h], axis=0, keepdims=True) for h in heads]
        mixeds = [
            mixed[t, h] * shrinks[h] + jnp.sum(es[h] * dprobs[h], axis=0, keepdims=True)
            for h in heads
        ]
        accs = [acc[t, h] * shrinks[h] + dot(t_s[b], es[h].astype(BF16)) for h in heads]
        for h in heads:
            high[t, h] = news[h]
            total[t, h] = totals[h]
            mixed[t, h] = mixeds[h]
            acc[t, h] = accs[h]

    def step(n, carry):
        b, t = n // 2, n & 1
        base, row, needed, whole = place(sc, b, t)

        @pl.when(needed & whole)
        def _():
            block(b, t, base, row, False)

        @pl.when(needed & jnp.logical_not(whole))
        def _():
            block(b, t, base, row, True)

        return carry

    lax.fori_loop(0, 4 * PIECES, step, 0)
    for t in range(TILES):
        for h in heads:
            values[t, h] = (acc[t, h] * (1.0 / jnp.maximum(total[t, h], 1e-30))).astype(BF16)
            stat[t, h : h + 1, :] = high[t, h]
            stat[t, group + h : group + h + 1, :] = total[t, h]
            stat[t, 2 * group + h : 2 * group + h + 1, :] = mixed[t, h]


def backward(group, width, span, begins, ends, sc, q_s, do_s, k_s, v_s, t_s, *refs):
    scale = 1.0 / math.sqrt(width)
    unit = LOG2E * scale
    heads = range(group)
    if begins:
        stats, own, values, refs = refs[:SLOTS], refs[SLOTS], refs[SLOTS + 1], refs[SLOTS + 2 :]
    else:
        acc_in, lse_in, delta_in, refs = *refs[:3], refs[3:]
    dkv, refs = refs[0], refs[1:]
    if begins:
        mixed, refs = refs[:SLOTS], refs[SLOTS:]
    if ends:
        dq, refs = refs[:SLOTS], refs[SLOTS:]
    acc, lse, delta, grads = refs
    if begins:
        acc[...] = jnp.zeros_like(acc)
        for t in range(TILES):
            for u in range(SLOTS):
                at = pl.ds(u * CHUNK, CHUNK)
                parts = [stats[s][t, :, pl.ds((u ^ s) * CHUNK, CHUNK)] for s in range(SLOTS)]
                top = functools.reduce(jnp.maximum, [p[:group] for p in parts])
                weights = [jnp.exp2((p[:group] - top) * unit) for p in parts]
                total = sum(w * p[group : 2 * group] for w, p in zip(weights, parts))
                product = sum(w * p[2 * group :] for w, p in zip(weights, parts))
                low, small = top * unit + jnp.log2(total), product / total
                part = own[t, group : 2 * group, at] * jnp.exp2(own[t, :group, at] * unit - low)
                for h in heads:
                    lse[t, h, :, at] = low[h : h + 1]
                    delta[t, h, :, at] = small[h : h + 1]
                    mixed[u][t, h * width : (h + 1) * width, :] = (
                        values[t, h, :, at].astype(F32) * part[h : h + 1]
                    ).astype(BF16)
    else:
        acc[...] = acc_in[...]
        lse[...] = lse_in[...]
        delta[...] = delta_in[...]

    def block(b, t, base, row, masked):
        scores = [dot_t(k_s[b], q_s[t, h]) for h in heads]
        dprobs = [dot_t(v_s[b], do_s[t, h]) for h in heads]
        if masked:
            allowed = allowed_of(sc, base, row)
            scores = [jnp.where(allowed, s, NEG) for s in scores]
        probs = [jnp.exp2(scores[h] * unit - lse[t, h]) for h in heads]
        dscores = [(probs[h] * (dprobs[h] - delta[t, h])).astype(BF16) for h in heads]
        lows = [p.astype(BF16) for p in probs]
        dk = sum(dot(dscores[h], q_s[t, h]) for h in heads)
        dv = sum(dot(lows[h], do_s[t, h]) for h in heads)
        accs = [acc[t, h] + dot(t_s[b], dscores[h]) for h in heads]
        for h in heads:
            acc[t, h] = accs[h]
        grads[:, :width] = grads[:, :width] + dk * scale
        grads[:, width:] = grads[:, width:] + dv

    def step(b, carry):
        grads[...] = jnp.zeros_like(grads)

        def tile(t, carry):
            base, row, needed, whole = place(sc, b, t)

            @pl.when(needed & whole)
            def _():
                block(b, t, base, row, False)

            @pl.when(needed & jnp.logical_not(whole))
            def _():
                block(b, t, base, row, True)

            return carry

        lax.fori_loop(0, TILES, tile, 0)
        dkv[b - 2 * span[0]] = grads[...].astype(BF16)
        return carry

    lax.fori_loop(2 * span[0], 2 * span[1], step, 0)
    if ends:
        for t in range(TILES):
            for h in heads:
                value = (acc[t, h] * scale).astype(BF16)
                for s in range(SLOTS):
                    dq[s][t, h * width : (h + 1) * width, :] = value[
                        :, s * CHUNK : (s + 1) * CHUNK
                    ]


def combine(group, width, *refs):
    for one, two, out in zip(refs[:2], refs[2:4], refs[4:]):
        for h in range(group):
            at = pl.ds(h * width, width)
            whole = one[at, :].astype(F32) + two[at, :].astype(F32)
            out[:, at] = jnp.transpose(whole).astype(BF16)


SMEM = pl.BlockSpec(memory_space=pltpu.SMEM)
VMEM = pl.BlockSpec(memory_space=pltpu.VMEM)
PARAMS = pltpu.CompilerParams(vmem_limit_bytes=20 * 1024 * 1024)


def cost(group, width, dots, pieces):
    work = TILES * ROWS * group * pieces * 2 * PAIR * width * 2
    return pl.CostEstimate(flops=2 * dots * work, bytes_accessed=1 << 23, transcendentals=0)


def state_shapes(group, width):
    acc = jax.ShapeDtypeStruct((TILES, group, width, ROWS), F32)
    line = jax.ShapeDtypeStruct((TILES, group, 1, ROWS), F32)
    return [acc, line, line]


def run_forward(group, width, sc, rows, keys):
    acc, line, _ = state_shapes(group, width)
    row = jax.ShapeDtypeStruct((TILES, group, ROWS, width), BF16)
    key = jax.ShapeDtypeStruct((2 * PIECES, PAIR, width), BF16)
    turned = jax.ShapeDtypeStruct((2 * PIECES, width, PAIR), BF16)
    stat = jax.ShapeDtypeStruct((TILES, 3 * group, ROWS), F32)
    return pl.pallas_call(
        functools.partial(forward, group, width),
        out_shape=[jax.ShapeDtypeStruct(acc.shape, BF16), stat, row, row, key, key, turned],
        in_specs=[SMEM] + [VMEM] * (TILES * SLOTS + 4),
        out_specs=[VMEM] * 7,
        scratch_shapes=[pltpu.VMEM(turned.shape, BF16), pltpu.VMEM(acc.shape, F32)]
        + [pltpu.VMEM(line.shape, F32)] * 3,
        compiler_params=PARAMS,
        cost_estimate=cost(group, width, 3, PIECES),
        name="forward",
    )(sc, *rows, *keys)


def run_backward(group, width, span, begins, ends, sc, held, *more):
    pieces = span[1] - span[0]
    carried = state_shapes(group, width)
    piece = jax.ShapeDtypeStruct((TILES, group * width, CHUNK), BF16)
    shapes = [jax.ShapeDtypeStruct((2 * pieces, PAIR, 2 * width), BF16)]
    shapes = shapes + [piece] * (SLOTS * (begins + ends))
    spaces = [pltpu.VMEM((PAIR, 2 * width), F32)]
    if not ends:
        shapes = shapes + carried
    else:
        spaces = [pltpu.VMEM(s.shape, F32) for s in carried] + spaces
    return pl.pallas_call(
        functools.partial(backward, group, width, span, begins, ends),
        out_shape=shapes,
        in_specs=[SMEM] + [VMEM] * (len(held) + len(more)),
        out_specs=[VMEM] * len(shapes),
        scratch_shapes=spaces,
        compiler_params=PARAMS,
        cost_estimate=cost(group, width, 5, pieces),
        name="backward_begin" if begins else "backward_end" if ends else "backward_middle",
    )(sc, *held, *more)


def add(*parts):
    return sum(part.astype(F32) for part in parts).astype(BF16)


def local(query, key, value, dout, document):
    width = key.shape[1]
    group = query.shape[1] // width
    send = functools.partial(lax.ppermute, axis_name=AXES)
    qrow, kcol = lax.axis_index("qrow"), lax.axis_index("kcol")
    z, x_lo, x_hi, y = qrow // 2, qrow % 2, kcol // 4, kcol % 4

    row_home, key_home = pl.pallas_call(
        pack,
        out_shape=[
            jax.ShapeDtypeStruct((CHUNK, 2 * group * width), BF16),
            jax.ShapeDtypeStruct((CHUNK, 2 * width), BF16),
        ],
        name="pack",
    )(query, key, value, dout)
    row_other = send(row_home, perm=NEXT)
    near, last = send(row_home, perm=Y[1]), send(row_home, perm=Y[3])
    a, b = send(key_home, perm=NEAR), send(key_home, perm=REST)
    row_other, near, last, a, b = lax.optimization_barrier((row_other, near, last, a, b))
    near_other, last_other = send(row_other, perm=Y[1]), send(row_other, perm=Y[3])
    held = jnp.concatenate([key_home, a, b, send(b, perm=NEAR)], axis=0)
    keys = [held] + [send(held, perm=X[n]) for n in range(1, 4)]
    far, far_other = send(last, perm=Y[1]), send(near_other, perm=Y[3])
    rows = [row_home, near, far, last, row_other, near_other, far_other, last_other]

    numbers = jnp.arange(DOCS, dtype=jnp.int32)
    starts = jnp.sum((document[None, :] < numbers[:, None]).astype(jnp.int32), axis=1)
    side = 2 - 4 * (z // 2 % 2)
    sources = jnp.stack([z, z + side, z - side, z + 4]) & 7
    sc = jnp.concatenate([jnp.stack([z, x_lo, x_hi, y]), starts, sources]).astype(jnp.int32)

    values, stat, *held = run_forward(group, width, sc, rows, keys)
    unit = LOG2E / math.sqrt(width)
    other = send(stat, perm=NEXT)[::-1]
    top = jnp.maximum(stat[:, :group], other[:, :group])
    mine, theirs = (jnp.exp2((s[:, :group] - top) * unit) for s in (stat, other))
    merged = jnp.concatenate(
        [top]
        + [
            stat[:, n * group : (n + 1) * group] * mine
            + other[:, n * group : (n + 1) * group] * theirs
            for n in (1, 2)
        ],
        axis=1,
    )
    stats = [merged] + [send(merged, perm=Y[s]) for s in range(1, SLOTS)]

    back = functools.partial(run_backward, group, width)
    out = back((3, 4), True, False, sc, held, *stats, stat, values)
    far, mixed, carried = out[0], out[1 : 1 + SLOTS], out[1 + SLOTS :]
    one, two = send(far[0], perm=NEAR), send(far[1], perm=REST)
    mixed = add(mixed[0], *[send(mixed[s], perm=Y[s]) for s in range(1, SLOTS)])
    near_by, *carried = back((1, 3), False, False, sc, held, *carried)
    ga = jnp.concatenate([near_by[0], add(near_by[1], two)], axis=0)
    gb = jnp.concatenate([add(near_by[2], one), near_by[3]], axis=0)
    ga, gb, mixed, carried = lax.optimization_barrier((ga, gb, mixed, carried))
    ga, gb = send(ga, perm=NEAR), send(gb, perm=REST)
    close, *dq = back((0, 1), False, True, sc, held, *carried)
    dq = [dq[0]] + [send(dq[s], perm=Y[s]) for s in range(1, SLOTS)]
    grad = add(close.reshape(2 * PAIR, 2 * width), ga, gb)
    _, mixed, dq = lax.optimization_barrier((grad, mixed, dq))
    mixed = [mixed[0], send(mixed[1], perm=NEXT)]
    grad = grad.reshape(4, CHUNK, 2 * width)
    grad = add(grad[0], *[send(grad[n], perm=X[n]) for n in range(1, 4)])
    dq = add(*dq)
    dq = [dq[0], send(dq[1], perm=NEXT)]
    out_shape = jax.ShapeDtypeStruct((CHUNK, group * width), BF16)
    attended, grad_query = pl.pallas_call(
        functools.partial(combine, group, width),
        out_shape=[out_shape, out_shape],
        in_specs=[VMEM] * 4,
        out_specs=[VMEM] * 2,
        compiler_params=PARAMS,
        name="combine",
    )(mixed[0], dq[0], mixed[1], dq[1])
    return attended, grad_query, grad[:, :width], grad[:, width:]


def solution(mesh):
    by_row = P(("qrow", "kcol"), "head")
    by_key = P(("kcol", "qrow"), "head")
    return jax.shard_map(
        local,
        mesh=mesh,
        in_specs=(by_row, by_key, by_key, by_row, P()),
        out_specs=(by_row, by_row, by_key, by_key),
        check_vma=False,
    )
```

```python
import functools
import math

import jax
import jax.numpy as jnp
from jax import lax
from jax.experimental import pallas as pl
from jax.experimental.pallas import tpu as pltpu
from jax.sharding import PartitionSpec as P

AXES = ("qrow", "kcol")
DEVICES = 128
CHUNK = 128
SLOTS = 4
TILES = 2
ROWS = SLOTS * CHUNK
PAIR = 2 * CHUNK
PIECES = 4
PLANE = 16 * CHUNK
DOCS = 8
NEG = -1e30
FLOOR = -1e29
LOG2E = math.log2(math.e)
F32 = jnp.float32
BF16 = jnp.bfloat16


def flip(mask):
    return [(d, d ^ mask) for d in range(DEVICES)]


Y = [flip(s) for s in range(SLOTS)]
X = [flip(m) for m in (0, 8, 4, 12)]
NEXT = flip(16)
NEAR = flip(32)
REST = [(d, (d + (32 if d // 32 % 2 else -32)) % DEVICES) for d in range(DEVICES)]

OPPOSITE = flip(64)


def dot(a, b):
    return lax.dot_general(a, b, (((1,), (0,)), ((), ())), preferred_element_type=F32)


def dot_t(a, b):
    return lax.dot_general(a, b, (((1,), (1,)), ((), ())), preferred_element_type=F32)


def fill(rows, keys, q_s, do_s, k_s, v_s, kt_s, vt_s, group, width):
    own, other, near, last, far_own, far_other = rows
    top, low = pl.ds(0, CHUNK), pl.ds(CHUNK, CHUNK)
    parts = [
        [(own, top), (near, top), (far_own, top), (last, top)],
        [(other, top), (near, low), (far_other, top), (last, low)],
    ]
    for t in range(TILES):
        for s in range(SLOTS):
            ref, at = parts[t][s]
            part, to = ref[at, :], pl.ds(s * CHUNK, CHUNK)
            for h in range(group):
                q_s[t, h, to, :] = part[:, h * width : (h + 1) * width]
                do_s[t, h, to, :] = part[:, (group + h) * width : (group + h + 1) * width]
    for piece in range(PIECES):
        for m, ref in enumerate(keys):
            part = ref[pl.ds(piece * CHUNK, CHUNK), :]
            block, at = 2 * piece + m // 2, pl.ds(m % 2 * CHUNK, CHUNK)
            k_s[block, at, :] = part[:, :width]
            v_s[block, at, :] = part[:, width:]
            kt_s[block, :, at] = jnp.transpose(part[:, :width])
            vt_s[block, :, at] = jnp.transpose(part[:, width:])


def start_of(sc, row):
    start = 0
    for n in range(DOCS):
        one = sc[4 + n]
        start = jnp.maximum(start, jnp.where(one <= row, one, 0))
    return start


def place(sc, block, t):
    z, x_lo, x_hi, y = (sc[n] for n in range(4))
    base = (4 * (x_hi ^ (block & 1)) + y) * PLANE + sc[4 + DOCS + block // 2] * PAIR
    row = ((z * 4 + x_lo * 2 + x_hi) ^ (4 * t)) * ROWS
    needed = (base <= row + ROWS - 1) & (base + PAIR - 1 >= start_of(sc, row))
    whole = (base + PAIR - 1 <= row) & (base >= start_of(sc, row + ROWS - 1))
    return base, row, needed, whole


def allowed_of(sc, base, row):
    key_at = base + (lax.broadcasted_iota(jnp.int32, (PAIR, 1), 0) ^ (sc[1] * CHUNK))
    row_at = row + (lax.broadcasted_iota(jnp.int32, (1, ROWS), 1) ^ (sc[3] * CHUNK))
    return (key_at >= start_of(sc, row_at)) & (key_at <= row_at)


def pack(query, key, value, dout, rows, keys):
    width = query.shape[1]
    rows[:, :width] = query[...]
    rows[:, width:] = dout[...]
    width = key.shape[1]
    keys[:, :width] = key[...]
    keys[:, width:] = value[...]


def forward(group, width, sc, *refs):
    rows, keys, refs = refs[:6], refs[6:10], refs[10:]
    values, stat, q_s, do_s, k_s, v_s, kt_s, t_s, acc, high, total, mixed = refs
    unit = LOG2E / math.sqrt(width)
    heads = range(group)
    fill(rows, keys, q_s, do_s, k_s, v_s, kt_s, t_s, group, width)
    acc[...] = jnp.zeros_like(acc)
    high[...] = jnp.full_like(high, FLOOR)
    total[...] = jnp.zeros_like(total)
    mixed[...] = jnp.zeros_like(mixed)

    def block(b, t, base, row, masked):
        scores = [dot_t(k_s[b], q_s[t, h]) for h in heads]
        dprobs = [dot_t(v_s[b], do_s[t, h]) for h in heads]
        if masked:
            allowed = allowed_of(sc, base, row)
            scores = [jnp.where(allowed, s, NEG) for s in scores]
        olds = [high[t, h] for h in heads]
        news = [jnp.maximum(o, jnp.max(s, axis=0, keepdims=True)) for o, s in zip(olds, scores)]
        shrinks = [jnp.exp2((o - n) * unit) for o, n in zip(olds, news)]
        es = [jnp.exp2(s * unit - n * unit) for s, n in zip(scores, news)]
        totals = [total[t, h] * shrinks[h] + jnp.sum(es[h], axis=0, keepdims=True) for h in heads]
        mixeds = [
            mixed[t, h] * shrinks[h] + jnp.sum(es[h] * dprobs[h], axis=0, keepdims=True)
            for h in heads
        ]
        accs = [acc[t, h] * shrinks[h] + dot(t_s[b], es[h].astype(BF16)) for h in heads]
        for h in heads:
            high[t, h] = news[h]
            total[t, h] = totals[h]
            mixed[t, h] = mixeds[h]
            acc[t, h] = accs[h]

    def step(n, carry):
        b, t = n // 2, n & 1
        base, row, needed, whole = place(sc, b, t)

        @pl.when(needed & whole)
        def _():
            block(b, t, base, row, False)

        @pl.when(needed & jnp.logical_not(whole))
        def _():
            block(b, t, base, row, True)

        return carry

    lax.fori_loop(0, 4 * PIECES, step, 0)
    for t in range(TILES):
        for h in heads:
            values[t, h] = (acc[t, h] * (1.0 / jnp.maximum(total[t, h], 1e-30))).astype(BF16)
            stat[t, h : h + 1, :] = high[t, h]
            stat[t, group + h : group + h + 1, :] = total[t, h]
            stat[t, 2 * group + h : 2 * group + h + 1, :] = mixed[t, h]


def backward(group, width, span, begins, ends, sc, q_s, do_s, k_s, v_s, t_s, *refs):
    scale = 1.0 / math.sqrt(width)
    unit = LOG2E * scale
    heads = range(group)
    if begins:
        stats, own, values, refs = refs[:SLOTS], refs[SLOTS], refs[SLOTS + 1], refs[SLOTS + 2 :]
    else:
        acc_in, lse_in, delta_in, refs = *refs[:3], refs[3:]
    dkv, refs = refs[0], refs[1:]
    if begins:
        mixed, refs = refs[:SLOTS], refs[SLOTS:]
    if ends:
        dq, refs = refs[:SLOTS], refs[SLOTS:]
    acc, lse, delta, grads = refs
    if begins:
        acc[...] = jnp.zeros_like(acc)
        for t in range(TILES):
            for u in range(SLOTS):
                at = pl.ds(u * CHUNK, CHUNK)
                parts = [stats[s][t, :, pl.ds((u ^ s) * CHUNK, CHUNK)] for s in range(SLOTS)]
                top = functools.reduce(jnp.maximum, [p[:group] for p in parts])
                weights = [jnp.exp2((p[:group] - top) * unit) for p in parts]
                total = sum(w * p[group : 2 * group] for w, p in zip(weights, parts))
                product = sum(w * p[2 * group :] for w, p in zip(weights, parts))
                low, small = top * unit + jnp.log2(total), product / total
                part = own[t, group : 2 * group, at] * jnp.exp2(own[t, :group, at] * unit - low)
                for h in heads:
                    lse[t, h, :, at] = low[h : h + 1]
                    delta[t, h, :, at] = small[h : h + 1]
                    mixed[u][t, h * width : (h + 1) * width, :] = (
                        values[t, h, :, at].astype(F32) * part[h : h + 1]
                    ).astype(BF16)
    else:
        acc[...] = acc_in[...]
        lse[...] = lse_in[...]
        delta[...] = delta_in[...]

    def block(b, t, base, row, masked):
        scores = [dot_t(k_s[b], q_s[t, h]) for h in heads]
        dprobs = [dot_t(v_s[b], do_s[t, h]) for h in heads]
        if masked:
            allowed = allowed_of(sc, base, row)
            scores = [jnp.where(allowed, s, NEG) for s in scores]
        probs = [jnp.exp2(scores[h] * unit - lse[t, h]) for h in heads]
        dscores = [(probs[h] * (dprobs[h] - delta[t, h])).astype(BF16) for h in heads]
        lows = [p.astype(BF16) for p in probs]
        dk = sum(dot(dscores[h], q_s[t, h]) for h in heads)
        dv = sum(dot(lows[h], do_s[t, h]) for h in heads)
        accs = [acc[t, h] + dot(t_s[b], dscores[h]) for h in heads]
        for h in heads:
            acc[t, h] = accs[h]
        grads[:, :width] = grads[:, :width] + dk * scale
        grads[:, width:] = grads[:, width:] + dv

    def step(b, carry):
        grads[...] = jnp.zeros_like(grads)

        def tile(t, carry):
            base, row, needed, whole = place(sc, b, t)

            @pl.when(needed & whole)
            def _():
                block(b, t, base, row, False)

            @pl.when(needed & jnp.logical_not(whole))
            def _():
                block(b, t, base, row, True)

            return carry

        lax.fori_loop(0, TILES, tile, 0)
        dkv[b - 2 * span[0]] = grads[...].astype(BF16)
        return carry

    lax.fori_loop(2 * span[0], 2 * span[1], step, 0)
    if ends:
        for t in range(TILES):
            for h in heads:
                value = (acc[t, h] * scale).astype(BF16)
                for s in range(SLOTS):
                    dq[s][t, h * width : (h + 1) * width, :] = value[
                        :, s * CHUNK : (s + 1) * CHUNK
                    ]


def combine(group, width, *refs):
    for one, two, out in zip(refs[:2], refs[2:4], refs[4:]):
        for h in range(group):
            at = pl.ds(h * width, width)
            whole = one[at, :].astype(F32) + two[at, :].astype(F32)
            out[:, at] = jnp.transpose(whole).astype(BF16)


SMEM = pl.BlockSpec(memory_space=pltpu.SMEM)
VMEM = pl.BlockSpec(memory_space=pltpu.VMEM)
PARAMS = pltpu.CompilerParams(vmem_limit_bytes=20 * 1024 * 1024)


def cost(group, width, dots, pieces):
    work = TILES * ROWS * group * pieces * 2 * PAIR * width * 2
    return pl.CostEstimate(flops=2 * dots * work, bytes_accessed=1 << 23, transcendentals=0)


def state_shapes(group, width):
    acc = jax.ShapeDtypeStruct((TILES, group, width, ROWS), F32)
    line = jax.ShapeDtypeStruct((TILES, group, 1, ROWS), F32)
    return [acc, line, line]


def run_forward(group, width, sc, rows, keys):
    acc, line, _ = state_shapes(group, width)
    row = jax.ShapeDtypeStruct((TILES, group, ROWS, width), BF16)
    key = jax.ShapeDtypeStruct((2 * PIECES, PAIR, width), BF16)
    turned = jax.ShapeDtypeStruct((2 * PIECES, width, PAIR), BF16)
    stat = jax.ShapeDtypeStruct((TILES, 3 * group, ROWS), F32)
    return pl.pallas_call(
        functools.partial(forward, group, width),
        out_shape=[jax.ShapeDtypeStruct(acc.shape, BF16), stat, row, row, key, key, turned],
        in_specs=[SMEM] + [VMEM] * 10,
        out_specs=[VMEM] * 7,
        scratch_shapes=[pltpu.VMEM(turned.shape, BF16), pltpu.VMEM(acc.shape, F32)]
        + [pltpu.VMEM(line.shape, F32)] * 3,
        compiler_params=PARAMS,
        cost_estimate=cost(group, width, 3, PIECES),
        name="forward",
    )(sc, *rows, *keys)


def run_backward(group, width, span, begins, ends, sc, held, *more):
    pieces = span[1] - span[0]
    carried = state_shapes(group, width)
    piece = jax.ShapeDtypeStruct((TILES, group * width, CHUNK), BF16)
    shapes = [jax.ShapeDtypeStruct((2 * pieces, PAIR, 2 * width), BF16)]
    shapes = shapes + [piece] * (SLOTS * (begins + ends))
    spaces = [pltpu.VMEM((PAIR, 2 * width), F32)]
    if not ends:
        shapes = shapes + carried
    else:
        spaces = [pltpu.VMEM(s.shape, F32) for s in carried] + spaces
    return pl.pallas_call(
        functools.partial(backward, group, width, span, begins, ends),
        out_shape=shapes,
        in_specs=[SMEM] + [VMEM] * (len(held) + len(more)),
        out_specs=[VMEM] * len(shapes),
        scratch_shapes=spaces,
        compiler_params=PARAMS,
        cost_estimate=cost(group, width, 5, pieces),
        name="backward_begin" if begins else "backward_end" if ends else "backward_middle",
    )(sc, *held, *more)


def add(*parts):
    return sum(part.astype(F32) for part in parts).astype(BF16)


def local(query, key, value, dout, document):
    width = key.shape[1]
    group = query.shape[1] // width
    send = functools.partial(lax.ppermute, axis_name=AXES)
    qrow, kcol = lax.axis_index("qrow"), lax.axis_index("kcol")
    z, x_lo, x_hi, y = qrow // 2, qrow % 2, kcol // 4, kcol % 4

    row_home, key_home = pl.pallas_call(
        pack,
        out_shape=[
            jax.ShapeDtypeStruct((CHUNK, 2 * group * width), BF16),
            jax.ShapeDtypeStruct((CHUNK, 2 * width), BF16),
        ],
        name="pack",
    )(query, key, value, dout)
    row_other = send(row_home, perm=NEXT)
    a, b = send(key_home, perm=NEAR), send(key_home, perm=REST)
    row_other, a, b = lax.optimization_barrier((row_other, a, b))
    both = jnp.concatenate([row_home, row_other], axis=0)
    near, last = send(both, perm=Y[1]), send(both, perm=Y[3])
    held = jnp.concatenate([key_home, a, b, send(b, perm=NEAR)], axis=0)
    keys = [held] + [send(held, perm=X[n]) for n in range(1, 4)]
    far_own, far_other = send(last[:CHUNK], perm=Y[1]), send(near[CHUNK:], perm=Y[3])
    rows = [row_home, row_other, near, last, far_own, far_other]

    numbers = jnp.arange(DOCS, dtype=jnp.int32)
    starts = jnp.sum((document[None, :] < numbers[:, None]).astype(jnp.int32), axis=1)
    side = 2 - 4 * (z // 2 % 2)
    sources = jnp.stack([z, z + side, z - side, z + 4]) & 7
    sc = jnp.concatenate([jnp.stack([z, x_lo, x_hi, y]), starts, sources]).astype(jnp.int32)

    values, stat, *held = run_forward(group, width, sc, rows, keys)
    unit = LOG2E / math.sqrt(width)
    other = send(stat, perm=NEXT)[::-1]
    top = jnp.maximum(stat[:, :group], other[:, :group])
    mine, theirs = (jnp.exp2((s[:, :group] - top) * unit) for s in (stat, other))
    merged = jnp.concatenate(
        [top]
        + [
            stat[:, n * group : (n + 1) * group] * mine
            + other[:, n * group : (n + 1) * group] * theirs
            for n in (1, 2)
        ],
        axis=1,
    )
    stats = [merged] + [send(merged, perm=Y[s]) for s in range(1, SLOTS)]

    back = functools.partial(run_backward, group, width)
    out = back((3, 4), True, False, sc, held, *stats, stat, values)
    far, mixed, carried = out[0], out[1 : 1 + SLOTS], out[1 + SLOTS :]
    flat = (2 * PAIR, 2 * width)
    gc = send(far.reshape(flat), perm=OPPOSITE)
    mixed = [mixed[0]] + [send(mixed[s], perm=Y[s]) for s in range(1, SLOTS)]
    near_by, *carried = back((1, 3), False, False, sc, held, *carried)
    near_by, mixed, carried = lax.optimization_barrier((near_by, mixed, carried))
    ga = send(near_by[:2].reshape(flat), perm=NEAR)
    gb = send(near_by[2:].reshape(flat), perm=REST)
    close, *dq = back((0, 1), False, True, sc, held, *carried)
    dq = [dq[0]] + [send(dq[s], perm=Y[s]) for s in range(1, SLOTS)]
    grad = add(close.reshape(flat), ga, gb, gc)
    _, mixed, dq = lax.optimization_barrier((grad, mixed, dq))
    mixed = add(*mixed)
    mixed = [mixed[0], send(mixed[1], perm=NEXT)]
    grad = grad.reshape(4, CHUNK, 2 * width)
    grad = add(grad[0], *[send(grad[n], perm=X[n]) for n in range(1, 4)])
    dq = add(*dq)
    dq = [dq[0], send(dq[1], perm=NEXT)]
    out_shape = jax.ShapeDtypeStruct((CHUNK, group * width), BF16)
    attended, grad_query = pl.pallas_call(
        functools.partial(combine, group, width),
        out_shape=[out_shape, out_shape],
        in_specs=[VMEM] * 4,
        out_specs=[VMEM] * 2,
        compiler_params=PARAMS,
        name="combine",
    )(mixed[0], dq[0], mixed[1], dq[1])
    return attended, grad_query, grad[:, :width], grad[:, width:]


def solution(mesh):
    by_row = P(("qrow", "kcol"), "head")
    by_key = P(("kcol", "qrow"), "head")
    return jax.shard_map(
        local,
        mesh=mesh,
        in_specs=(by_row, by_key, by_key, by_row, P()),
        out_specs=(by_row, by_row, by_key, by_key),
        check_vma=False,
    )
```

```python
import functools
import math

import jax
import jax.numpy as jnp
from jax import lax
from jax.experimental import pallas as pl
from jax.experimental.pallas import tpu as pltpu
from jax.sharding import PartitionSpec as P

AXES = ("qrow", "kcol")
DEVICES = 128
CHUNK = 128
SLOTS = 4
TILES = 2
ROWS = SLOTS * CHUNK
PAIR = 2 * CHUNK
PIECES = 4
PLANE = 16 * CHUNK
DOCS = 8
NEG = -1e30
FLOOR = -1e29
SAFE = 60.0
LOG2E = math.log2(math.e)
F32 = jnp.float32
BF16 = jnp.bfloat16


def flip(mask):
    return [(d, d ^ mask) for d in range(DEVICES)]


Y = [flip(s) for s in range(SLOTS)]
X = [flip(m) for m in (0, 8, 4, 12)]
NEXT = flip(16)
NEAR = flip(32)
REST = [(d, (d + (32 if d // 32 % 2 else -32)) % DEVICES) for d in range(DEVICES)]

OPPOSITE = flip(64)


def dot(a, b):
    return lax.dot_general(a, b, (((1,), (0,)), ((), ())), preferred_element_type=F32)


def dot_t(a, b):
    return lax.dot_general(a, b, (((1,), (1,)), ((), ())), preferred_element_type=F32)


def fill(rows, keys, q_s, do_s, k_s, v_s, kt_s, vt_s, group, width):
    own, other, near, last, far_own, far_other = rows
    top, low = pl.ds(0, CHUNK), pl.ds(CHUNK, CHUNK)
    parts = [
        [(own, top), (near, top), (far_own, top), (last, top)],
        [(other, top), (near, low), (far_other, top), (last, low)],
    ]
    for t in range(TILES):
        for s in range(SLOTS):
            ref, at = parts[t][s]
            part, to = ref[at, :], pl.ds(s * CHUNK, CHUNK)
            for h in range(group):
                q_s[t, h, to, :] = part[:, h * width : (h + 1) * width]
                do_s[t, h, to, :] = part[:, (group + h) * width : (group + h + 1) * width]
    for piece in range(PIECES):
        for m, ref in enumerate(keys):
            part = ref[pl.ds(piece * CHUNK, CHUNK), :]
            block, at = 2 * piece + m // 2, pl.ds(m % 2 * CHUNK, CHUNK)
            k_s[block, at, :] = part[:, :width]
            v_s[block, at, :] = part[:, width:]
            kt_s[block, :, at] = jnp.transpose(part[:, :width])
            vt_s[block, :, at] = jnp.transpose(part[:, width:])


def start_of(sc, row):
    start = 0
    for n in range(DOCS):
        one = sc[4 + n]
        start = jnp.maximum(start, jnp.where(one <= row, one, 0))
    return start


def place(sc, block, t):
    z, x_lo, x_hi, y = (sc[n] for n in range(4))
    base = (4 * (x_hi ^ (block & 1)) + y) * PLANE + sc[4 + DOCS + block // 2] * PAIR
    row = ((z * 4 + x_lo * 2 + x_hi) ^ (4 * t)) * ROWS
    needed = (base <= row + ROWS - 1) & (base + PAIR - 1 >= start_of(sc, row))
    whole = (base + PAIR - 1 <= row) & (base >= start_of(sc, row + ROWS - 1))
    return base, row, needed, whole


def allowed_of(sc, base, row):
    key_at = base + (lax.broadcasted_iota(jnp.int32, (PAIR, 1), 0) ^ (sc[1] * CHUNK))
    row_at = row + (lax.broadcasted_iota(jnp.int32, (1, ROWS), 1) ^ (sc[3] * CHUNK))
    return (key_at >= start_of(sc, row_at)) & (key_at <= row_at)


def pack(query, key, value, dout, rows, keys):
    width = query.shape[1]
    rows[:, :width] = query[...]
    rows[:, width:] = dout[...]
    width = key.shape[1]
    keys[:, :width] = key[...]
    keys[:, width:] = value[...]


def forward(group, width, sc, *refs):
    rows, keys, refs = refs[:6], refs[6:10], refs[10:]
    values, stat, q_s, do_s, k_s, v_s, kt_s, t_s, acc, high, total = refs
    unit = LOG2E / math.sqrt(width)
    heads = range(group)
    fill(rows, keys, q_s, do_s, k_s, v_s, kt_s, t_s, group, width)
    acc[...] = jnp.zeros_like(acc)
    high[...] = jnp.full_like(high, FLOOR)
    total[...] = jnp.zeros_like(total)

    def widest(parts):
        ones = jnp.ones((width, width), BF16)
        return jnp.max(functools.reduce(jnp.maximum, [dot(p * p, ones) for p in parts]))

    rows_widest = widest([q_s[t, h] for t in range(TILES) for h in heads])
    keys_widest = widest([k_s[b] for b in range(2 * PIECES)])
    small = rows_widest * keys_widest * (unit * unit) <= SAFE * SAFE

    def scores_of(b, t, base, row, masked):
        scores = [dot_t(k_s[b], q_s[t, h]) for h in heads]
        if masked:
            allowed = allowed_of(sc, base, row)
            scores = [jnp.where(allowed, s, NEG) for s in scores]
        return scores

    def shifted(b, t, base, row, masked):
        scores = scores_of(b, t, base, row, masked)
        olds = [high[t, h] for h in heads]
        news = [jnp.maximum(o, jnp.max(s, axis=0, keepdims=True)) for o, s in zip(olds, scores)]
        shrinks = [jnp.exp2((o - n) * unit) for o, n in zip(olds, news)]
        es = [jnp.exp2(s * unit - n * unit) for s, n in zip(scores, news)]
        totals = [total[t, h] * shrinks[h] + jnp.sum(es[h], axis=0, keepdims=True) for h in heads]
        accs = [acc[t, h] * shrinks[h] + dot(t_s[b], es[h].astype(BF16)) for h in heads]
        for h in heads:
            high[t, h] = news[h]
            total[t, h] = totals[h]
            acc[t, h] = accs[h]

    def direct(b, t, base, row, masked):
        es = [jnp.exp2(s * unit) for s in scores_of(b, t, base, row, masked)]
        totals = [total[t, h] + jnp.sum(es[h], axis=0, keepdims=True) for h in heads]
        accs = [acc[t, h] + dot(t_s[b], es[h].astype(BF16)) for h in heads]
        for h in heads:
            total[t, h] = totals[h]
            acc[t, h] = accs[h]

    def over_blocks(block):
        def step(n, carry):
            b, t = n // 2, n & 1
            base, row, needed, whole = place(sc, b, t)

            @pl.when(needed & whole)
            def _():
                block(b, t, base, row, False)

            @pl.when(needed & jnp.logical_not(whole))
            def _():
                block(b, t, base, row, True)

            return carry

        lax.fori_loop(0, 4 * PIECES, step, 0)

    @pl.when(small)
    def _():
        over_blocks(direct)
        high[...] = jnp.where(total[...] > 0.0, 0.0, FLOOR)

    @pl.when(jnp.logical_not(small))
    def _():
        over_blocks(shifted)

    for t in range(TILES):
        for h in heads:
            product = acc[t, h] * jnp.transpose(do_s[t, h]).astype(F32)
            values[t, h] = (acc[t, h] * (1.0 / jnp.maximum(total[t, h], 1e-30))).astype(BF16)
            stat[t, h : h + 1, :] = high[t, h]
            stat[t, group + h : group + h + 1, :] = total[t, h]
            stat[t, 2 * group + h : 2 * group + h + 1, :] = jnp.sum(product, axis=0, keepdims=True)


def backward(group, width, span, begins, ends, sc, q_s, do_s, k_s, v_s, t_s, *refs):
    scale = 1.0 / math.sqrt(width)
    unit = LOG2E * scale
    heads = range(group)
    if begins:
        stats, own, values, refs = refs[:SLOTS], refs[SLOTS], refs[SLOTS + 1], refs[SLOTS + 2 :]
    else:
        acc_in, lse_in, delta_in, refs = *refs[:3], refs[3:]
    dkv, refs = refs[0], refs[1:]
    if begins:
        mixed, refs = refs[:SLOTS], refs[SLOTS:]
    if ends:
        dq, refs = refs[:SLOTS], refs[SLOTS:]
    acc, lse, delta, grads = refs
    if begins:
        acc[...] = jnp.zeros_like(acc)
        for t in range(TILES):
            for u in range(SLOTS):
                at = pl.ds(u * CHUNK, CHUNK)
                parts = [stats[s][t, :, pl.ds((u ^ s) * CHUNK, CHUNK)] for s in range(SLOTS)]
                top = functools.reduce(jnp.maximum, [p[:group] for p in parts])
                weights = [jnp.exp2((p[:group] - top) * unit) for p in parts]
                total = sum(w * p[group : 2 * group] for w, p in zip(weights, parts))
                product = sum(w * p[2 * group :] for w, p in zip(weights, parts))
                low, small = top * unit + jnp.log2(total), product / total
                part = own[t, group : 2 * group, at] * jnp.exp2(own[t, :group, at] * unit - low)
                for h in heads:
                    lse[t, h, :, at] = low[h : h + 1]
                    delta[t, h, :, at] = small[h : h + 1]
                    mixed[u][t, h * width : (h + 1) * width, :] = (
                        values[t, h, :, at].astype(F32) * part[h : h + 1]
                    ).astype(BF16)
    else:
        acc[...] = acc_in[...]
        lse[...] = lse_in[...]
        delta[...] = delta_in[...]

    def block(b, t, base, row, masked):
        scores = [dot_t(k_s[b], q_s[t, h]) for h in heads]
        dprobs = [dot_t(v_s[b], do_s[t, h]) for h in heads]
        if masked:
            allowed = allowed_of(sc, base, row)
            scores = [jnp.where(allowed, s, NEG) for s in scores]
        probs = [jnp.exp2(scores[h] * unit - lse[t, h]) for h in heads]
        dscores = [(probs[h] * (dprobs[h] - delta[t, h])).astype(BF16) for h in heads]
        lows = [p.astype(BF16) for p in probs]
        dk = sum(dot(dscores[h], q_s[t, h]) for h in heads)
        dv = sum(dot(lows[h], do_s[t, h]) for h in heads)
        accs = [acc[t, h] + dot(t_s[b], dscores[h]) for h in heads]
        for h in heads:
            acc[t, h] = accs[h]
        grads[:, :width] = grads[:, :width] + dk * scale
        grads[:, width:] = grads[:, width:] + dv

    def step(b, carry):
        grads[...] = jnp.zeros_like(grads)

        def tile(t, carry):
            base, row, needed, whole = place(sc, b, t)

            @pl.when(needed & whole)
            def _():
                block(b, t, base, row, False)

            @pl.when(needed & jnp.logical_not(whole))
            def _():
                block(b, t, base, row, True)

            return carry

        lax.fori_loop(0, TILES, tile, 0)
        dkv[b - 2 * span[0]] = grads[...].astype(BF16)
        return carry

    lax.fori_loop(2 * span[0], 2 * span[1], step, 0)
    if ends:
        for t in range(TILES):
            for h in heads:
                value = (acc[t, h] * scale).astype(BF16)
                for s in range(SLOTS):
                    dq[s][t, h * width : (h + 1) * width, :] = value[
                        :, s * CHUNK : (s + 1) * CHUNK
                    ]


def combine(group, width, *refs):
    for one, two, out in zip(refs[:2], refs[2:4], refs[4:]):
        for h in range(group):
            at = pl.ds(h * width, width)
            whole = one[at, :].astype(F32) + two[at, :].astype(F32)
            out[:, at] = jnp.transpose(whole).astype(BF16)


SMEM = pl.BlockSpec(memory_space=pltpu.SMEM)
VMEM = pl.BlockSpec(memory_space=pltpu.VMEM)
PARAMS = pltpu.CompilerParams(vmem_limit_bytes=20 * 1024 * 1024)


def cost(group, width, dots, pieces):
    work = TILES * ROWS * group * pieces * 2 * PAIR * width * 2
    return pl.CostEstimate(flops=2 * dots * work, bytes_accessed=1 << 23, transcendentals=0)


def state_shapes(group, width):
    acc = jax.ShapeDtypeStruct((TILES, group, width, ROWS), F32)
    line = jax.ShapeDtypeStruct((TILES, group, 1, ROWS), F32)
    return [acc, line, line]


def run_forward(group, width, sc, rows, keys):
    acc, line, _ = state_shapes(group, width)
    row = jax.ShapeDtypeStruct((TILES, group, ROWS, width), BF16)
    key = jax.ShapeDtypeStruct((2 * PIECES, PAIR, width), BF16)
    turned = jax.ShapeDtypeStruct((2 * PIECES, width, PAIR), BF16)
    stat = jax.ShapeDtypeStruct((TILES, 3 * group, ROWS), F32)
    return pl.pallas_call(
        functools.partial(forward, group, width),
        out_shape=[jax.ShapeDtypeStruct(acc.shape, BF16), stat, row, row, key, key, turned],
        in_specs=[SMEM] + [VMEM] * 10,
        out_specs=[VMEM] * 7,
        scratch_shapes=[pltpu.VMEM(turned.shape, BF16), pltpu.VMEM(acc.shape, F32)]
        + [pltpu.VMEM(line.shape, F32)] * 2,
        compiler_params=PARAMS,
        cost_estimate=cost(group, width, 3, PIECES),
        name="forward",
    )(sc, *rows, *keys)


def run_backward(group, width, span, begins, ends, sc, held, *more):
    pieces = span[1] - span[0]
    carried = state_shapes(group, width)
    piece = jax.ShapeDtypeStruct((TILES, group * width, CHUNK), BF16)
    shapes = [jax.ShapeDtypeStruct((2 * pieces, PAIR, 2 * width), BF16)]
    shapes = shapes + [piece] * (SLOTS * (begins + ends))
    spaces = [pltpu.VMEM((PAIR, 2 * width), F32)]
    if not ends:
        shapes = shapes + carried
    else:
        spaces = [pltpu.VMEM(s.shape, F32) for s in carried] + spaces
    return pl.pallas_call(
        functools.partial(backward, group, width, span, begins, ends),
        out_shape=shapes,
        in_specs=[SMEM] + [VMEM] * (len(held) + len(more)),
        out_specs=[VMEM] * len(shapes),
        scratch_shapes=spaces,
        compiler_params=PARAMS,
        cost_estimate=cost(group, width, 5, pieces),
        name="backward_begin" if begins else "backward_end" if ends else "backward_middle",
    )(sc, *held, *more)


def add(*parts):
    return sum(part.astype(F32) for part in parts).astype(BF16)


def local(query, key, value, dout, document):
    width = key.shape[1]
    group = query.shape[1] // width
    send = functools.partial(lax.ppermute, axis_name=AXES)
    qrow, kcol = lax.axis_index("qrow"), lax.axis_index("kcol")
    z, x_lo, x_hi, y = qrow // 2, qrow % 2, kcol // 4, kcol % 4

    row_home, key_home = pl.pallas_call(
        pack,
        out_shape=[
            jax.ShapeDtypeStruct((CHUNK, 2 * group * width), BF16),
            jax.ShapeDtypeStruct((CHUNK, 2 * width), BF16),
        ],
        name="pack",
    )(query, key, value, dout)
    row_other = send(row_home, perm=NEXT)
    a, b = send(key_home, perm=NEAR), send(key_home, perm=REST)
    row_other, a, b = lax.optimization_barrier((row_other, a, b))
    both = jnp.concatenate([row_home, row_other], axis=0)
    near, last = send(both, perm=Y[1]), send(both, perm=Y[3])
    held = jnp.concatenate([key_home, a, b, send(b, perm=NEAR)], axis=0)
    keys = [held] + [send(held, perm=X[n]) for n in range(1, 4)]
    far_own, far_other = send(last[:CHUNK], perm=Y[1]), send(near[CHUNK:], perm=Y[3])
    rows = [row_home, row_other, near, last, far_own, far_other]

    numbers = jnp.arange(DOCS, dtype=jnp.int32)
    starts = jnp.sum((document[None, :] < numbers[:, None]).astype(jnp.int32), axis=1)
    side = 2 - 4 * (z // 2 % 2)
    sources = jnp.stack([z, z + side, z - side, z + 4]) & 7
    sc = jnp.concatenate([jnp.stack([z, x_lo, x_hi, y]), starts, sources]).astype(jnp.int32)

    values, stat, *held = run_forward(group, width, sc, rows, keys)
    unit = LOG2E / math.sqrt(width)
    other = send(stat, perm=NEXT)[::-1]
    top = jnp.maximum(stat[:, :group], other[:, :group])
    mine, theirs = (jnp.exp2((s[:, :group] - top) * unit) for s in (stat, other))
    merged = jnp.concatenate(
        [top]
        + [
            stat[:, n * group : (n + 1) * group] * mine
            + other[:, n * group : (n + 1) * group] * theirs
            for n in (1, 2)
        ],
        axis=1,
    )
    stats = [merged] + [send(merged, perm=Y[s]) for s in range(1, SLOTS)]

    back = functools.partial(run_backward, group, width)
    out = back((3, 4), True, False, sc, held, *stats, stat, values)
    far, mixed, carried = out[0], out[1 : 1 + SLOTS], out[1 + SLOTS :]
    flat = (2 * PAIR, 2 * width)
    gc = send(far.reshape(flat), perm=OPPOSITE)
    mixed = [mixed[0]] + [send(mixed[s], perm=Y[s]) for s in range(1, SLOTS)]
    near_by, *carried = back((1, 3), False, False, sc, held, *carried)
    near_by, mixed, carried = lax.optimization_barrier((near_by, mixed, carried))
    ga = send(near_by[:2].reshape(flat), perm=NEAR)
    gb = send(near_by[2:].reshape(flat), perm=REST)
    close, *dq = back((0, 1), False, True, sc, held, *carried)
    dq = [dq[0]] + [send(dq[s], perm=Y[s]) for s in range(1, SLOTS)]
    grad = add(close.reshape(flat), ga, gb, gc)
    _, mixed, dq = lax.optimization_barrier((grad, mixed, dq))
    mixed = add(*mixed)
    mixed = [mixed[0], send(mixed[1], perm=NEXT)]
    grad = grad.reshape(4, CHUNK, 2 * width)
    grad = add(grad[0], *[send(grad[n], perm=X[n]) for n in range(1, 4)])
    dq = add(*dq)
    dq = [dq[0], send(dq[1], perm=NEXT)]
    out_shape = jax.ShapeDtypeStruct((CHUNK, group * width), BF16)
    attended, grad_query = pl.pallas_call(
        functools.partial(combine, group, width),
        out_shape=[out_shape, out_shape],
        in_specs=[VMEM] * 4,
        out_specs=[VMEM] * 2,
        compiler_params=PARAMS,
        name="combine",
    )(mixed[0], dq[0], mixed[1], dq[1])
    return attended, grad_query, grad[:, :width], grad[:, width:]


def solution(mesh):
    by_row = P(("qrow", "kcol"), "head")
    by_key = P(("kcol", "qrow"), "head")
    return jax.shard_map(
        local,
        mesh=mesh,
        in_specs=(by_row, by_key, by_key, by_row, P()),
        out_specs=(by_row, by_row, by_key, by_key),
        check_vma=False,
    )
```

```python
import functools
import math

import jax
import jax.numpy as jnp
from jax import lax
from jax.experimental import pallas as pl
from jax.experimental.pallas import tpu as pltpu
from jax.sharding import PartitionSpec as P

AXES = ("qrow", "kcol")
DEVICES = 128
CHUNK = 128
SLOTS = 4
TILES = 2
ROWS = SLOTS * CHUNK
PAIR = 2 * CHUNK
PIECES = 4
PLANE = 16 * CHUNK
DOCS = 8
NEG = -1e30
FLOOR = -1e29
SAFE = 60.0
LOG2E = math.log2(math.e)
F32 = jnp.float32
BF16 = jnp.bfloat16


def flip(mask):
    return [(d, d ^ mask) for d in range(DEVICES)]


Y = [flip(s) for s in range(SLOTS)]
X = [flip(m) for m in (0, 8, 4, 12)]
NEXT = flip(16)
NEAR = flip(32)
REST = [(d, (d + (32 if d // 32 % 2 else -32)) % DEVICES) for d in range(DEVICES)]

OPPOSITE = flip(64)


def dot(a, b):
    return lax.dot_general(a, b, (((1,), (0,)), ((), ())), preferred_element_type=F32)


def dot_t(a, b):
    return lax.dot_general(a, b, (((1,), (1,)), ((), ())), preferred_element_type=F32)


def fill(rows, keys, q_s, do_s, k_s, v_s, kt_s, vt_s, group, width):
    own, other, near, last, far_own, far_other = rows
    top, low = pl.ds(0, CHUNK), pl.ds(CHUNK, CHUNK)
    parts = [
        [(own, top), (near, top), (far_own, top), (last, top)],
        [(other, top), (near, low), (far_other, top), (last, low)],
    ]
    for t in range(TILES):
        for s in range(SLOTS):
            ref, at = parts[t][s]
            part, to = ref[at, :], pl.ds(s * CHUNK, CHUNK)
            for h in range(group):
                q_s[t, h, to, :] = part[:, h * width : (h + 1) * width]
                do_s[t, h, to, :] = part[:, (group + h) * width : (group + h + 1) * width]
    for piece in range(PIECES):
        for m, ref in enumerate(keys):
            part = ref[pl.ds(piece * CHUNK, CHUNK), :]
            block, at = 2 * piece + m // 2, pl.ds(m % 2 * CHUNK, CHUNK)
            k_s[block, at, :] = part[:, :width]
            v_s[block, at, :] = part[:, width:]
            kt_s[block, :, at] = jnp.transpose(part[:, :width])
            vt_s[block, :, at] = jnp.transpose(part[:, width:])


def start_of(sc, row):
    start = 0
    for n in range(DOCS):
        one = sc[4 + n]
        start = jnp.maximum(start, jnp.where(one <= row, one, 0))
    return start


def place(sc, block, t):
    z, x_lo, x_hi, y = (sc[n] for n in range(4))
    base = (4 * (x_hi ^ (block & 1)) + y) * PLANE + sc[4 + DOCS + block // 2] * PAIR
    row = ((z * 4 + x_lo * 2 + x_hi) ^ (4 * t)) * ROWS
    needed = (base <= row + ROWS - 1) & (base + PAIR - 1 >= start_of(sc, row))
    whole = (base + PAIR - 1 <= row) & (base >= start_of(sc, row + ROWS - 1))
    return base, row, needed, whole


def allowed_of(sc, base, row):
    key_at = base + (lax.broadcasted_iota(jnp.int32, (PAIR, 1), 0) ^ (sc[1] * CHUNK))
    row_at = row + (lax.broadcasted_iota(jnp.int32, (1, ROWS), 1) ^ (sc[3] * CHUNK))
    return (key_at >= start_of(sc, row_at)) & (key_at <= row_at)


def pack(query, key, value, dout, rows, keys):
    width = query.shape[1]
    rows[:, :width] = query[...]
    rows[:, width:] = dout[...]
    width = key.shape[1]
    keys[:, :width] = key[...]
    keys[:, width:] = value[...]


def forward(group, width, sc, *refs):
    rows, keys, refs = refs[:6], refs[6:10], refs[10:]
    values, stat, q_s, do_s, k_s, v_s, kt_s, t_s, acc, high, total = refs
    unit = LOG2E / math.sqrt(width)
    heads = range(group)
    fill(rows, keys, q_s, do_s, k_s, v_s, kt_s, t_s, group, width)
    acc[...] = jnp.zeros_like(acc)
    high[...] = jnp.full_like(high, FLOOR)
    total[...] = jnp.zeros_like(total)

    def widest(parts):
        ones = jnp.ones((width, width), BF16)
        return jnp.max(functools.reduce(jnp.maximum, [dot(p * p, ones) for p in parts]))

    rows_widest = widest([q_s[t, h] for t in range(TILES) for h in heads])
    keys_widest = widest([k_s[b] for b in range(2 * PIECES)])
    small = rows_widest * keys_widest * (unit * unit) <= SAFE * SAFE

    def scores_of(b, t, base, row, masked):
        scores = [dot_t(k_s[b], q_s[t, h]) for h in heads]
        if masked:
            allowed = allowed_of(sc, base, row)
            scores = [jnp.where(allowed, s, NEG) for s in scores]
        return scores

    def shifted(b, t, base, row, masked):
        scores = scores_of(b, t, base, row, masked)
        olds = [high[t, h] for h in heads]
        news = [jnp.maximum(o, jnp.max(s, axis=0, keepdims=True)) for o, s in zip(olds, scores)]
        shrinks = [jnp.exp2((o - n) * unit) for o, n in zip(olds, news)]
        es = [jnp.exp2(s * unit - n * unit) for s, n in zip(scores, news)]
        totals = [total[t, h] * shrinks[h] + jnp.sum(es[h], axis=0, keepdims=True) for h in heads]
        accs = [acc[t, h] * shrinks[h] + dot(t_s[b], es[h].astype(BF16)) for h in heads]
        for h in heads:
            high[t, h] = news[h]
            total[t, h] = totals[h]
            acc[t, h] = accs[h]

    def direct(b, t, base, row, masked):
        es = [jnp.exp2(s * unit) for s in scores_of(b, t, base, row, masked)]
        totals = [total[t, h] + jnp.sum(es[h], axis=0, keepdims=True) for h in heads]
        accs = [acc[t, h] + dot(t_s[b], es[h].astype(BF16)) for h in heads]
        for h in heads:
            total[t, h] = totals[h]
            acc[t, h] = accs[h]

    def over_blocks(block):
        def step(n, carry):
            b, t = n // 2, n & 1
            base, row, needed, whole = place(sc, b, t)

            @pl.when(needed & whole)
            def _():
                block(b, t, base, row, False)

            @pl.when(needed & jnp.logical_not(whole))
            def _():
                block(b, t, base, row, True)

            return carry

        lax.fori_loop(0, 4 * PIECES, step, 0)

    @pl.when(small)
    def _():
        over_blocks(direct)
        high[...] = jnp.where(total[...] > 0.0, 0.0, FLOOR)

    @pl.when(jnp.logical_not(small))
    def _():
        over_blocks(shifted)

    for t in range(TILES):
        for h in heads:
            product = acc[t, h] * jnp.transpose(do_s[t, h]).astype(F32)
            values[t, h] = (acc[t, h] * (1.0 / jnp.maximum(total[t, h], 1e-30))).astype(BF16)
            stat[t, h : h + 1, :] = high[t, h]
            stat[t, group + h : group + h + 1, :] = total[t, h]
            stat[t, 2 * group + h : 2 * group + h + 1, :] = jnp.sum(product, axis=0, keepdims=True)


def backward(group, width, span, begins, ends, sc, q_s, do_s, k_s, v_s, t_s, *refs):
    scale = 1.0 / math.sqrt(width)
    unit = LOG2E * scale
    heads = range(group)
    if begins:
        stats, own, values, refs = refs[:SLOTS], refs[SLOTS], refs[SLOTS + 1], refs[SLOTS + 2 :]
    else:
        acc_in, lse_in, delta_in, refs = *refs[:3], refs[3:]
    dkv, refs = refs[0], refs[1:]
    if begins:
        mixed, refs = refs[:SLOTS], refs[SLOTS:]
    if ends:
        dq, refs = refs[:SLOTS], refs[SLOTS:]
    acc, lse, delta, grads = refs
    if begins:
        acc[...] = jnp.zeros_like(acc)
        for t in range(TILES):
            for u in range(SLOTS):
                at = pl.ds(u * CHUNK, CHUNK)
                parts = [stats[s][t, :, pl.ds((u ^ s) * CHUNK, CHUNK)] for s in range(SLOTS)]
                top = functools.reduce(jnp.maximum, [p[:group] for p in parts])
                weights = [jnp.exp2((p[:group] - top) * unit) for p in parts]
                total = sum(w * p[group : 2 * group] for w, p in zip(weights, parts))
                product = sum(w * p[2 * group :] for w, p in zip(weights, parts))
                low, small = top * unit + jnp.log2(total), product / total
                part = own[t, group : 2 * group, at] * jnp.exp2(own[t, :group, at] * unit - low)
                for h in heads:
                    lse[t, h, :, at] = low[h : h + 1]
                    delta[t, h, :, at] = small[h : h + 1]
                    mixed[u][t, h * width : (h + 1) * width, :] = (
                        values[t, h, :, at].astype(F32) * part[h : h + 1]
                    ).astype(BF16)
    else:
        acc[...] = acc_in[...]
        lse[...] = lse_in[...]
        delta[...] = delta_in[...]

    def block(b, t, base, row, masked):
        scores = [dot_t(k_s[b], q_s[t, h]) for h in heads]
        dprobs = [dot_t(v_s[b], do_s[t, h]) for h in heads]
        if masked:
            allowed = allowed_of(sc, base, row)
            scores = [jnp.where(allowed, s, NEG) for s in scores]
        probs = [jnp.exp2(scores[h] * unit - lse[t, h]) for h in heads]
        dscores = [(probs[h] * (dprobs[h] - delta[t, h])).astype(BF16) for h in heads]
        lows = [p.astype(BF16) for p in probs]
        dk = sum(dot(dscores[h], q_s[t, h]) for h in heads)
        dv = sum(dot(lows[h], do_s[t, h]) for h in heads)
        accs = [acc[t, h] + dot(t_s[b], dscores[h]) for h in heads]
        for h in heads:
            acc[t, h] = accs[h]
        grads[:, :width] = grads[:, :width] + dk * scale
        grads[:, width:] = grads[:, width:] + dv

    def step(b, carry):
        grads[...] = jnp.zeros_like(grads)

        def tile(t, carry):
            base, row, needed, whole = place(sc, b, t)

            @pl.when(needed & whole)
            def _():
                block(b, t, base, row, False)

            @pl.when(needed & jnp.logical_not(whole))
            def _():
                block(b, t, base, row, True)

            return carry

        lax.fori_loop(0, TILES, tile, 0)
        dkv[b - 2 * span[0]] = grads[...].astype(BF16)
        return carry

    lax.fori_loop(2 * span[0], 2 * span[1], step, 0)
    if ends:
        for t in range(TILES):
            for h in heads:
                value = (acc[t, h] * scale).astype(BF16)
                for s in range(SLOTS):
                    dq[s][t, h * width : (h + 1) * width, :] = value[
                        :, s * CHUNK : (s + 1) * CHUNK
                    ]


def combine(group, width, *refs):
    for one, two, out in zip(refs[:2], refs[2:4], refs[4:]):
        for h in range(group):
            at = pl.ds(h * width, width)
            whole = one[at, :].astype(F32) + two[at, :].astype(F32)
            out[:, at] = jnp.transpose(whole).astype(BF16)


SMEM = pl.BlockSpec(memory_space=pltpu.SMEM)
VMEM = pl.BlockSpec(memory_space=pltpu.VMEM)
PARAMS = pltpu.CompilerParams(vmem_limit_bytes=20 * 1024 * 1024)


def cost(group, width, dots, pieces):
    work = TILES * ROWS * group * pieces * 2 * PAIR * width * 2
    return pl.CostEstimate(flops=2 * dots * work, bytes_accessed=1 << 23, transcendentals=0)


def state_shapes(group, width):
    acc = jax.ShapeDtypeStruct((TILES, group, width, ROWS), F32)
    line = jax.ShapeDtypeStruct((TILES, group, 1, ROWS), F32)
    return [acc, line, line]


def run_forward(group, width, sc, rows, keys):
    acc, line, _ = state_shapes(group, width)
    row = jax.ShapeDtypeStruct((TILES, group, ROWS, width), BF16)
    key = jax.ShapeDtypeStruct((2 * PIECES, PAIR, width), BF16)
    turned = jax.ShapeDtypeStruct((2 * PIECES, width, PAIR), BF16)
    stat = jax.ShapeDtypeStruct((TILES, 3 * group, ROWS), F32)
    return pl.pallas_call(
        functools.partial(forward, group, width),
        out_shape=[jax.ShapeDtypeStruct(acc.shape, BF16), stat, row, row, key, key, turned],
        in_specs=[SMEM] + [VMEM] * 10,
        out_specs=[VMEM] * 7,
        scratch_shapes=[pltpu.VMEM(turned.shape, BF16), pltpu.VMEM(acc.shape, F32)]
        + [pltpu.VMEM(line.shape, F32)] * 2,
        compiler_params=PARAMS,
        cost_estimate=cost(group, width, 3, PIECES),
        name="forward",
    )(sc, *rows, *keys)


def run_backward(group, width, span, begins, ends, sc, held, *more):
    pieces = span[1] - span[0]
    carried = state_shapes(group, width)
    piece = jax.ShapeDtypeStruct((TILES, group * width, CHUNK), BF16)
    shapes = [jax.ShapeDtypeStruct((2 * pieces, PAIR, 2 * width), BF16)]
    shapes = shapes + [piece] * (SLOTS * (begins + ends))
    spaces = [pltpu.VMEM((PAIR, 2 * width), F32)]
    if not ends:
        shapes = shapes + carried
    else:
        spaces = [pltpu.VMEM(s.shape, F32) for s in carried] + spaces
    return pl.pallas_call(
        functools.partial(backward, group, width, span, begins, ends),
        out_shape=shapes,
        in_specs=[SMEM] + [VMEM] * (len(held) + len(more)),
        out_specs=[VMEM] * len(shapes),
        scratch_shapes=spaces,
        compiler_params=PARAMS,
        cost_estimate=cost(group, width, 5, pieces),
        name="backward_begin" if begins else "backward_end" if ends else "backward_middle",
    )(sc, *held, *more)


def add(*parts):
    return sum(part.astype(F32) for part in parts).astype(BF16)


def local(query, key, value, dout, document):
    width = key.shape[1]
    group = query.shape[1] // width
    send = functools.partial(lax.ppermute, axis_name=AXES)
    qrow, kcol = lax.axis_index("qrow"), lax.axis_index("kcol")
    z, x_lo, x_hi, y = qrow // 2, qrow % 2, kcol // 4, kcol % 4

    row_home, key_home = pl.pallas_call(
        pack,
        out_shape=[
            jax.ShapeDtypeStruct((CHUNK, 2 * group * width), BF16),
            jax.ShapeDtypeStruct((CHUNK, 2 * width), BF16),
        ],
        name="pack",
    )(query, key, value, dout)
    row_other = send(row_home, perm=NEXT)
    a, b = send(key_home, perm=NEAR), send(key_home, perm=REST)
    row_other, a, b = lax.optimization_barrier((row_other, a, b))
    both = jnp.concatenate([row_home, row_other], axis=0)
    near, last = send(both, perm=Y[1]), send(both, perm=Y[3])
    held = jnp.concatenate([key_home, a, b, send(b, perm=NEAR)], axis=0)
    keys = [held] + [send(held, perm=X[n]) for n in range(1, 4)]
    far_own, far_other = send(last[:CHUNK], perm=Y[1]), send(near[CHUNK:], perm=Y[3])
    rows = [row_home, row_other, near, last, far_own, far_other]

    numbers = jnp.arange(DOCS, dtype=jnp.int32)
    starts = jnp.sum((document[None, :] < numbers[:, None]).astype(jnp.int32), axis=1)
    side = 2 - 4 * (z // 2 % 2)
    sources = jnp.stack([z, z + side, z - side, z + 4]) & 7
    sc = jnp.concatenate([jnp.stack([z, x_lo, x_hi, y]), starts, sources]).astype(jnp.int32)

    values, stat, *held = run_forward(group, width, sc, rows, keys)
    unit = LOG2E / math.sqrt(width)
    other = send(stat, perm=NEXT)[::-1]
    top = jnp.maximum(stat[:, :group], other[:, :group])
    mine, theirs = (jnp.exp2((s[:, :group] - top) * unit) for s in (stat, other))
    merged = jnp.concatenate(
        [top]
        + [
            stat[:, n * group : (n + 1) * group] * mine
            + other[:, n * group : (n + 1) * group] * theirs
            for n in (1, 2)
        ],
        axis=1,
    )
    stats = [merged] + [send(merged, perm=Y[s]) for s in range(1, SLOTS)]

    back = functools.partial(run_backward, group, width)
    out = back((3, 4), True, False, sc, held, *stats, stat, values)
    far, mixed, carried = out[0], out[1 : 1 + SLOTS], out[1 + SLOTS :]
    flat = (2 * PAIR, 2 * width)
    gc = send(far.reshape(flat), perm=OPPOSITE)
    mixed = [mixed[0]] + [send(mixed[s], perm=Y[s]) for s in range(1, SLOTS)]
    near_by, *carried = back((1, 3), False, False, sc, held, *carried)
    near_by, carried = lax.optimization_barrier((near_by, carried))
    ga = send(near_by[:2].reshape(flat), perm=NEAR)
    gb = send(near_by[2:].reshape(flat), perm=REST)
    close, *dq = back((0, 1), False, True, sc, held, *carried)
    close, dq, mixed = lax.optimization_barrier((close, dq, mixed))
    dq = [dq[0]] + [send(dq[s], perm=Y[s]) for s in range(1, SLOTS)]
    grad = add(close.reshape(flat), ga, gb, gc)
    _, mixed = lax.optimization_barrier((grad, mixed))
    grad = grad.reshape(4, CHUNK, 2 * width)
    grad = [grad[0]] + [send(grad[n], perm=X[n]) for n in range(1, 4)]
    mixed = add(*mixed)
    mixed = [mixed[0], send(mixed[1], perm=NEXT)]
    grad, dq = lax.optimization_barrier((grad, dq))
    grad, dq = add(*grad), add(*dq)
    dq = [dq[0], send(dq[1], perm=NEXT)]
    out_shape = jax.ShapeDtypeStruct((CHUNK, group * width), BF16)
    attended, grad_query = pl.pallas_call(
        functools.partial(combine, group, width),
        out_shape=[out_shape, out_shape],
        in_specs=[VMEM] * 4,
        out_specs=[VMEM] * 2,
        compiler_params=PARAMS,
        name="combine",
    )(mixed[0], dq[0], mixed[1], dq[1])
    return attended, grad_query, grad[:, :width], grad[:, width:]


def solution(mesh):
    by_row = P(("qrow", "kcol"), "head")
    by_key = P(("kcol", "qrow"), "head")
    return jax.shard_map(
        local,
        mesh=mesh,
        in_specs=(by_row, by_key, by_key, by_row, P()),
        out_specs=(by_row, by_row, by_key, by_key),
        check_vma=False,
    )
```

```python
import functools
import math

import jax
import jax.numpy as jnp
from jax import lax
from jax.experimental import pallas as pl
from jax.experimental.pallas import tpu as pltpu
from jax.sharding import PartitionSpec as P

AXES = ("qrow", "kcol")
DEVICES = 128
CHUNK = 128
SLOTS = 4
TILES = 2
ROWS = SLOTS * CHUNK
PAIR = 2 * CHUNK
PIECES = 4
PLANE = 16 * CHUNK
DOCS = 8
NEG = -1e30
FLOOR = -1e29
SAFE = 60.0
LOG2E = math.log2(math.e)
F32 = jnp.float32
BF16 = jnp.bfloat16


def flip(mask):
    return [(d, d ^ mask) for d in range(DEVICES)]


Y = [flip(s) for s in range(SLOTS)]
X = [flip(m) for m in (0, 8, 4, 12)]
NEXT = flip(16)
NEAR = flip(32)
REST = [(d, (d + (32 if d // 32 % 2 else -32)) % DEVICES) for d in range(DEVICES)]


def dot(a, b):
    return lax.dot_general(a, b, (((1,), (0,)), ((), ())), preferred_element_type=F32)


def dot_t(a, b):
    return lax.dot_general(a, b, (((1,), (1,)), ((), ())), preferred_element_type=F32)


def fill(rows, keys, q_s, do_s, k_s, v_s, kt_s, vt_s, group, width):
    own, other, near, last, far_own, far_other = rows
    top, low = pl.ds(0, CHUNK), pl.ds(CHUNK, CHUNK)
    parts = [
        [(own, top), (near, top), (far_own, top), (last, top)],
        [(other, top), (near, low), (far_other, top), (last, low)],
    ]
    for t in range(TILES):
        for s in range(SLOTS):
            ref, at = parts[t][s]
            part, to = ref[at, :], pl.ds(s * CHUNK, CHUNK)
            for h in range(group):
                q_s[t, h, to, :] = part[:, h * width : (h + 1) * width]
                do_s[t, h, to, :] = part[:, (group + h) * width : (group + h + 1) * width]
    for piece in range(PIECES):
        for m, ref in enumerate(keys):
            part = ref[pl.ds(piece * CHUNK, CHUNK), :]
            block, at = 2 * piece + m // 2, pl.ds(m % 2 * CHUNK, CHUNK)
            k_s[block, at, :] = part[:, :width]
            v_s[block, at, :] = part[:, width:]
            kt_s[block, :, at] = jnp.transpose(part[:, :width])
            vt_s[block, :, at] = jnp.transpose(part[:, width:])


def start_of(sc, row):
    start = 0
    for n in range(DOCS):
        one = sc[4 + n]
        start = jnp.maximum(start, jnp.where(one <= row, one, 0))
    return start


def place(sc, block, t):
    z, x_lo, x_hi, y = (sc[n] for n in range(4))
    base = (4 * (x_hi ^ (block & 1)) + y) * PLANE + sc[4 + DOCS + block // 2] * PAIR
    row = ((z * 4 + x_lo * 2 + x_hi) ^ (4 * t)) * ROWS
    needed = (base <= row + ROWS - 1) & (base + PAIR - 1 >= start_of(sc, row))
    whole = (base + PAIR - 1 <= row) & (base >= start_of(sc, row + ROWS - 1))
    return base, row, needed, whole


def allowed_of(sc, base, row):
    key_at = base + (lax.broadcasted_iota(jnp.int32, (PAIR, 1), 0) ^ (sc[1] * CHUNK))
    row_at = row + (lax.broadcasted_iota(jnp.int32, (1, ROWS), 1) ^ (sc[3] * CHUNK))
    return (key_at >= start_of(sc, row_at)) & (key_at <= row_at)


def pack(query, key, value, dout, rows, keys):
    width = query.shape[1]
    rows[:, :width] = query[...]
    rows[:, width:] = dout[...]
    width = key.shape[1]
    keys[:, :width] = key[...]
    keys[:, width:] = value[...]


def forward(group, width, sc, *refs):
    rows, keys, refs = refs[:6], refs[6:10], refs[10:]
    values, stat, q_s, do_s, k_s, v_s, kt_s, t_s, acc, high, total = refs
    unit = LOG2E / math.sqrt(width)
    heads = range(group)
    fill(rows, keys, q_s, do_s, k_s, v_s, kt_s, t_s, group, width)
    acc[...] = jnp.zeros_like(acc)
    high[...] = jnp.full_like(high, FLOOR)
    total[...] = jnp.zeros_like(total)

    def widest(parts):
        ones = jnp.ones((width, width), BF16)
        return jnp.max(functools.reduce(jnp.maximum, [dot(p * p, ones) for p in parts]))

    rows_widest = widest([q_s[t, h] for t in range(TILES) for h in heads])
    keys_widest = widest([k_s[b] for b in range(2 * PIECES)])
    small = rows_widest * keys_widest * (unit * unit) <= SAFE * SAFE

    def scores_of(b, t, base, row, masked):
        scores = [dot_t(k_s[b], q_s[t, h]) for h in heads]
        if masked:
            allowed = allowed_of(sc, base, row)
            scores = [jnp.where(allowed, s, NEG) for s in scores]
        return scores

    def shifted(b, t, base, row, masked):
        scores = scores_of(b, t, base, row, masked)
        olds = [high[t, h] for h in heads]
        news = [jnp.maximum(o, jnp.max(s, axis=0, keepdims=True)) for o, s in zip(olds, scores)]
        shrinks = [jnp.exp2((o - n) * unit) for o, n in zip(olds, news)]
        es = [jnp.exp2(s * unit - n * unit) for s, n in zip(scores, news)]
        totals = [total[t, h] * shrinks[h] + jnp.sum(es[h], axis=0, keepdims=True) for h in heads]
        accs = [acc[t, h] * shrinks[h] + dot(t_s[b], es[h].astype(BF16)) for h in heads]
        for h in heads:
            high[t, h] = news[h]
            total[t, h] = totals[h]
            acc[t, h] = accs[h]

    def direct(b, t, base, row, masked):
        es = [jnp.exp2(s * unit) for s in scores_of(b, t, base, row, masked)]
        totals = [total[t, h] + jnp.sum(es[h], axis=0, keepdims=True) for h in heads]
        accs = [acc[t, h] + dot(t_s[b], es[h].astype(BF16)) for h in heads]
        for h in heads:
            total[t, h] = totals[h]
            acc[t, h] = accs[h]

    def over_blocks(block):
        def step(n, carry):
            b, t = n // 2, n & 1
            base, row, needed, whole = place(sc, b, t)

            @pl.when(needed & whole)
            def _():
                block(b, t, base, row, False)

            @pl.when(needed & jnp.logical_not(whole))
            def _():
                block(b, t, base, row, True)

            return carry

        lax.fori_loop(0, 4 * PIECES, step, 0)

    @pl.when(small)
    def _():
        over_blocks(direct)
        high[...] = jnp.where(total[...] > 0.0, 0.0, FLOOR)

    @pl.when(jnp.logical_not(small))
    def _():
        over_blocks(shifted)

    for t in range(TILES):
        for h in heads:
            product = acc[t, h] * jnp.transpose(do_s[t, h]).astype(F32)
            values[t, h] = (acc[t, h] * (1.0 / jnp.maximum(total[t, h], 1e-30))).astype(BF16)
            stat[t, h : h + 1, :] = high[t, h]
            stat[t, group + h : group + h + 1, :] = total[t, h]
            stat[t, 2 * group + h : 2 * group + h + 1, :] = jnp.sum(product, axis=0, keepdims=True)


def backward(group, width, span, begins, ends, sc, q_s, do_s, k_s, v_s, t_s, *refs):
    scale = 1.0 / math.sqrt(width)
    unit = LOG2E * scale
    heads = range(group)
    if begins:
        stats, own, values, refs = refs[:SLOTS], refs[SLOTS], refs[SLOTS + 1], refs[SLOTS + 2 :]
    else:
        acc_in, lse_in, delta_in, refs = *refs[:3], refs[3:]
    dkv, refs = refs[0], refs[1:]
    if begins:
        mixed, refs = refs[:SLOTS], refs[SLOTS:]
    if ends:
        dq, refs = refs[:SLOTS], refs[SLOTS:]
    acc, lse, delta, grads = refs
    if begins:
        acc[...] = jnp.zeros_like(acc)
        for t in range(TILES):
            for u in range(SLOTS):
                at = pl.ds(u * CHUNK, CHUNK)
                parts = [stats[s][t, :, pl.ds((u ^ s) * CHUNK, CHUNK)] for s in range(SLOTS)]
                top = functools.reduce(jnp.maximum, [p[:group] for p in parts])
                weights = [jnp.exp2((p[:group] - top) * unit) for p in parts]
                total = sum(w * p[group : 2 * group] for w, p in zip(weights, parts))
                product = sum(w * p[2 * group :] for w, p in zip(weights, parts))
                low, small = top * unit + jnp.log2(total), product / total
                part = own[t, group : 2 * group, at] * jnp.exp2(own[t, :group, at] * unit - low)
                for h in heads:
                    lse[t, h, :, at] = low[h : h + 1]
                    delta[t, h, :, at] = small[h : h + 1]
                    mixed[u][t, h * width : (h + 1) * width, :] = (
                        values[t, h, :, at].astype(F32) * part[h : h + 1]
                    ).astype(BF16)
    else:
        acc[...] = acc_in[...]
        lse[...] = lse_in[...]
        delta[...] = delta_in[...]

    def block(b, t, base, row, masked):
        scores = [dot_t(k_s[b], q_s[t, h]) for h in heads]
        dprobs = [dot_t(v_s[b], do_s[t, h]) for h in heads]
        if masked:
            allowed = allowed_of(sc, base, row)
            scores = [jnp.where(allowed, s, NEG) for s in scores]
        probs = [jnp.exp2(scores[h] * unit - lse[t, h]) for h in heads]
        dscores = [(probs[h] * (dprobs[h] - delta[t, h])).astype(BF16) for h in heads]
        lows = [p.astype(BF16) for p in probs]
        dk = sum(dot(dscores[h], q_s[t, h]) for h in heads)
        dv = sum(dot(lows[h], do_s[t, h]) for h in heads)
        accs = [acc[t, h] + dot(t_s[b], dscores[h]) for h in heads]
        for h in heads:
            acc[t, h] = accs[h]
        grads[:, :width] = grads[:, :width] + dk * scale
        grads[:, width:] = grads[:, width:] + dv

    def step(b, carry):
        grads[...] = jnp.zeros_like(grads)

        def tile(t, carry):
            base, row, needed, whole = place(sc, b, t)

            @pl.when(needed & whole)
            def _():
                block(b, t, base, row, False)

            @pl.when(needed & jnp.logical_not(whole))
            def _():
                block(b, t, base, row, True)

            return carry

        lax.fori_loop(0, TILES, tile, 0)
        dkv[b - 2 * span[0]] = grads[...].astype(BF16)
        return carry

    lax.fori_loop(2 * span[0], 2 * span[1], step, 0)
    if ends:
        for t in range(TILES):
            for h in heads:
                value = (acc[t, h] * scale).astype(BF16)
                for s in range(SLOTS):
                    dq[s][t, h * width : (h + 1) * width, :] = value[
                        :, s * CHUNK : (s + 1) * CHUNK
                    ]


def combine(group, width, *refs):
    for one, two, out in zip(refs[:2], refs[2:4], refs[4:]):
        for h in range(group):
            at = pl.ds(h * width, width)
            whole = one[at, :].astype(F32) + two[at, :].astype(F32)
            out[:, at] = jnp.transpose(whole).astype(BF16)


SMEM = pl.BlockSpec(memory_space=pltpu.SMEM)
VMEM = pl.BlockSpec(memory_space=pltpu.VMEM)
PARAMS = pltpu.CompilerParams(vmem_limit_bytes=20 * 1024 * 1024)


def cost(group, width, dots, pieces):
    work = TILES * ROWS * group * pieces * 2 * PAIR * width * 2
    return pl.CostEstimate(flops=2 * dots * work, bytes_accessed=1 << 23, transcendentals=0)


def state_shapes(group, width):
    acc = jax.ShapeDtypeStruct((TILES, group, width, ROWS), F32)
    line = jax.ShapeDtypeStruct((TILES, group, 1, ROWS), F32)
    return [acc, line, line]


def run_forward(group, width, sc, rows, keys):
    acc, line, _ = state_shapes(group, width)
    row = jax.ShapeDtypeStruct((TILES, group, ROWS, width), BF16)
    key = jax.ShapeDtypeStruct((2 * PIECES, PAIR, width), BF16)
    turned = jax.ShapeDtypeStruct((2 * PIECES, width, PAIR), BF16)
    stat = jax.ShapeDtypeStruct((TILES, 3 * group, ROWS), F32)
    return pl.pallas_call(
        functools.partial(forward, group, width),
        out_shape=[jax.ShapeDtypeStruct(acc.shape, BF16), stat, row, row, key, key, turned],
        in_specs=[SMEM] + [VMEM] * 10,
        out_specs=[VMEM] * 7,
        scratch_shapes=[pltpu.VMEM(turned.shape, BF16), pltpu.VMEM(acc.shape, F32)]
        + [pltpu.VMEM(line.shape, F32)] * 2,
        compiler_params=PARAMS,
        cost_estimate=cost(group, width, 3, PIECES),
        name="forward",
    )(sc, *rows, *keys)


def run_backward(group, width, span, begins, ends, sc, held, *more):
    pieces = span[1] - span[0]
    carried = state_shapes(group, width)
    piece = jax.ShapeDtypeStruct((TILES, group * width, CHUNK), BF16)
    shapes = [jax.ShapeDtypeStruct((2 * pieces, PAIR, 2 * width), BF16)]
    shapes = shapes + [piece] * (SLOTS * (begins + ends))
    spaces = [pltpu.VMEM((PAIR, 2 * width), F32)]
    if not ends:
        shapes = shapes + carried
    else:
        spaces = [pltpu.VMEM(s.shape, F32) for s in carried] + spaces
    return pl.pallas_call(
        functools.partial(backward, group, width, span, begins, ends),
        out_shape=shapes,
        in_specs=[SMEM] + [VMEM] * (len(held) + len(more)),
        out_specs=[VMEM] * len(shapes),
        scratch_shapes=spaces,
        compiler_params=PARAMS,
        cost_estimate=cost(group, width, 5, pieces),
        name="backward_begin" if begins else "backward_end" if ends else "backward_middle",
    )(sc, *held, *more)


def add(*parts):
    return sum(part.astype(F32) for part in parts).astype(BF16)


def local(query, key, value, dout, document):
    width = key.shape[1]
    group = query.shape[1] // width
    send = functools.partial(lax.ppermute, axis_name=AXES)
    qrow, kcol = lax.axis_index("qrow"), lax.axis_index("kcol")
    z, x_lo, x_hi, y = qrow // 2, qrow % 2, kcol // 4, kcol % 4

    row_home, key_home = pl.pallas_call(
        pack,
        out_shape=[
            jax.ShapeDtypeStruct((CHUNK, 2 * group * width), BF16),
            jax.ShapeDtypeStruct((CHUNK, 2 * width), BF16),
        ],
        name="pack",
    )(query, key, value, dout)
    row_other = send(row_home, perm=NEXT)
    a, b = send(key_home, perm=NEAR), send(key_home, perm=REST)
    row_other, a, b = lax.optimization_barrier((row_other, a, b))
    both = jnp.concatenate([row_home, row_other], axis=0)
    near, last = send(both, perm=Y[1]), send(both, perm=Y[3])
    held = jnp.concatenate([key_home, a, b, send(b, perm=NEAR)], axis=0)
    keys = [held] + [send(held, perm=X[n]) for n in range(1, 4)]
    far_own, far_other = send(last[:CHUNK], perm=Y[1]), send(near[CHUNK:], perm=Y[3])
    rows = [row_home, row_other, near, last, far_own, far_other]

    numbers = jnp.arange(DOCS, dtype=jnp.int32)
    starts = jnp.sum((document[None, :] < numbers[:, None]).astype(jnp.int32), axis=1)
    side = 2 - 4 * (z // 2 % 2)
    sources = jnp.stack([z, z + side, z - side, z + 4]) & 7
    sc = jnp.concatenate([jnp.stack([z, x_lo, x_hi, y]), starts, sources]).astype(jnp.int32)

    values, stat, *held = run_forward(group, width, sc, rows, keys)
    unit = LOG2E / math.sqrt(width)
    other = send(stat, perm=NEXT)[::-1]
    top = jnp.maximum(stat[:, :group], other[:, :group])
    mine, theirs = (jnp.exp2((s[:, :group] - top) * unit) for s in (stat, other))
    merged = jnp.concatenate(
        [top]
        + [
            stat[:, n * group : (n + 1) * group] * mine
            + other[:, n * group : (n + 1) * group] * theirs
            for n in (1, 2)
        ],
        axis=1,
    )
    stats = [merged] + [send(merged, perm=Y[s]) for s in range(1, SLOTS)]

    back = functools.partial(run_backward, group, width)
    out = back((3, 4), True, False, sc, held, *stats, stat, values)
    far, mixed, carried = out[0], out[1 : 1 + SLOTS], out[1 + SLOTS :]
    flat = (2 * PAIR, 2 * width)
    one, two = send(far[0], perm=NEAR), send(far[1], perm=REST)
    mixed = [mixed[0]] + [send(mixed[s], perm=Y[s]) for s in range(1, SLOTS)]
    near_by, *carried = back((1, 3), False, False, sc, held, *carried)
    ga = jnp.concatenate([near_by[0], add(near_by[1], two)], axis=0)
    gb = jnp.concatenate([add(near_by[2], one), near_by[3]], axis=0)
    ga, gb, carried = lax.optimization_barrier((ga, gb, carried))
    ga, gb = send(ga, perm=NEAR), send(gb, perm=REST)
    close, *dq = back((0, 1), False, True, sc, held, *carried)
    close, dq, mixed = lax.optimization_barrier((close, dq, mixed))
    dq = [dq[0]] + [send(dq[s], perm=Y[s]) for s in (2, 1, 3)]
    grad = add(close.reshape(flat), ga, gb)
    _, mixed = lax.optimization_barrier((grad, mixed))
    grad = grad.reshape(4, CHUNK, 2 * width)
    grad = [grad[0]] + [send(grad[n], perm=X[n]) for n in range(1, 4)]
    mixed = add(*mixed)
    mixed = [mixed[0], send(mixed[1], perm=NEXT)]
    grad, dq = lax.optimization_barrier((grad, dq))
    grad, dq = add(*grad), add(*dq)
    dq = [dq[0], send(dq[1], perm=NEXT)]
    out_shape = jax.ShapeDtypeStruct((CHUNK, group * width), BF16)
    attended, grad_query = pl.pallas_call(
        functools.partial(combine, group, width),
        out_shape=[out_shape, out_shape],
        in_specs=[VMEM] * 4,
        out_specs=[VMEM] * 2,
        compiler_params=PARAMS,
        name="combine",
    )(mixed[0], dq[0], mixed[1], dq[1])
    return attended, grad_query, grad[:, :width], grad[:, width:]


def solution(mesh):
    by_row = P(("qrow", "kcol"), "head")
    by_key = P(("kcol", "qrow"), "head")
    return jax.shard_map(
        local,
        mesh=mesh,
        in_specs=(by_row, by_key, by_key, by_row, P()),
        out_specs=(by_row, by_row, by_key, by_key),
        check_vma=False,
    )
```

```python
import functools
import math

import jax
import jax.numpy as jnp
from jax import lax
from jax.experimental import pallas as pl
from jax.experimental.pallas import tpu as pltpu
from jax.sharding import PartitionSpec as P

AXES = ("qrow", "kcol")
DEVICES = 128
CHUNK = 128
SLOTS = 4
TILES = 2
ROWS = SLOTS * CHUNK
PAIR = 2 * CHUNK
PIECES = 4
PLANE = 16 * CHUNK
DOCS = 8
NEG = -1e30
FLOOR = -1e29
SAFE = 60.0
LOG2E = math.log2(math.e)
F32 = jnp.float32
BF16 = jnp.bfloat16


def flip(mask):
    return [(d, d ^ mask) for d in range(DEVICES)]


Y = [flip(s) for s in range(SLOTS)]
X = [flip(m) for m in (0, 8, 4, 12)]
NEXT = flip(16)
NEAR = flip(32)
REST = [(d, (d + (32 if d // 32 % 2 else -32)) % DEVICES) for d in range(DEVICES)]


def dot(a, b):
    return lax.dot_general(a, b, (((1,), (0,)), ((), ())), preferred_element_type=F32)


def dot_t(a, b):
    return lax.dot_general(a, b, (((1,), (1,)), ((), ())), preferred_element_type=F32)


def fill(rows, keys, q_s, do_s, k_s, v_s, kt_s, vt_s, group, width):
    own, other, near, last, far_own, far_other = rows
    top, low = pl.ds(0, CHUNK), pl.ds(CHUNK, CHUNK)
    parts = [
        [(own, top), (near, top), (far_own, top), (last, top)],
        [(other, top), (near, low), (far_other, top), (last, low)],
    ]
    for t in range(TILES):
        for s in range(SLOTS):
            ref, at = parts[t][s]
            part, to = ref[at, :], pl.ds(s * CHUNK, CHUNK)
            for h in range(group):
                q_s[t, h, to, :] = part[:, h * width : (h + 1) * width]
                do_s[t, h, to, :] = part[:, (group + h) * width : (group + h + 1) * width]
    for piece in range(PIECES):
        for m, ref in enumerate(keys):
            part = ref[pl.ds(piece * CHUNK, CHUNK), :]
            block, at = 2 * piece + m // 2, pl.ds(m % 2 * CHUNK, CHUNK)
            k_s[block, at, :] = part[:, :width]
            v_s[block, at, :] = part[:, width:]
            kt_s[block, :, at] = jnp.transpose(part[:, :width])
            vt_s[block, :, at] = jnp.transpose(part[:, width:])


def start_of(sc, row):
    start = 0
    for n in range(DOCS):
        one = sc[4 + n]
        start = jnp.maximum(start, jnp.where(one <= row, one, 0))
    return start


def place(sc, block, t):
    z, x_lo, x_hi, y = (sc[n] for n in range(4))
    base = (4 * (x_hi ^ (block & 1)) + y) * PLANE + sc[4 + DOCS + block // 2] * PAIR
    row = ((z * 4 + x_lo * 2 + x_hi) ^ (4 * t)) * ROWS
    needed = (base <= row + ROWS - 1) & (base + PAIR - 1 >= start_of(sc, row))
    whole = (base + PAIR - 1 <= row) & (base >= start_of(sc, row + ROWS - 1))
    return base, row, needed, whole


def allowed_of(sc, base, row):
    key_at = base + (lax.broadcasted_iota(jnp.int32, (PAIR, 1), 0) ^ (sc[1] * CHUNK))
    row_at = row + (lax.broadcasted_iota(jnp.int32, (1, ROWS), 1) ^ (sc[3] * CHUNK))
    return (key_at >= start_of(sc, row_at)) & (key_at <= row_at)


def pack(query, key, value, dout, rows, keys):
    width = query.shape[1]
    rows[:, :width] = query[...]
    rows[:, width:] = dout[...]
    width = key.shape[1]
    keys[:, :width] = key[...]
    keys[:, width:] = value[...]


def forward(group, width, sc, *refs):
    rows, keys, refs = refs[:6], refs[6:10], refs[10:]
    values, stat, q_s, do_s, k_s, v_s, kt_s, t_s, acc, high, total = refs
    unit = LOG2E / math.sqrt(width)
    heads = range(group)
    fill(rows, keys, q_s, do_s, k_s, v_s, kt_s, t_s, group, width)
    acc[...] = jnp.zeros_like(acc)
    high[...] = jnp.full_like(high, FLOOR)
    total[...] = jnp.zeros_like(total)

    def widest(parts):
        ones = jnp.ones((width, width), BF16)
        return jnp.max(functools.reduce(jnp.maximum, [dot(p * p, ones) for p in parts]))

    rows_widest = widest([q_s[t, h] for t in range(TILES) for h in heads])
    keys_widest = widest([k_s[b] for b in range(2 * PIECES)])
    small = rows_widest * keys_widest * (unit * unit) <= SAFE * SAFE

    def scores_of(b, t, base, row, masked):
        scores = [dot_t(k_s[b], q_s[t, h]) for h in heads]
        if masked:
            allowed = allowed_of(sc, base, row)
            scores = [jnp.where(allowed, s, NEG) for s in scores]
        return scores

    def shifted(b, t, base, row, masked):
        scores = scores_of(b, t, base, row, masked)
        olds = [high[t, h] for h in heads]
        news = [jnp.maximum(o, jnp.max(s, axis=0, keepdims=True)) for o, s in zip(olds, scores)]
        shrinks = [jnp.exp2((o - n) * unit) for o, n in zip(olds, news)]
        es = [jnp.exp2(s * unit - n * unit) for s, n in zip(scores, news)]
        totals = [total[t, h] * shrinks[h] + jnp.sum(es[h], axis=0, keepdims=True) for h in heads]
        accs = [acc[t, h] * shrinks[h] + dot(t_s[b], es[h].astype(BF16)) for h in heads]
        for h in heads:
            high[t, h] = news[h]
            total[t, h] = totals[h]
            acc[t, h] = accs[h]

    def direct(b, t, base, row, masked):
        es = [jnp.exp2(s * unit) for s in scores_of(b, t, base, row, masked)]
        totals = [total[t, h] + jnp.sum(es[h], axis=0, keepdims=True) for h in heads]
        accs = [acc[t, h] + dot(t_s[b], es[h].astype(BF16)) for h in heads]
        for h in heads:
            total[t, h] = totals[h]
            acc[t, h] = accs[h]

    def over_blocks(block):
        def step(n, carry):
            b, t = n // 2, n & 1
            base, row, needed, whole = place(sc, b, t)

            @pl.when(needed & whole)
            def _():
                block(b, t, base, row, False)

            @pl.when(needed & jnp.logical_not(whole))
            def _():
                block(b, t, base, row, True)

            return carry

        lax.fori_loop(0, 4 * PIECES, step, 0)

    @pl.when(small)
    def _():
        over_blocks(direct)
        high[...] = jnp.where(total[...] > 0.0, 0.0, FLOOR)

    @pl.when(jnp.logical_not(small))
    def _():
        over_blocks(shifted)

    for t in range(TILES):
        for h in heads:
            product = acc[t, h] * jnp.transpose(do_s[t, h]).astype(F32)
            values[t, h] = (acc[t, h] * (1.0 / jnp.maximum(total[t, h], 1e-30))).astype(BF16)
            stat[t, h : h + 1, :] = high[t, h]
            stat[t, group + h : group + h + 1, :] = total[t, h]
            stat[t, 2 * group + h : 2 * group + h + 1, :] = jnp.sum(product, axis=0, keepdims=True)


def backward(group, width, span, begins, ends, sc, q_s, do_s, k_s, v_s, t_s, *refs):
    scale = 1.0 / math.sqrt(width)
    unit = LOG2E * scale
    heads = range(group)
    if begins:
        stats, own, values, refs = refs[:SLOTS], refs[SLOTS], refs[SLOTS + 1], refs[SLOTS + 2 :]
    else:
        acc_in, lse_in, delta_in, refs = *refs[:3], refs[3:]
    dkv, refs = refs[0], refs[1:]
    if begins:
        mixed, refs = refs[:SLOTS], refs[SLOTS:]
    if ends:
        dq, refs = refs[:SLOTS], refs[SLOTS:]
    acc, lse, delta, grads = refs
    if begins:
        acc[...] = jnp.zeros_like(acc)
        for t in range(TILES):
            for u in range(SLOTS):
                at = pl.ds(u * CHUNK, CHUNK)
                parts = [stats[s][t, :, pl.ds((u ^ s) * CHUNK, CHUNK)] for s in range(SLOTS)]
                top = functools.reduce(jnp.maximum, [p[:group] for p in parts])
                weights = [jnp.exp2((p[:group] - top) * unit) for p in parts]
                total = sum(w * p[group : 2 * group] for w, p in zip(weights, parts))
                product = sum(w * p[2 * group :] for w, p in zip(weights, parts))
                low, small = top * unit + jnp.log2(total), product / total
                part = own[t, group : 2 * group, at] * jnp.exp2(own[t, :group, at] * unit - low)
                for h in heads:
                    lse[t, h, :, at] = low[h : h + 1]
                    delta[t, h, :, at] = small[h : h + 1]
                    mixed[u][t, h * width : (h + 1) * width, :] = (
                        values[t, h, :, at].astype(F32) * part[h : h + 1]
                    ).astype(BF16)
    else:
        acc[...] = acc_in[...]
        lse[...] = lse_in[...]
        delta[...] = delta_in[...]

    def block(b, t, base, row, masked):
        scores = [dot_t(k_s[b], q_s[t, h]) for h in heads]
        dprobs = [dot_t(v_s[b], do_s[t, h]) for h in heads]
        if masked:
            allowed = allowed_of(sc, base, row)
            scores = [jnp.where(allowed, s, NEG) for s in scores]
        probs = [jnp.exp2(scores[h] * unit - lse[t, h]) for h in heads]
        dscores = [(probs[h] * (dprobs[h] - delta[t, h])).astype(BF16) for h in heads]
        lows = [p.astype(BF16) for p in probs]
        dk = sum(dot(dscores[h], q_s[t, h]) for h in heads)
        dv = sum(dot(lows[h], do_s[t, h]) for h in heads)
        accs = [acc[t, h] + dot(t_s[b], dscores[h]) for h in heads]
        for h in heads:
            acc[t, h] = accs[h]
        grads[:, :width] = grads[:, :width] + dk * scale
        grads[:, width:] = grads[:, width:] + dv

    def step(b, carry):
        grads[...] = jnp.zeros_like(grads)

        def tile(t, carry):
            base, row, needed, whole = place(sc, b, t)

            @pl.when(needed & whole)
            def _():
                block(b, t, base, row, False)

            @pl.when(needed & jnp.logical_not(whole))
            def _():
                block(b, t, base, row, True)

            return carry

        lax.fori_loop(0, TILES, tile, 0)
        dkv[b - 2 * span[0]] = grads[...].astype(BF16)
        return carry

    lax.fori_loop(2 * span[0], 2 * span[1], step, 0)
    if ends:
        for t in range(TILES):
            for h in heads:
                value = (acc[t, h] * scale).astype(BF16)
                for s in range(SLOTS):
                    dq[s][t, h * width : (h + 1) * width, :] = value[
                        :, s * CHUNK : (s + 1) * CHUNK
                    ]


def combine(group, width, *refs):
    for one, two, out in zip(refs[:2], refs[2:4], refs[4:]):
        for h in range(group):
            at = pl.ds(h * width, width)
            whole = one[at, :].astype(F32) + two[at, :].astype(F32)
            out[:, at] = jnp.transpose(whole).astype(BF16)


SMEM = pl.BlockSpec(memory_space=pltpu.SMEM)
VMEM = pl.BlockSpec(memory_space=pltpu.VMEM)
PARAMS = pltpu.CompilerParams(vmem_limit_bytes=20 * 1024 * 1024)


def cost(group, width, dots, pieces):
    work = TILES * ROWS * group * pieces * 2 * PAIR * width * 2
    return pl.CostEstimate(flops=2 * dots * work, bytes_accessed=1 << 23, transcendentals=0)


def state_shapes(group, width):
    acc = jax.ShapeDtypeStruct((TILES, group, width, ROWS), F32)
    line = jax.ShapeDtypeStruct((TILES, group, 1, ROWS), F32)
    return [acc, line, line]


def run_forward(group, width, sc, rows, keys):
    acc, line, _ = state_shapes(group, width)
    row = jax.ShapeDtypeStruct((TILES, group, ROWS, width), BF16)
    key = jax.ShapeDtypeStruct((2 * PIECES, PAIR, width), BF16)
    turned = jax.ShapeDtypeStruct((2 * PIECES, width, PAIR), BF16)
    stat = jax.ShapeDtypeStruct((TILES, 3 * group, ROWS), F32)
    return pl.pallas_call(
        functools.partial(forward, group, width),
        out_shape=[jax.ShapeDtypeStruct(acc.shape, BF16), stat, row, row, key, key, turned],
        in_specs=[SMEM] + [VMEM] * 10,
        out_specs=[VMEM] * 7,
        scratch_shapes=[pltpu.VMEM(turned.shape, BF16), pltpu.VMEM(acc.shape, F32)]
        + [pltpu.VMEM(line.shape, F32)] * 2,
        compiler_params=PARAMS,
        cost_estimate=cost(group, width, 3, PIECES),
        name="forward",
    )(sc, *rows, *keys)


def run_backward(group, width, span, begins, ends, sc, held, *more):
    pieces = span[1] - span[0]
    carried = state_shapes(group, width)
    piece = jax.ShapeDtypeStruct((TILES, group * width, CHUNK), BF16)
    shapes = [jax.ShapeDtypeStruct((2 * pieces, PAIR, 2 * width), BF16)]
    shapes = shapes + [piece] * (SLOTS * (begins + ends))
    spaces = [pltpu.VMEM((PAIR, 2 * width), F32)]
    if not ends:
        shapes = shapes + carried
    else:
        spaces = [pltpu.VMEM(s.shape, F32) for s in carried] + spaces
    return pl.pallas_call(
        functools.partial(backward, group, width, span, begins, ends),
        out_shape=shapes,
        in_specs=[SMEM] + [VMEM] * (len(held) + len(more)),
        out_specs=[VMEM] * len(shapes),
        scratch_shapes=spaces,
        compiler_params=PARAMS,
        cost_estimate=cost(group, width, 5, pieces),
        name="backward_begin" if begins else "backward_end" if ends else "backward_middle",
    )(sc, *held, *more)


def add(*parts):
    return sum(part.astype(F32) for part in parts).astype(BF16)


def local(query, key, value, dout, document):
    width = key.shape[1]
    group = query.shape[1] // width
    send = functools.partial(lax.ppermute, axis_name=AXES)
    qrow, kcol = lax.axis_index("qrow"), lax.axis_index("kcol")
    z, x_lo, x_hi, y = qrow // 2, qrow % 2, kcol // 4, kcol % 4

    row_home, key_home = pl.pallas_call(
        pack,
        out_shape=[
            jax.ShapeDtypeStruct((CHUNK, 2 * group * width), BF16),
            jax.ShapeDtypeStruct((CHUNK, 2 * width), BF16),
        ],
        name="pack",
    )(query, key, value, dout)
    row_other = send(row_home, perm=NEXT)
    a, b = send(key_home, perm=NEAR), send(key_home, perm=REST)
    row_other, a = lax.optimization_barrier((row_other, a))
    both = jnp.concatenate([row_home, row_other], axis=0)
    near, last = send(both, perm=Y[1]), send(both, perm=Y[3])
    held = jnp.concatenate([key_home, a, b, send(a, perm=REST)], axis=0)
    keys = [held] + [send(held, perm=X[n]) for n in range(1, 4)]
    far_own, far_other = send(last[:CHUNK], perm=Y[1]), send(near[CHUNK:], perm=Y[3])
    rows = [row_home, row_other, near, last, far_own, far_other]

    numbers = jnp.arange(DOCS, dtype=jnp.int32)
    starts = jnp.sum((document[None, :] < numbers[:, None]).astype(jnp.int32), axis=1)
    side = 2 - 4 * (z // 2 % 2)
    sources = jnp.stack([z, z + side, z - side, z + 4]) & 7
    sc = jnp.concatenate([jnp.stack([z, x_lo, x_hi, y]), starts, sources]).astype(jnp.int32)

    values, stat, *held = run_forward(group, width, sc, rows, keys)
    unit = LOG2E / math.sqrt(width)
    other = send(stat, perm=NEXT)[::-1]
    top = jnp.maximum(stat[:, :group], other[:, :group])
    mine, theirs = (jnp.exp2((s[:, :group] - top) * unit) for s in (stat, other))
    merged = jnp.concatenate(
        [top]
        + [
            stat[:, n * group : (n + 1) * group] * mine
            + other[:, n * group : (n + 1) * group] * theirs
            for n in (1, 2)
        ],
        axis=1,
    )
    stats = [merged] + [send(merged, perm=Y[s]) for s in range(1, SLOTS)]

    back = functools.partial(run_backward, group, width)
    out = back((3, 4), True, False, sc, held, *stats, stat, values)
    far, mixed, carried = out[0], out[1 : 1 + SLOTS], out[1 + SLOTS :]
    flat = (2 * PAIR, 2 * width)
    one, two = send(far[0], perm=NEAR), send(far[1], perm=REST)
    mixed = [mixed[0]] + [send(mixed[s], perm=Y[s]) for s in range(1, SLOTS)]
    near_by, *carried = back((1, 3), False, False, sc, held, *carried)
    ga = jnp.concatenate([near_by[0], add(near_by[1], two)], axis=0)
    gb = jnp.concatenate([add(near_by[2], one), near_by[3]], axis=0)
    ga, gb, carried = lax.optimization_barrier((ga, gb, carried))
    ga, gb = send(ga, perm=NEAR), send(gb, perm=REST)
    close, *dq = back((0, 1), False, True, sc, held, *carried)
    close, dq, mixed = lax.optimization_barrier((close, dq, mixed))
    dq = [dq[0]] + [send(dq[s], perm=Y[s]) for s in (2, 1, 3)]
    grad = add(close.reshape(flat), ga, gb)
    _, mixed = lax.optimization_barrier((grad, mixed))
    grad = grad.reshape(4, CHUNK, 2 * width)
    grad = [grad[0]] + [send(grad[n], perm=X[n]) for n in range(1, 4)]
    mixed = add(*mixed)
    mixed = [mixed[0], send(mixed[1], perm=NEXT)]
    grad, dq = lax.optimization_barrier((grad, dq))
    grad, dq = add(*grad), add(*dq)
    dq = [dq[0], send(dq[1], perm=NEXT)]
    out_shape = jax.ShapeDtypeStruct((CHUNK, group * width), BF16)
    attended, grad_query = pl.pallas_call(
        functools.partial(combine, group, width),
        out_shape=[out_shape, out_shape],
        in_specs=[VMEM] * 4,
        out_specs=[VMEM] * 2,
        compiler_params=PARAMS,
        name="combine",
    )(mixed[0], dq[0], mixed[1], dq[1])
    return attended, grad_query, grad[:, :width], grad[:, width:]


def solution(mesh):
    by_row = P(("qrow", "kcol"), "head")
    by_key = P(("kcol", "qrow"), "head")
    return jax.shard_map(
        local,
        mesh=mesh,
        in_specs=(by_row, by_key, by_key, by_row, P()),
        out_specs=(by_row, by_row, by_key, by_key),
        check_vma=False,
    )
```

```python
import functools
import math

import jax
import jax.numpy as jnp
from jax import lax
from jax.experimental import pallas as pl
from jax.experimental.pallas import tpu as pltpu
from jax.sharding import PartitionSpec as P

AXES = ("qrow", "kcol")
DEVICES = 128
CHUNK = 128
SLOTS = 4
TILES = 2
ROWS = SLOTS * CHUNK
PAIR = 2 * CHUNK
PIECES = 4
PLANE = 16 * CHUNK
DOCS = 8
NEG = -1e30
FLOOR = -1e29
SAFE = 60.0
LOG2E = math.log2(math.e)
F32 = jnp.float32
BF16 = jnp.bfloat16


def flip(mask):
    return [(d, d ^ mask) for d in range(DEVICES)]


Y = [flip(s) for s in range(SLOTS)]
X = [flip(m) for m in (0, 8, 4, 12)]
NEXT = flip(16)
NEAR = flip(32)
REST = [(d, (d + (32 if d // 32 % 2 else -32)) % DEVICES) for d in range(DEVICES)]


def dot(a, b):
    return lax.dot_general(a, b, (((1,), (0,)), ((), ())), preferred_element_type=F32)


def dot_t(a, b):
    return lax.dot_general(a, b, (((1,), (1,)), ((), ())), preferred_element_type=F32)


def fill(rows, keys, q_s, do_s, k_s, v_s, kt_s, vt_s, group, width):
    own, other, near, last, far_own, far_other = rows
    top, low = pl.ds(0, CHUNK), pl.ds(CHUNK, CHUNK)
    parts = [
        [(own, top), (near, top), (far_own, top), (last, top)],
        [(other, top), (near, low), (far_other, top), (last, low)],
    ]
    for t in range(TILES):
        for s in range(SLOTS):
            ref, at = parts[t][s]
            part, to = ref[at, :], pl.ds(s * CHUNK, CHUNK)
            for h in range(group):
                q_s[t, h, to, :] = part[:, h * width : (h + 1) * width]
                do_s[t, h, to, :] = part[:, (group + h) * width : (group + h + 1) * width]
    for piece in range(PIECES):
        for m, ref in enumerate(keys):
            part = ref[pl.ds(piece * CHUNK, CHUNK), :]
            block, at = 2 * piece + m // 2, pl.ds(m % 2 * CHUNK, CHUNK)
            k_s[block, at, :] = part[:, :width]
            v_s[block, at, :] = part[:, width:]
            kt_s[block, :, at] = jnp.transpose(part[:, :width])
            vt_s[block, :, at] = jnp.transpose(part[:, width:])


def start_of(sc, row):
    start = 0
    for n in range(DOCS):
        one = sc[4 + n]
        start = jnp.maximum(start, jnp.where(one <= row, one, 0))
    return start


def place(sc, block, t):
    z, x_lo, x_hi, y = (sc[n] for n in range(4))
    base = (4 * (x_hi ^ (block & 1)) + y) * PLANE + sc[4 + DOCS + block // 2] * PAIR
    row = ((z * 4 + x_lo * 2 + x_hi) ^ (4 * t)) * ROWS
    needed = (base <= row + ROWS - 1) & (base + PAIR - 1 >= start_of(sc, row))
    whole = (base + PAIR - 1 <= row) & (base >= start_of(sc, row + ROWS - 1))
    return base, row, needed, whole


def allowed_of(sc, base, row):
    key_at = base + (lax.broadcasted_iota(jnp.int32, (PAIR, 1), 0) ^ (sc[1] * CHUNK))
    row_at = row + (lax.broadcasted_iota(jnp.int32, (1, ROWS), 1) ^ (sc[3] * CHUNK))
    return (key_at >= start_of(sc, row_at)) & (key_at <= row_at)


def pack(query, key, value, dout, rows, keys):
    width = query.shape[1]
    rows[:, :width] = query[...]
    rows[:, width:] = dout[...]
    width = key.shape[1]
    keys[:, :width] = key[...]
    keys[:, width:] = value[...]


def forward(group, width, sc, *refs):
    rows, keys, refs = refs[:6], refs[6:10], refs[10:]
    values, stat, q_s, do_s, k_s, v_s, kt_s, t_s, acc, high, total = refs
    unit = LOG2E / math.sqrt(width)
    heads = range(group)
    fill(rows, keys, q_s, do_s, k_s, v_s, kt_s, t_s, group, width)
    acc[...] = jnp.zeros_like(acc)
    high[...] = jnp.full_like(high, FLOOR)
    total[...] = jnp.zeros_like(total)

    def widest(parts):
        ones = jnp.ones((width, width), BF16)
        return jnp.max(functools.reduce(jnp.maximum, [dot(p * p, ones) for p in parts]))

    rows_widest = widest([q_s[t, h] for t in range(TILES) for h in heads])
    keys_widest = widest([k_s[b] for b in range(2 * PIECES)])
    small = rows_widest * keys_widest * (unit * unit) <= SAFE * SAFE

    def scores_of(b, t, base, row, masked):
        scores = [dot_t(k_s[b], q_s[t, h]) for h in heads]
        if masked:
            allowed = allowed_of(sc, base, row)
            scores = [jnp.where(allowed, s, NEG) for s in scores]
        return scores

    def shifted(b, t, base, row, masked):
        scores = scores_of(b, t, base, row, masked)
        olds = [high[t, h] for h in heads]
        news = [jnp.maximum(o, jnp.max(s, axis=0, keepdims=True)) for o, s in zip(olds, scores)]
        shrinks = [jnp.exp2((o - n) * unit) for o, n in zip(olds, news)]
        es = [jnp.exp2(s * unit - n * unit) for s, n in zip(scores, news)]
        totals = [total[t, h] * shrinks[h] + jnp.sum(es[h], axis=0, keepdims=True) for h in heads]
        accs = [acc[t, h] * shrinks[h] + dot(t_s[b], es[h].astype(BF16)) for h in heads]
        for h in heads:
            high[t, h] = news[h]
            total[t, h] = totals[h]
            acc[t, h] = accs[h]

    def direct(b, t, base, row, masked):
        es = [jnp.exp2(s * unit) for s in scores_of(b, t, base, row, masked)]
        totals = [total[t, h] + jnp.sum(es[h], axis=0, keepdims=True) for h in heads]
        accs = [acc[t, h] + dot(t_s[b], es[h].astype(BF16)) for h in heads]
        for h in heads:
            total[t, h] = totals[h]
            acc[t, h] = accs[h]

    def over_blocks(block):
        def step(n, carry):
            b, t = n // 2, n & 1
            base, row, needed, whole = place(sc, b, t)

            @pl.when(needed & whole)
            def _():
                block(b, t, base, row, False)

            @pl.when(needed & jnp.logical_not(whole))
            def _():
                block(b, t, base, row, True)

            return carry

        lax.fori_loop(0, 4 * PIECES, step, 0)

    @pl.when(small)
    def _():
        over_blocks(direct)
        high[...] = jnp.where(total[...] > 0.0, 0.0, FLOOR)

    @pl.when(jnp.logical_not(small))
    def _():
        over_blocks(shifted)

    for t in range(TILES):
        for h in heads:
            product = acc[t, h] * jnp.transpose(do_s[t, h]).astype(F32)
            values[t, h] = (acc[t, h] * (1.0 / jnp.maximum(total[t, h], 1e-30))).astype(BF16)
            stat[t, h : h + 1, :] = high[t, h]
            stat[t, group + h : group + h + 1, :] = total[t, h]
            stat[t, 2 * group + h : 2 * group + h + 1, :] = jnp.sum(product, axis=0, keepdims=True)


def backward(group, width, span, begins, ends, sc, q_s, do_s, k_s, v_s, t_s, *refs):
    scale = 1.0 / math.sqrt(width)
    unit = LOG2E * scale
    heads = range(group)
    if begins:
        stats, own, values, refs = refs[:SLOTS], refs[SLOTS], refs[SLOTS + 1], refs[SLOTS + 2 :]
    else:
        acc_in, lse_in, delta_in, refs = *refs[:3], refs[3:]
    dkv, refs = refs[0], refs[1:]
    if begins:
        mixed, refs = refs[:SLOTS], refs[SLOTS:]
    if ends:
        dq, refs = refs[:SLOTS], refs[SLOTS:]
    acc, lse, delta, grads = refs
    if begins:
        acc[...] = jnp.zeros_like(acc)
        for t in range(TILES):
            for u in range(SLOTS):
                at = pl.ds(u * CHUNK, CHUNK)
                parts = [stats[s][t, :, pl.ds((u ^ s) * CHUNK, CHUNK)] for s in range(SLOTS)]
                top = functools.reduce(jnp.maximum, [p[:group] for p in parts])
                weights = [jnp.exp2((p[:group] - top) * unit) for p in parts]
                total = sum(w * p[group : 2 * group] for w, p in zip(weights, parts))
                product = sum(w * p[2 * group :] for w, p in zip(weights, parts))
                low, small = top * unit + jnp.log2(total), product / total
                part = own[t, group : 2 * group, at] * jnp.exp2(own[t, :group, at] * unit - low)
                for h in heads:
                    lse[t, h, :, at] = low[h : h + 1]
                    delta[t, h, :, at] = small[h : h + 1]
                    mixed[u][t, h * width : (h + 1) * width, :] = (
                        values[t, h, :, at].astype(F32) * part[h : h + 1]
                    ).astype(BF16)
    else:
        acc[...] = acc_in[...]
        lse[...] = lse_in[...]
        delta[...] = delta_in[...]

    def block(b, t, base, row, masked):
        scores = [dot_t(k_s[b], q_s[t, h]) for h in heads]
        dprobs = [dot_t(v_s[b], do_s[t, h]) for h in heads]
        if masked:
            allowed = allowed_of(sc, base, row)
            scores = [jnp.where(allowed, s, NEG) for s in scores]
        probs = [jnp.exp2(scores[h] * unit - lse[t, h]) for h in heads]
        dscores = [(probs[h] * (dprobs[h] - delta[t, h])).astype(BF16) for h in heads]
        lows = [p.astype(BF16) for p in probs]
        dk = sum(dot(dscores[h], q_s[t, h]) for h in heads)
        dv = sum(dot(lows[h], do_s[t, h]) for h in heads)
        accs = [acc[t, h] + dot(t_s[b], dscores[h]) for h in heads]
        for h in heads:
            acc[t, h] = accs[h]
        grads[:, :width] = grads[:, :width] + dk * scale
        grads[:, width:] = grads[:, width:] + dv

    def step(b, carry):
        grads[...] = jnp.zeros_like(grads)

        def tile(t, carry):
            base, row, needed, whole = place(sc, b, t)

            @pl.when(needed & whole)
            def _():
                block(b, t, base, row, False)

            @pl.when(needed & jnp.logical_not(whole))
            def _():
                block(b, t, base, row, True)

            return carry

        lax.fori_loop(0, TILES, tile, 0)
        dkv[b - 2 * span[0]] = grads[...].astype(BF16)
        return carry

    lax.fori_loop(2 * span[0], 2 * span[1], step, 0)
    if ends:
        for t in range(TILES):
            for h in heads:
                value = (acc[t, h] * scale).astype(BF16)
                for s in range(SLOTS):
                    dq[s][t, h * width : (h + 1) * width, :] = value[
                        :, s * CHUNK : (s + 1) * CHUNK
                    ]


def combine(group, width, *refs):
    for one, two, out in zip(refs[:2], refs[2:4], refs[4:]):
        for h in range(group):
            at = pl.ds(h * width, width)
            whole = one[at, :].astype(F32) + two[at, :].astype(F32)
            out[:, at] = jnp.transpose(whole).astype(BF16)


SMEM = pl.BlockSpec(memory_space=pltpu.SMEM)
VMEM = pl.BlockSpec(memory_space=pltpu.VMEM)
PARAMS = pltpu.CompilerParams(vmem_limit_bytes=20 * 1024 * 1024)


def cost(group, width, dots, pieces):
    work = TILES * ROWS * group * pieces * 2 * PAIR * width * 2
    return pl.CostEstimate(flops=2 * dots * work, bytes_accessed=1 << 23, transcendentals=0)


def state_shapes(group, width):
    acc = jax.ShapeDtypeStruct((TILES, group, width, ROWS), F32)
    line = jax.ShapeDtypeStruct((TILES, group, 1, ROWS), F32)
    return [acc, line, line]


def run_forward(group, width, sc, rows, keys):
    acc, line, _ = state_shapes(group, width)
    row = jax.ShapeDtypeStruct((TILES, group, ROWS, width), BF16)
    key = jax.ShapeDtypeStruct((2 * PIECES, PAIR, width), BF16)
    turned = jax.ShapeDtypeStruct((2 * PIECES, width, PAIR), BF16)
    stat = jax.ShapeDtypeStruct((TILES, 3 * group, ROWS), F32)
    return pl.pallas_call(
        functools.partial(forward, group, width),
        out_shape=[jax.ShapeDtypeStruct(acc.shape, BF16), stat, row, row, key, key, turned],
        in_specs=[SMEM] + [VMEM] * 10,
        out_specs=[VMEM] * 7,
        scratch_shapes=[pltpu.VMEM(turned.shape, BF16), pltpu.VMEM(acc.shape, F32)]
        + [pltpu.VMEM(line.shape, F32)] * 2,
        compiler_params=PARAMS,
        cost_estimate=cost(group, width, 3, PIECES),
        name="forward",
    )(sc, *rows, *keys)


def run_backward(group, width, span, begins, ends, sc, held, *more):
    pieces = span[1] - span[0]
    carried = state_shapes(group, width)
    piece = jax.ShapeDtypeStruct((TILES, group * width, CHUNK), BF16)
    shapes = [jax.ShapeDtypeStruct((2 * pieces, PAIR, 2 * width), BF16)]
    shapes = shapes + [piece] * (SLOTS * (begins + ends))
    spaces = [pltpu.VMEM((PAIR, 2 * width), F32)]
    if not ends:
        shapes = shapes + carried
    else:
        spaces = [pltpu.VMEM(s.shape, F32) for s in carried] + spaces
    return pl.pallas_call(
        functools.partial(backward, group, width, span, begins, ends),
        out_shape=shapes,
        in_specs=[SMEM] + [VMEM] * (len(held) + len(more)),
        out_specs=[VMEM] * len(shapes),
        scratch_shapes=spaces,
        compiler_params=PARAMS,
        cost_estimate=cost(group, width, 5, pieces),
        name="backward_begin" if begins else "backward_end" if ends else "backward_middle",
    )(sc, *held, *more)


def add(*parts):
    return sum(part.astype(F32) for part in parts).astype(BF16)


def local(query, key, value, dout, document):
    width = key.shape[1]
    group = query.shape[1] // width
    send = functools.partial(lax.ppermute, axis_name=AXES)
    qrow, kcol = lax.axis_index("qrow"), lax.axis_index("kcol")
    z, x_lo, x_hi, y = qrow // 2, qrow % 2, kcol // 4, kcol % 4

    row_home, key_home = pl.pallas_call(
        pack,
        out_shape=[
            jax.ShapeDtypeStruct((CHUNK, 2 * group * width), BF16),
            jax.ShapeDtypeStruct((CHUNK, 2 * width), BF16),
        ],
        name="pack",
    )(query, key, value, dout)
    row_other = send(row_home, perm=NEXT)
    a, b = send(key_home, perm=NEAR), send(key_home, perm=REST)
    row_other, a, b = lax.optimization_barrier((row_other, a, b))
    both = jnp.concatenate([row_home, row_other], axis=0)
    near, last = send(both, perm=Y[1]), send(both, perm=Y[3])
    held = jnp.concatenate([key_home, a, b, send(a, perm=REST)], axis=0)
    keys = [held] + [send(held, perm=X[n]) for n in range(1, 4)]
    far_own, far_other = send(last[:CHUNK], perm=Y[1]), send(near[CHUNK:], perm=Y[3])
    rows = [row_home, row_other, near, last, far_own, far_other]

    numbers = jnp.arange(DOCS, dtype=jnp.int32)
    starts = jnp.sum((document[None, :] < numbers[:, None]).astype(jnp.int32), axis=1)
    side = 2 - 4 * (z // 2 % 2)
    sources = jnp.stack([z, z + side, z - side, z + 4]) & 7
    sc = jnp.concatenate([jnp.stack([z, x_lo, x_hi, y]), starts, sources]).astype(jnp.int32)

    values, stat, *held = run_forward(group, width, sc, rows, keys)
    unit = LOG2E / math.sqrt(width)
    other = send(stat, perm=NEXT)[::-1]
    top = jnp.maximum(stat[:, :group], other[:, :group])
    mine, theirs = (jnp.exp2((s[:, :group] - top) * unit) for s in (stat, other))
    merged = jnp.concatenate(
        [top]
        + [
            stat[:, n * group : (n + 1) * group] * mine
            + other[:, n * group : (n + 1) * group] * theirs
            for n in (1, 2)
        ],
        axis=1,
    )
    stats = [merged] + [send(merged, perm=Y[s]) for s in range(1, SLOTS)]

    back = functools.partial(run_backward, group, width)
    out = back((3, 4), True, False, sc, held, *stats, stat, values)
    far, mixed, carried = out[0], out[1 : 1 + SLOTS], out[1 + SLOTS :]
    flat = (2 * PAIR, 2 * width)
    one, two = send(far[0], perm=NEAR), send(far[1], perm=REST)
    mixed = [mixed[0]] + [send(mixed[s], perm=Y[s]) for s in range(1, SLOTS)]
    near_by, *carried = back((1, 3), False, False, sc, held, *carried)
    ga = jnp.concatenate([near_by[0], add(near_by[1], two)], axis=0)
    gb = jnp.concatenate([add(near_by[2], one), near_by[3]], axis=0)
    ga, gb, carried = lax.optimization_barrier((ga, gb, carried))
    ga, gb = send(ga, perm=NEAR), send(gb, perm=REST)
    close, *dq = back((0, 1), False, True, sc, held, *carried)
    close, dq, mixed = lax.optimization_barrier((close, dq, mixed))
    dq = [dq[0]] + [send(dq[s], perm=Y[s]) for s in (2, 1, 3)]
    grad = add(close.reshape(flat), ga, gb)
    _, mixed = lax.optimization_barrier((grad, mixed))
    grad = grad.reshape(4, CHUNK, 2 * width)
    grad = [grad[0]] + [send(grad[n], perm=X[n]) for n in range(1, 4)]
    mixed = [add(*[part[t] for part in mixed]) for t in range(TILES)]
    mixed = [mixed[0], send(mixed[1], perm=NEXT)]
    grad, dq = lax.optimization_barrier((grad, dq))
    dq = [add(*[part[t] for part in dq]) for t in range(TILES)]
    dq = [dq[0], send(dq[1], perm=NEXT)]
    grad = add(*grad)
    out_shape = jax.ShapeDtypeStruct((CHUNK, group * width), BF16)
    attended, grad_query = pl.pallas_call(
        functools.partial(combine, group, width),
        out_shape=[out_shape, out_shape],
        in_specs=[VMEM] * 4,
        out_specs=[VMEM] * 2,
        compiler_params=PARAMS,
        name="combine",
    )(mixed[0], dq[0], mixed[1], dq[1])
    return attended, grad_query, grad[:, :width], grad[:, width:]


def solution(mesh):
    by_row = P(("qrow", "kcol"), "head")
    by_key = P(("kcol", "qrow"), "head")
    return jax.shard_map(
        local,
        mesh=mesh,
        in_specs=(by_row, by_key, by_key, by_row, P()),
        out_specs=(by_row, by_row, by_key, by_key),
        check_vma=False,
    )
```

```python
import functools
import math

import jax
import jax.numpy as jnp
from jax import lax
from jax.experimental import pallas as pl
from jax.experimental.pallas import tpu as pltpu
from jax.sharding import PartitionSpec as P

AXES = ("qrow", "kcol")
DEVICES = 128
CHUNK = 128
SLOTS = 4
TILES = 2
ROWS = SLOTS * CHUNK
PAIR = 2 * CHUNK
PIECES = 4
PLANE = 16 * CHUNK
DOCS = 8
NEG = -1e30
FLOOR = -1e29
SAFE = 60.0
LOG2E = math.log2(math.e)
F32 = jnp.float32
BF16 = jnp.bfloat16


def flip(mask):
    return [(d, d ^ mask) for d in range(DEVICES)]


Y = [flip(s) for s in range(SLOTS)]
X = [flip(m) for m in (0, 8, 4, 12)]
NEXT = flip(16)
NEAR = flip(32)
REST = [(d, (d + (32 if d // 32 % 2 else -32)) % DEVICES) for d in range(DEVICES)]


def dot(a, b):
    return lax.dot_general(a, b, (((1,), (0,)), ((), ())), preferred_element_type=F32)


def dot_t(a, b):
    return lax.dot_general(a, b, (((1,), (1,)), ((), ())), preferred_element_type=F32)


def fill(rows, keys, q_s, do_s, k_s, v_s, kt_s, vt_s, group, width):
    own, other, near, last, far_own, far_other = rows
    top, low = pl.ds(0, CHUNK), pl.ds(CHUNK, CHUNK)
    parts = [
        [(own, top), (near, top), (far_own, top), (last, top)],
        [(other, top), (near, low), (far_other, top), (last, low)],
    ]
    for t in range(TILES):
        for s in range(SLOTS):
            ref, at = parts[t][s]
            part, to = ref[at, :], pl.ds(s * CHUNK, CHUNK)
            for h in range(group):
                q_s[t, h, to, :] = part[:, h * width : (h + 1) * width]
                do_s[t, h, to, :] = part[:, (group + h) * width : (group + h + 1) * width]
    for piece in range(PIECES):
        for m, ref in enumerate(keys):
            part = ref[pl.ds(piece * CHUNK, CHUNK), :]
            block, at = 2 * piece + m // 2, pl.ds(m % 2 * CHUNK, CHUNK)
            k_s[block, at, :] = part[:, :width]
            v_s[block, at, :] = part[:, width:]
            kt_s[block, :, at] = jnp.transpose(part[:, :width])
            vt_s[block, :, at] = jnp.transpose(part[:, width:])


def start_of(sc, row):
    start = 0
    for n in range(DOCS):
        one = sc[4 + n]
        start = jnp.maximum(start, jnp.where(one <= row, one, 0))
    return start


def place(sc, block, t):
    z, x_lo, x_hi, y = (sc[n] for n in range(4))
    base = (4 * (x_hi ^ (block & 1)) + y) * PLANE + sc[4 + DOCS + block // 2] * PAIR
    row = ((z * 4 + x_lo * 2 + x_hi) ^ (4 * t)) * ROWS
    needed = (base <= row + ROWS - 1) & (base + PAIR - 1 >= start_of(sc, row))
    whole = (base + PAIR - 1 <= row) & (base >= start_of(sc, row + ROWS - 1))
    return base, row, needed, whole


def allowed_of(sc, base, row):
    key_at = base + (lax.broadcasted_iota(jnp.int32, (PAIR, 1), 0) ^ (sc[1] * CHUNK))
    row_at = row + (lax.broadcasted_iota(jnp.int32, (1, ROWS), 1) ^ (sc[3] * CHUNK))
    return (key_at >= start_of(sc, row_at)) & (key_at <= row_at)


def pack(query, key, value, dout, rows, keys):
    width = query.shape[1]
    rows[:, :width] = query[...]
    rows[:, width:] = dout[...]
    width = key.shape[1]
    keys[:, :width] = key[...]
    keys[:, width:] = value[...]


def forward(group, width, sc, *refs):
    rows, keys, refs = refs[:6], refs[6:10], refs[10:]
    values, stat, q_s, do_s, k_s, v_s, kt_s, t_s, acc, high, total = refs
    unit = LOG2E / math.sqrt(width)
    heads = range(group)
    fill(rows, keys, q_s, do_s, k_s, v_s, kt_s, t_s, group, width)
    acc[...] = jnp.zeros_like(acc)
    high[...] = jnp.full_like(high, FLOOR)
    total[...] = jnp.zeros_like(total)

    def widest(parts):
        ones = jnp.ones((width, width), BF16)
        return jnp.max(functools.reduce(jnp.maximum, [dot(p * p, ones) for p in parts]))

    rows_widest = widest([q_s[t, h] for t in range(TILES) for h in heads])
    keys_widest = widest([k_s[b] for b in range(2 * PIECES)])
    small = rows_widest * keys_widest * (unit * unit) <= SAFE * SAFE

    def scores_of(b, t, base, row, masked):
        scores = [dot_t(k_s[b], q_s[t, h]) for h in heads]
        if masked:
            allowed = allowed_of(sc, base, row)
            scores = [jnp.where(allowed, s, NEG) for s in scores]
        return scores

    def shifted(b, t, base, row, masked):
        scores = scores_of(b, t, base, row, masked)
        olds = [high[t, h] for h in heads]
        news = [jnp.maximum(o, jnp.max(s, axis=0, keepdims=True)) for o, s in zip(olds, scores)]
        shrinks = [jnp.exp2((o - n) * unit) for o, n in zip(olds, news)]
        es = [jnp.exp2(s * unit - n * unit) for s, n in zip(scores, news)]
        totals = [total[t, h] * shrinks[h] + jnp.sum(es[h], axis=0, keepdims=True) for h in heads]
        accs = [acc[t, h] * shrinks[h] + dot(t_s[b], es[h].astype(BF16)) for h in heads]
        for h in heads:
            high[t, h] = news[h]
            total[t, h] = totals[h]
            acc[t, h] = accs[h]

    def direct(b, t, base, row, masked):
        es = [jnp.exp2(s * unit) for s in scores_of(b, t, base, row, masked)]
        totals = [total[t, h] + jnp.sum(es[h], axis=0, keepdims=True) for h in heads]
        accs = [acc[t, h] + dot(t_s[b], es[h].astype(BF16)) for h in heads]
        for h in heads:
            total[t, h] = totals[h]
            acc[t, h] = accs[h]

    def over_blocks(block):
        def step(n, carry):
            b, t = n // 2, n & 1
            base, row, needed, whole = place(sc, b, t)

            @pl.when(needed & whole)
            def _():
                block(b, t, base, row, False)

            @pl.when(needed & jnp.logical_not(whole))
            def _():
                block(b, t, base, row, True)

            return carry

        lax.fori_loop(0, 4 * PIECES, step, 0)

    @pl.when(small)
    def _():
        over_blocks(direct)
        high[...] = jnp.where(total[...] > 0.0, 0.0, FLOOR)

    @pl.when(jnp.logical_not(small))
    def _():
        over_blocks(shifted)

    for t in range(TILES):
        for h in heads:
            product = acc[t, h] * jnp.transpose(do_s[t, h]).astype(F32)
            values[t, h] = (acc[t, h] * (1.0 / jnp.maximum(total[t, h], 1e-30))).astype(BF16)
            stat[t, h : h + 1, :] = high[t, h]
            stat[t, group + h : group + h + 1, :] = total[t, h]
            stat[t, 2 * group + h : 2 * group + h + 1, :] = jnp.sum(product, axis=0, keepdims=True)


def backward(group, width, span, begins, ends, sc, q_s, do_s, k_s, v_s, t_s, *refs):
    scale = 1.0 / math.sqrt(width)
    unit = LOG2E * scale
    heads = range(group)
    if begins:
        stats, own, values, refs = refs[:SLOTS], refs[SLOTS], refs[SLOTS + 1], refs[SLOTS + 2 :]
    else:
        acc_in, lse_in, delta_in, refs = *refs[:3], refs[3:]
    dkv, refs = refs[0], refs[1:]
    if begins:
        mixed, refs = refs[:SLOTS], refs[SLOTS:]
    if ends:
        dq, refs = refs[:SLOTS], refs[SLOTS:]
    acc, lse, delta, grads = refs
    if begins:
        acc[...] = jnp.zeros_like(acc)
        for t in range(TILES):
            for u in range(SLOTS):
                at = pl.ds(u * CHUNK, CHUNK)
                parts = [stats[s][t, :, pl.ds((u ^ s) * CHUNK, CHUNK)] for s in range(SLOTS)]
                top = functools.reduce(jnp.maximum, [p[:group] for p in parts])
                weights = [jnp.exp2((p[:group] - top) * unit) for p in parts]
                total = sum(w * p[group : 2 * group] for w, p in zip(weights, parts))
                product = sum(w * p[2 * group :] for w, p in zip(weights, parts))
                low, small = top * unit + jnp.log2(total), product / total
                part = own[t, group : 2 * group, at] * jnp.exp2(own[t, :group, at] * unit - low)
                for h in heads:
                    lse[t, h, :, at] = low[h : h + 1]
                    delta[t, h, :, at] = small[h : h + 1]
                    mixed[u][t, h * width : (h + 1) * width, :] = (
                        values[t, h, :, at].astype(F32) * part[h : h + 1]
                    ).astype(BF16)
    else:
        acc[...] = acc_in[...]
        lse[...] = lse_in[...]
        delta[...] = delta_in[...]

    def block(b, t, base, row, masked):
        scores = [dot_t(k_s[b], q_s[t, h]) for h in heads]
        dprobs = [dot_t(v_s[b], do_s[t, h]) for h in heads]
        if masked:
            allowed = allowed_of(sc, base, row)
            scores = [jnp.where(allowed, s, NEG) for s in scores]
        probs = [jnp.exp2(scores[h] * unit - lse[t, h]) for h in heads]
        dscores = [(probs[h] * (dprobs[h] - delta[t, h])).astype(BF16) for h in heads]
        lows = [p.astype(BF16) for p in probs]
        dk = sum(dot(dscores[h], q_s[t, h]) for h in heads)
        dv = sum(dot(lows[h], do_s[t, h]) for h in heads)
        accs = [acc[t, h] + dot(t_s[b], dscores[h]) for h in heads]
        for h in heads:
            acc[t, h] = accs[h]
        grads[:, :width] = grads[:, :width] + dk * scale
        grads[:, width:] = grads[:, width:] + dv

    def step(b, carry):
        grads[...] = jnp.zeros_like(grads)

        def tile(t, carry):
            base, row, needed, whole = place(sc, b, t)

            @pl.when(needed & whole)
            def _():
                block(b, t, base, row, False)

            @pl.when(needed & jnp.logical_not(whole))
            def _():
                block(b, t, base, row, True)

            return carry

        lax.fori_loop(0, TILES, tile, 0)
        dkv[b - 2 * span[0]] = grads[...].astype(BF16)
        return carry

    lax.fori_loop(2 * span[0], 2 * span[1], step, 0)
    if ends:
        for t in range(TILES):
            for h in heads:
                value = (acc[t, h] * scale).astype(BF16)
                for s in range(SLOTS):
                    dq[s][t, h * width : (h + 1) * width, :] = value[
                        :, s * CHUNK : (s + 1) * CHUNK
                    ]


def combine(group, width, *refs):
    for one, two, out in zip(refs[:2], refs[2:4], refs[4:]):
        for h in range(group):
            at = pl.ds(h * width, width)
            whole = one[at, :].astype(F32) + two[at, :].astype(F32)
            out[:, at] = jnp.transpose(whole).astype(BF16)


SMEM = pl.BlockSpec(memory_space=pltpu.SMEM)
VMEM = pl.BlockSpec(memory_space=pltpu.VMEM)
PARAMS = pltpu.CompilerParams(vmem_limit_bytes=20 * 1024 * 1024)


def cost(group, width, dots, pieces):
    work = TILES * ROWS * group * pieces * 2 * PAIR * width * 2
    return pl.CostEstimate(flops=2 * dots * work, bytes_accessed=1 << 23, transcendentals=0)


def state_shapes(group, width):
    acc = jax.ShapeDtypeStruct((TILES, group, width, ROWS), F32)
    line = jax.ShapeDtypeStruct((TILES, group, 1, ROWS), F32)
    return [acc, line, line]


def run_forward(group, width, sc, rows, keys):
    acc, line, _ = state_shapes(group, width)
    row = jax.ShapeDtypeStruct((TILES, group, ROWS, width), BF16)
    key = jax.ShapeDtypeStruct((2 * PIECES, PAIR, width), BF16)
    turned = jax.ShapeDtypeStruct((2 * PIECES, width, PAIR), BF16)
    stat = jax.ShapeDtypeStruct((TILES, 3 * group, ROWS), F32)
    return pl.pallas_call(
        functools.partial(forward, group, width),
        out_shape=[jax.ShapeDtypeStruct(acc.shape, BF16), stat, row, row, key, key, turned],
        in_specs=[SMEM] + [VMEM] * 10,
        out_specs=[VMEM] * 7,
        scratch_shapes=[pltpu.VMEM(turned.shape, BF16), pltpu.VMEM(acc.shape, F32)]
        + [pltpu.VMEM(line.shape, F32)] * 2,
        compiler_params=PARAMS,
        cost_estimate=cost(group, width, 3, PIECES),
        name="forward",
    )(sc, *rows, *keys)


def run_backward(group, width, span, begins, ends, sc, held, *more):
    pieces = span[1] - span[0]
    carried = state_shapes(group, width)
    piece = jax.ShapeDtypeStruct((TILES, group * width, CHUNK), BF16)
    shapes = [jax.ShapeDtypeStruct((2 * pieces, PAIR, 2 * width), BF16)]
    shapes = shapes + [piece] * (SLOTS * (begins + ends))
    spaces = [pltpu.VMEM((PAIR, 2 * width), F32)]
    if not ends:
        shapes = shapes + carried
    else:
        spaces = [pltpu.VMEM(s.shape, F32) for s in carried] + spaces
    return pl.pallas_call(
        functools.partial(backward, group, width, span, begins, ends),
        out_shape=shapes,
        in_specs=[SMEM] + [VMEM] * (len(held) + len(more)),
        out_specs=[VMEM] * len(shapes),
        scratch_shapes=spaces,
        compiler_params=PARAMS,
        cost_estimate=cost(group, width, 5, pieces),
        name="backward_begin" if begins else "backward_end" if ends else "backward_middle",
    )(sc, *held, *more)


def add(*parts):
    return sum(part.astype(F32) for part in parts).astype(BF16)


def local(query, key, value, dout, document):
    width = key.shape[1]
    group = query.shape[1] // width
    send = functools.partial(lax.ppermute, axis_name=AXES)
    qrow, kcol = lax.axis_index("qrow"), lax.axis_index("kcol")
    z, x_lo, x_hi, y = qrow // 2, qrow % 2, kcol // 4, kcol % 4

    row_home, key_home = pl.pallas_call(
        pack,
        out_shape=[
            jax.ShapeDtypeStruct((CHUNK, 2 * group * width), BF16),
            jax.ShapeDtypeStruct((CHUNK, 2 * width), BF16),
        ],
        name="pack",
    )(query, key, value, dout)
    row_other = send(row_home, perm=NEXT)
    a, b = send(key_home, perm=NEAR), send(key_home, perm=REST)
    row_other, a, b = lax.optimization_barrier((row_other, a, b))
    both = jnp.concatenate([row_home, row_other], axis=0)
    near, last = send(both, perm=Y[1]), send(both, perm=Y[3])
    held = jnp.concatenate([key_home, a, b, send(a, perm=REST)], axis=0)
    keys = [held] + [send(held, perm=X[n]) for n in range(1, 4)]
    far_own, far_other = send(last[:CHUNK], perm=Y[1]), send(near[CHUNK:], perm=Y[3])
    rows = [row_home, row_other, near, last, far_own, far_other]

    numbers = jnp.arange(DOCS, dtype=jnp.int32)
    starts = jnp.sum((document[None, :] < numbers[:, None]).astype(jnp.int32), axis=1)
    side = 2 - 4 * (z // 2 % 2)
    sources = jnp.stack([z, z + side, z - side, z + 4]) & 7
    sc = jnp.concatenate([jnp.stack([z, x_lo, x_hi, y]), starts, sources]).astype(jnp.int32)

    values, stat, *held = run_forward(group, width, sc, rows, keys)
    unit = LOG2E / math.sqrt(width)
    other = send(stat, perm=NEXT)[::-1]
    top = jnp.maximum(stat[:, :group], other[:, :group])
    mine, theirs = (jnp.exp2((s[:, :group] - top) * unit) for s in (stat, other))
    merged = jnp.concatenate(
        [top]
        + [
            stat[:, n * group : (n + 1) * group] * mine
            + other[:, n * group : (n + 1) * group] * theirs
            for n in (1, 2)
        ],
        axis=1,
    )
    stats = [merged] + [send(merged, perm=Y[s]) for s in range(1, SLOTS)]

    back = functools.partial(run_backward, group, width)
    out = back((3, 4), True, False, sc, held, *stats, stat, values)
    far, mixed, carried = out[0], out[1 : 1 + SLOTS], out[1 + SLOTS :]
    flat = (2 * PAIR, 2 * width)
    one, two = send(far[0], perm=NEAR), send(far[1], perm=REST)
    mixed = [mixed[0]] + [send(mixed[s], perm=Y[s]) for s in range(1, SLOTS)]
    near_by, *carried = back((1, 3), False, False, sc, held, *carried)
    ga = jnp.concatenate([near_by[0], add(near_by[1], two)], axis=0)
    gb = jnp.concatenate([add(near_by[2], one), near_by[3]], axis=0)
    ga, gb, carried = lax.optimization_barrier((ga, gb, carried))
    ga, gb = send(ga, perm=NEAR), send(gb, perm=REST)
    close, *dq = back((0, 1), False, True, sc, held, *carried)
    close, dq, mixed = lax.optimization_barrier((close, dq, mixed))
    dq = [dq[0]] + [send(dq[s], perm=Y[s]) for s in (2, 1, 3)]
    grad = add(close.reshape(flat), ga, gb)
    _, mixed = lax.optimization_barrier((grad, mixed))
    grad = grad.reshape(4, CHUNK, 2 * width)
    grad = [grad[0]] + [send(grad[n], perm=X[n]) for n in range(1, 4)]
    mixed = add(*mixed)
    mixed = [mixed[0], send(mixed[1], perm=NEXT)]
    grad, dq = lax.optimization_barrier((grad, dq))
    dq = [add(*[part[t] for part in dq]) for t in range(TILES)]
    dq = [dq[0], send(dq[1], perm=NEXT)]
    grad = add(*grad)
    out_shape = jax.ShapeDtypeStruct((CHUNK, group * width), BF16)
    attended, grad_query = pl.pallas_call(
        functools.partial(combine, group, width),
        out_shape=[out_shape, out_shape],
        in_specs=[VMEM] * 4,
        out_specs=[VMEM] * 2,
        compiler_params=PARAMS,
        name="combine",
    )(mixed[0], dq[0], mixed[1], dq[1])
    return attended, grad_query, grad[:, :width], grad[:, width:]


def solution(mesh):
    by_row = P(("qrow", "kcol"), "head")
    by_key = P(("kcol", "qrow"), "head")
    return jax.shard_map(
        local,
        mesh=mesh,
        in_specs=(by_row, by_key, by_key, by_row, P()),
        out_specs=(by_row, by_row, by_key, by_key),
        check_vma=False,
    )
```

```python
import functools
import math

import jax
import jax.numpy as jnp
from jax import lax
from jax.experimental import pallas as pl
from jax.experimental.pallas import tpu as pltpu
from jax.sharding import PartitionSpec as P

AXES = ("qrow", "kcol")
DEVICES = 128
CHUNK = 128
SLOTS = 4
TILES = 2
ROWS = SLOTS * CHUNK
PAIR = 2 * CHUNK
PIECES = 4
PLANE = 16 * CHUNK
DOCS = 8
NEG = -1e30
FLOOR = -1e29
SAFE = 60.0
LOG2E = math.log2(math.e)
F32 = jnp.float32
BF16 = jnp.bfloat16


def flip(mask):
    return [(d, d ^ mask) for d in range(DEVICES)]


Y = [flip(s) for s in range(SLOTS)]
X = [flip(m) for m in (0, 8, 4, 12)]
NEXT = flip(16)
NEAR = flip(32)
REST = [(d, (d + (32 if d // 32 % 2 else -32)) % DEVICES) for d in range(DEVICES)]


def dot(a, b):
    return lax.dot_general(a, b, (((1,), (0,)), ((), ())), preferred_element_type=F32)


def dot_t(a, b):
    return lax.dot_general(a, b, (((1,), (1,)), ((), ())), preferred_element_type=F32)


def fill(rows, keys, q_s, do_s, k_s, v_s, kt_s, vt_s, group, width):
    own, other, near, last, far_own, far_other = rows
    top, low = pl.ds(0, CHUNK), pl.ds(CHUNK, CHUNK)
    parts = [
        [(own, top), (near, top), (far_own, top), (last, top)],
        [(other, top), (near, low), (far_other, top), (last, low)],
    ]
    for t in range(TILES):
        for s in range(SLOTS):
            ref, at = parts[t][s]
            part, to = ref[at, :], pl.ds(s * CHUNK, CHUNK)
            for h in range(group):
                q_s[t, h, to, :] = part[:, h * width : (h + 1) * width]
                do_s[t, h, to, :] = part[:, (group + h) * width : (group + h + 1) * width]
    for piece in range(PIECES):
        for m, ref in enumerate(keys):
            part = ref[pl.ds(piece * CHUNK, CHUNK), :]
            block, at = 2 * piece + m // 2, pl.ds(m % 2 * CHUNK, CHUNK)
            k_s[block, at, :] = part[:, :width]
            v_s[block, at, :] = part[:, width:]
            kt_s[block, :, at] = jnp.transpose(part[:, :width])
            vt_s[block, :, at] = jnp.transpose(part[:, width:])


def start_of(sc, row):
    start = 0
    for n in range(DOCS):
        one = sc[4 + n]
        start = jnp.maximum(start, jnp.where(one <= row, one, 0))
    return start


def place(sc, block, t):
    z, x_lo, x_hi, y = (sc[n] for n in range(4))
    base = (4 * (x_hi ^ (block & 1)) + y) * PLANE + sc[4 + DOCS + block // 2] * PAIR
    row = ((z * 4 + x_lo * 2 + x_hi) ^ (4 * t)) * ROWS
    needed = (base <= row + ROWS - 1) & (base + PAIR - 1 >= start_of(sc, row))
    whole = (base + PAIR - 1 <= row) & (base >= start_of(sc, row + ROWS - 1))
    return base, row, needed, whole


def allowed_of(sc, base, row):
    key_at = base + (lax.broadcasted_iota(jnp.int32, (PAIR, 1), 0) ^ (sc[1] * CHUNK))
    row_at = row + (lax.broadcasted_iota(jnp.int32, (1, ROWS), 1) ^ (sc[3] * CHUNK))
    return (key_at >= start_of(sc, row_at)) & (key_at <= row_at)


def pack(query, key, value, dout, rows, keys):
    width = query.shape[1]
    rows[:, :width] = query[...]
    rows[:, width:] = dout[...]
    width = key.shape[1]
    keys[:, :width] = key[...]
    keys[:, width:] = value[...]


def forward(group, width, sc, *refs):
    rows, keys, refs = refs[:6], refs[6:10], refs[10:]
    values, stat, q_s, do_s, k_s, v_s, kt_s, t_s, acc, high, total = refs
    unit = LOG2E / math.sqrt(width)
    heads = range(group)
    fill(rows, keys, q_s, do_s, k_s, v_s, kt_s, t_s, group, width)
    acc[...] = jnp.zeros_like(acc)
    high[...] = jnp.full_like(high, FLOOR)
    total[...] = jnp.zeros_like(total)

    def widest(parts):
        ones = jnp.ones((width, width), BF16)
        return jnp.max(functools.reduce(jnp.maximum, [dot(p * p, ones) for p in parts]))

    rows_widest = widest([q_s[t, h] for t in range(TILES) for h in heads])
    keys_widest = widest([k_s[b] for b in range(2 * PIECES)])
    small = rows_widest * keys_widest * (unit * unit) <= SAFE * SAFE

    def scores_of(b, t, base, row, masked):
        scores = [dot_t(k_s[b], q_s[t, h]) for h in heads]
        if masked:
            allowed = allowed_of(sc, base, row)
            scores = [jnp.where(allowed, s, NEG) for s in scores]
        return scores

    def shifted(b, t, base, row, masked):
        scores = scores_of(b, t, base, row, masked)
        olds = [high[t, h] for h in heads]
        news = [jnp.maximum(o, jnp.max(s, axis=0, keepdims=True)) for o, s in zip(olds, scores)]
        shrinks = [jnp.exp2((o - n) * unit) for o, n in zip(olds, news)]
        es = [jnp.exp2(s * unit - n * unit) for s, n in zip(scores, news)]
        totals = [total[t, h] * shrinks[h] + jnp.sum(es[h], axis=0, keepdims=True) for h in heads]
        accs = [acc[t, h] * shrinks[h] + dot(t_s[b], es[h].astype(BF16)) for h in heads]
        for h in heads:
            high[t, h] = news[h]
            total[t, h] = totals[h]
            acc[t, h] = accs[h]

    def direct(b, t, base, row, masked):
        es = [jnp.exp2(s * unit) for s in scores_of(b, t, base, row, masked)]
        totals = [total[t, h] + jnp.sum(es[h], axis=0, keepdims=True) for h in heads]
        accs = [acc[t, h] + dot(t_s[b], es[h].astype(BF16)) for h in heads]
        for h in heads:
            total[t, h] = totals[h]
            acc[t, h] = accs[h]

    def over_blocks(block):
        def step(n, carry):
            b, t = n // 2, n & 1
            base, row, needed, whole = place(sc, b, t)

            @pl.when(needed & whole)
            def _():
                block(b, t, base, row, False)

            @pl.when(needed & jnp.logical_not(whole))
            def _():
                block(b, t, base, row, True)

            return carry

        lax.fori_loop(0, 4 * PIECES, step, 0)

    @pl.when(small)
    def _():
        over_blocks(direct)
        high[...] = jnp.where(total[...] > 0.0, 0.0, FLOOR)

    @pl.when(jnp.logical_not(small))
    def _():
        over_blocks(shifted)

    for t in range(TILES):
        for h in heads:
            product = acc[t, h] * jnp.transpose(do_s[t, h]).astype(F32)
            values[t, h] = (acc[t, h] * (1.0 / jnp.maximum(total[t, h], 1e-30))).astype(BF16)
            stat[t, h : h + 1, :] = high[t, h]
            stat[t, group + h : group + h + 1, :] = total[t, h]
            stat[t, 2 * group + h : 2 * group + h + 1, :] = jnp.sum(product, axis=0, keepdims=True)


def backward(group, width, span, begins, ends, sc, q_s, do_s, k_s, v_s, t_s, *refs):
    scale = 1.0 / math.sqrt(width)
    unit = LOG2E * scale
    heads = range(group)
    if begins:
        stats, own, values, refs = refs[:SLOTS], refs[SLOTS], refs[SLOTS + 1], refs[SLOTS + 2 :]
    else:
        acc_in, lse_in, delta_in, refs = *refs[:3], refs[3:]
    dkv, refs = refs[0], refs[1:]
    if begins:
        mixed, refs = refs[:SLOTS], refs[SLOTS:]
    if ends:
        dq, refs = refs[:SLOTS], refs[SLOTS:]
    acc, lse, delta, grads = refs
    if begins:
        acc[...] = jnp.zeros_like(acc)
        for t in range(TILES):
            for u in range(SLOTS):
                at = pl.ds(u * CHUNK, CHUNK)
                parts = [stats[s][t, :, pl.ds((u ^ s) * CHUNK, CHUNK)] for s in range(SLOTS)]
                top = functools.reduce(jnp.maximum, [p[:group] for p in parts])
                weights = [jnp.exp2((p[:group] - top) * unit) for p in parts]
                total = sum(w * p[group : 2 * group] for w, p in zip(weights, parts))
                product = sum(w * p[2 * group :] for w, p in zip(weights, parts))
                low, small = top * unit + jnp.log2(total), product / total
                part = own[t, group : 2 * group, at] * jnp.exp2(own[t, :group, at] * unit - low)
                for h in heads:
                    lse[t, h, :, at] = low[h : h + 1]
                    delta[t, h, :, at] = small[h : h + 1]
                    mixed[u][t, h * width : (h + 1) * width, :] = (
                        values[t, h, :, at].astype(F32) * part[h : h + 1]
                    ).astype(BF16)
    else:
        acc[...] = acc_in[...]
        lse[...] = lse_in[...]
        delta[...] = delta_in[...]

    def block(b, t, base, row, masked):
        scores = [dot_t(k_s[b], q_s[t, h]) for h in heads]
        dprobs = [dot_t(v_s[b], do_s[t, h]) for h in heads]
        if masked:
            allowed = allowed_of(sc, base, row)
            scores = [jnp.where(allowed, s, NEG) for s in scores]
        probs = [jnp.exp2(scores[h] * unit - lse[t, h]) for h in heads]
        dscores = [(probs[h] * (dprobs[h] - delta[t, h])).astype(BF16) for h in heads]
        lows = [p.astype(BF16) for p in probs]
        dk = sum(dot(dscores[h], q_s[t, h]) for h in heads)
        dv = sum(dot(lows[h], do_s[t, h]) for h in heads)
        accs = [acc[t, h] + dot(t_s[b], dscores[h]) for h in heads]
        for h in heads:
            acc[t, h] = accs[h]
        grads[:, :width] = grads[:, :width] + dk * scale
        grads[:, width:] = grads[:, width:] + dv

    def step(b, carry):
        grads[...] = jnp.zeros_like(grads)

        def tile(t, carry):
            base, row, needed, whole = place(sc, b, t)

            @pl.when(needed & whole)
            def _():
                block(b, t, base, row, False)

            @pl.when(needed & jnp.logical_not(whole))
            def _():
                block(b, t, base, row, True)

            return carry

        lax.fori_loop(0, TILES, tile, 0)
        dkv[b - 2 * span[0]] = grads[...].astype(BF16)
        return carry

    lax.fori_loop(2 * span[0], 2 * span[1], step, 0)
    if ends:
        for t in range(TILES):
            for h in heads:
                value = (acc[t, h] * scale).astype(BF16)
                for s in range(SLOTS):
                    dq[s][t, h * width : (h + 1) * width, :] = value[
                        :, s * CHUNK : (s + 1) * CHUNK
                    ]


def combine(group, width, *refs):
    for one, two, out in zip(refs[:2], refs[2:4], refs[4:]):
        for h in range(group):
            at = pl.ds(h * width, width)
            whole = one[at, :].astype(F32) + two[at, :].astype(F32)
            out[:, at] = jnp.transpose(whole).astype(BF16)


SMEM = pl.BlockSpec(memory_space=pltpu.SMEM)
VMEM = pl.BlockSpec(memory_space=pltpu.VMEM)
PARAMS = pltpu.CompilerParams(vmem_limit_bytes=20 * 1024 * 1024)


def cost(group, width, dots, pieces):
    work = TILES * ROWS * group * pieces * 2 * PAIR * width * 2
    return pl.CostEstimate(flops=2 * dots * work, bytes_accessed=1 << 23, transcendentals=0)


def state_shapes(group, width):
    acc = jax.ShapeDtypeStruct((TILES, group, width, ROWS), F32)
    line = jax.ShapeDtypeStruct((TILES, group, 1, ROWS), F32)
    return [acc, line, line]


def run_forward(group, width, sc, rows, keys):
    acc, line, _ = state_shapes(group, width)
    row = jax.ShapeDtypeStruct((TILES, group, ROWS, width), BF16)
    key = jax.ShapeDtypeStruct((2 * PIECES, PAIR, width), BF16)
    turned = jax.ShapeDtypeStruct((2 * PIECES, width, PAIR), BF16)
    stat = jax.ShapeDtypeStruct((TILES, 3 * group, ROWS), F32)
    return pl.pallas_call(
        functools.partial(forward, group, width),
        out_shape=[jax.ShapeDtypeStruct(acc.shape, BF16), stat, row, row, key, key, turned],
        in_specs=[SMEM] + [VMEM] * 10,
        out_specs=[VMEM] * 7,
        scratch_shapes=[pltpu.VMEM(turned.shape, BF16), pltpu.VMEM(acc.shape, F32)]
        + [pltpu.VMEM(line.shape, F32)] * 2,
        compiler_params=PARAMS,
        cost_estimate=cost(group, width, 3, PIECES),
        name="forward",
    )(sc, *rows, *keys)


def run_backward(group, width, span, begins, ends, sc, held, *more):
    pieces = span[1] - span[0]
    carried = state_shapes(group, width)
    piece = jax.ShapeDtypeStruct((TILES, group * width, CHUNK), BF16)
    shapes = [jax.ShapeDtypeStruct((2 * pieces, PAIR, 2 * width), BF16)]
    shapes = shapes + [piece] * (SLOTS * (begins + ends))
    spaces = [pltpu.VMEM((PAIR, 2 * width), F32)]
    if not ends:
        shapes = shapes + carried
    else:
        spaces = [pltpu.VMEM(s.shape, F32) for s in carried] + spaces
    return pl.pallas_call(
        functools.partial(backward, group, width, span, begins, ends),
        out_shape=shapes,
        in_specs=[SMEM] + [VMEM] * (len(held) + len(more)),
        out_specs=[VMEM] * len(shapes),
        scratch_shapes=spaces,
        compiler_params=PARAMS,
        cost_estimate=cost(group, width, 5, pieces),
        name="backward_begin" if begins else "backward_end" if ends else "backward_middle",
    )(sc, *held, *more)


def add(*parts):
    return sum(part.astype(F32) for part in parts).astype(BF16)


def local(query, key, value, dout, document):
    width = key.shape[1]
    group = query.shape[1] // width
    send = functools.partial(lax.ppermute, axis_name=AXES)
    qrow, kcol = lax.axis_index("qrow"), lax.axis_index("kcol")
    z, x_lo, x_hi, y = qrow // 2, qrow % 2, kcol // 4, kcol % 4

    row_home, key_home = pl.pallas_call(
        pack,
        out_shape=[
            jax.ShapeDtypeStruct((CHUNK, 2 * group * width), BF16),
            jax.ShapeDtypeStruct((CHUNK, 2 * width), BF16),
        ],
        name="pack",
    )(query, key, value, dout)
    row_other = send(row_home, perm=NEXT)
    a, b = send(key_home, perm=NEAR), send(key_home, perm=REST)
    row_other, a, b = lax.optimization_barrier((row_other, a, b))
    both = jnp.concatenate([row_home, row_other], axis=0)
    near, last = send(both, perm=Y[1]), send(both, perm=Y[3])
    held = jnp.concatenate([key_home, a, b, send(a, perm=REST)], axis=0)
    one, three, two = (send(held, perm=X[n]) for n in (1, 3, 2))
    keys = [held, one, two, three]
    far_own, far_other = send(last[:CHUNK], perm=Y[1]), send(near[CHUNK:], perm=Y[3])
    rows = [row_home, row_other, near, last, far_own, far_other]

    numbers = jnp.arange(DOCS, dtype=jnp.int32)
    starts = jnp.sum((document[None, :] < numbers[:, None]).astype(jnp.int32), axis=1)
    side = 2 - 4 * (z // 2 % 2)
    sources = jnp.stack([z, z + side, z - side, z + 4]) & 7
    sc = jnp.concatenate([jnp.stack([z, x_lo, x_hi, y]), starts, sources]).astype(jnp.int32)

    values, stat, *held = run_forward(group, width, sc, rows, keys)
    unit = LOG2E / math.sqrt(width)
    other = send(stat, perm=NEXT)[::-1]
    top = jnp.maximum(stat[:, :group], other[:, :group])
    mine, theirs = (jnp.exp2((s[:, :group] - top) * unit) for s in (stat, other))
    merged = jnp.concatenate(
        [top]
        + [
            stat[:, n * group : (n + 1) * group] * mine
            + other[:, n * group : (n + 1) * group] * theirs
            for n in (1, 2)
        ],
        axis=1,
    )
    one, three, two = (send(merged, perm=Y[s]) for s in (1, 3, 2))
    stats = [merged, one, two, three]

    back = functools.partial(run_backward, group, width)
    out = back((3, 4), True, False, sc, held, *stats, stat, values)
    far, mixed, carried = out[0], out[1 : 1 + SLOTS], out[1 + SLOTS :]
    flat = (2 * PAIR, 2 * width)
    one, two = send(far[0], perm=NEAR), send(far[1], perm=REST)
    mixed = [mixed[0]] + [send(mixed[s], perm=Y[s]) for s in range(1, SLOTS)]
    near_by, *carried = back((1, 3), False, False, sc, held, *carried)
    ga = jnp.concatenate([near_by[0], add(near_by[1], two)], axis=0)
    gb = jnp.concatenate([add(near_by[2], one), near_by[3]], axis=0)
    ga, gb, carried = lax.optimization_barrier((ga, gb, carried))
    ga, gb = send(ga, perm=NEAR), send(gb, perm=REST)
    close, *dq = back((0, 1), False, True, sc, held, *carried)
    close, dq, mixed = lax.optimization_barrier((close, dq, mixed))
    dq = [dq[0]] + [send(dq[s], perm=Y[s]) for s in (2, 1, 3)]
    grad = add(close.reshape(flat), ga, gb)
    _, mixed = lax.optimization_barrier((grad, mixed))
    grad = grad.reshape(4, CHUNK, 2 * width)
    grad = [grad[0]] + [send(grad[n], perm=X[n]) for n in range(1, 4)]
    mixed = add(*mixed)
    mixed = [mixed[0], send(mixed[1], perm=NEXT)]
    grad, dq = lax.optimization_barrier((grad, dq))
    dq = [add(*[part[t] for part in dq]) for t in range(TILES)]
    dq = [dq[0], send(dq[1], perm=NEXT)]
    grad = add(*grad)
    out_shape = jax.ShapeDtypeStruct((CHUNK, group * width), BF16)
    attended, grad_query = pl.pallas_call(
        functools.partial(combine, group, width),
        out_shape=[out_shape, out_shape],
        in_specs=[VMEM] * 4,
        out_specs=[VMEM] * 2,
        compiler_params=PARAMS,
        name="combine",
    )(mixed[0], dq[0], mixed[1], dq[1])
    return attended, grad_query, grad[:, :width], grad[:, width:]


def solution(mesh):
    by_row = P(("qrow", "kcol"), "head")
    by_key = P(("kcol", "qrow"), "head")
    return jax.shard_map(
        local,
        mesh=mesh,
        in_specs=(by_row, by_key, by_key, by_row, P()),
        out_specs=(by_row, by_row, by_key, by_key),
        check_vma=False,
    )
```
